256 devices in a mesh: gx: 8 (over x_hi, y), gy: 32 (over x_lo, z, core).
Axes of the slice: x: 4 (x_hi: 2, x_lo: 2; x = x_hi * 2 + x_lo), y: 4, z: 8, core: 2. Of those that a mesh axis runs over, the one named last changes fastest.
Arguments:
- features: bfloat16 [8, 32, 4, 512, 128], P('gx', 'gy')
- occupancy: int32 [8, 32, 4, 512], P('gx', 'gy'), may hold values 0 or 1
- counts: int32 [8, 32], P('gx', 'gy'), may hold values from 1 to 4, as said below
- kernel_map: int32 [8, 32, 4, 27], P('gx', 'gy'), may hold values from 0 to 16, as said below
- x_send: int32 [8, 32, 2, 2], P('gx', 'gy'), may hold values from 0 to 4, as said below
- y_send: int32 [8, 32, 2, 4], P('gx', 'gy'), may hold values from 0 to 8, as said below
- weight: bfloat16 [27, 128, 128], replicated, may hold values from -0.109375 to 0.109375
- norm_gain: float32 [128], replicated, may hold values from 0.5 to 1.5
- norm_shift: float32 [128], replicated, may hold values from -3 to 3
- cotangent: bfloat16 [8, 32, 4, 512, 128], P('gx', 'gy'), may hold values from -6 to 6
Outputs:
- activations: bfloat16 [8, 32, 4, 512, 128], P('gx', 'gy')
- features_grad: bfloat16 [8, 32, 4, 512, 128], P('gx', 'gy')
- weight_grad: float32 [27, 128, 128], replicated
- gain_grad: float32 [128], replicated
- shift_grad: float32 [128], replicated
The draws below stay inside these ranges and needn't reach their ends.
Inputs may be any that keep to these rules, and one draw needn't show every extreme that they name: `counts`: slots at or past a tile's count are empty; some tile is full. `kernel_map`: rows are numbered as in the brick table; 16 stands for an empty neighbour, and so does every tap of an empty slot. `x_send`: listed slots are live and distinct, in increasing order, followed by 4 as padding. `y_send`: entries index the first 8 rows of the sender's brick table, distinct, followed by 4 + 2 * 2 as padding.
All inputs are finite; a program needn't handle non-finite values. No bound on the sum of `occupancy` on one device may be relied on, other than what follows from the above.
Results may differ from the reference program's by a relative error of at most 0.0049.
Values may be sent and summed in bfloat16 or wider, within the bound.
No kernel may reach another device: no remote copies, remote signals or barrier semaphores. Data moves between devices by JAX's collectives and lax.ppermute only.
A program may use at most 192 MiB of HBM per device.

```python
import jax
import jax.numpy as jnp
from jax import lax

CH = 128
EDGE = 8
KTAPS = 27
SIDE = 2
ZLEV = 1
VOX = 512
TILEB = 4
HX = 2
HY = 4
ROWS = 17
TILES_X = 8
TILES_Y = 32


def build_scene(key):
    scene_key = jax.random.fold_in(key, 7)
    key_count, key_full, key_score = jax.random.split(scene_key, 3)
    live_count = jax.random.randint(key_count, (TILES_X, TILES_Y), 1, TILEB + 1)
    full_tile = jax.random.randint(key_full, (), 0, TILES_X * TILES_Y)
    tile_number = jnp.arange(TILES_X * TILES_Y, dtype=jnp.int32).reshape(TILES_X, TILES_Y)
    live_count = jnp.where(tile_number == full_tile, TILEB, live_count).astype(jnp.int32)
    scores = jax.random.randint(key_score, (TILES_X, TILES_Y, TILEB), 0, 1 << 20) * TILEB + jnp.arange(TILEB, dtype=jnp.int32)
    ranking = jnp.sum((scores[..., None, :] < scores[..., :, None]).astype(jnp.int32), axis=-1)
    filled = (ranking < live_count[..., None]).astype(jnp.int32)
    return (jnp.pad(filled, ((1, 1), (1, 1), (0, 0))), live_count)


def cell_select(want_x, want_y):
    cell_index = jnp.arange(TILEB, dtype=jnp.int32)
    chosen = jnp.ones((TILEB,), jnp.int32)
    if want_x >= 0:
        chosen = chosen * (cell_index % SIDE == want_x * (SIDE - 1)).astype(jnp.int32)
    if want_y >= 0:
        chosen = chosen * (cell_index // SIDE % SIDE == want_y * (SIDE - 1)).astype(jnp.int32)
    return chosen


def rank_among(filled_pad, select):
    cell_index = jnp.arange(TILEB, dtype=jnp.int32)
    earlier = (cell_index[:, None] < cell_index[None, :]).astype(jnp.int32)
    return jnp.sum((filled_pad * select)[..., :, None] * earlier, axis=-2)


def count_among(filled_pad, select):
    return jnp.sum(filled_pad * select, axis=-1)


def shifted(values, move_x, move_y):
    return values[1 + move_x:1 + move_x + TILES_X, 1 + move_y:1 + move_y + TILES_Y]


def place_items(valid, position, target, list_width, empty_row):
    slot_index = jnp.arange(list_width, dtype=jnp.int32)
    hit_table = valid[..., None] * (position[..., None] == slot_index).astype(jnp.int32)
    return empty_row + jnp.sum(hit_table * (target[..., None] - empty_row), axis=-2)


def draw_counts(key, part):
    filled_pad, live_count = build_scene(key)
    return live_count


def draw_x_send(key, part):
    filled_pad, live_count = build_scene(key)
    slot_rank = shifted(rank_among(filled_pad, cell_select(-1, -1)), 0, 0)
    own_fill = shifted(filled_pad, 0, 0)
    send_lists = []
    for direction in (0, 1):
        select = cell_select(direction, -1)
        send_lists.append(place_items(own_fill * select, shifted(rank_among(filled_pad, select), 0, 0), slot_rank, HX, TILEB))
    return jnp.stack(send_lists, axis=2)


def draw_y_send(key, part):
    filled_pad, live_count = build_scene(key)
    slot_rank = shifted(rank_among(filled_pad, cell_select(-1, -1)), 0, 0)
    low_rank = shifted(rank_among(filled_pad, cell_select(1, -1)), -1, 0)
    high_rank = shifted(rank_among(filled_pad, cell_select(0, -1)), 1, 0)
    send_lists = []
    for direction in (0, 1):
        own_select = cell_select(-1, direction)
        low_select = cell_select(1, direction)
        high_select = cell_select(0, direction)
        own_total = shifted(count_among(filled_pad, own_select), 0, 0)
        low_total = shifted(count_among(filled_pad, low_select), -1, 0)
        valid = jnp.concatenate((shifted(filled_pad, 0, 0) * own_select, shifted(filled_pad, -1, 0) * low_select, shifted(filled_pad, 1, 0) * high_select), axis=-1)
        position = jnp.concatenate((shifted(rank_among(filled_pad, own_select), 0, 0), own_total[..., None] + shifted(rank_among(filled_pad, low_select), -1, 0), (own_total + low_total)[..., None] + shifted(rank_among(filled_pad, high_select), 1, 0)), axis=-1)
        target = jnp.concatenate((slot_rank, TILEB + low_rank, TILEB + HX + high_rank), axis=-1)
        send_lists.append(place_items(valid, position, target, HY, TILEB + 2 * HX))
    return jnp.stack(send_lists, axis=2)


def draw_kernel_map(key, part):
    filled_pad, live_count = build_scene(key)
    empty_row = ROWS - 1
    slot_rank = rank_among(filled_pad, cell_select(-1, -1))
    face_rank = [rank_among(filled_pad, cell_select(0, -1)), rank_among(filled_pad, cell_select(1, -1))]
    line_rank = [rank_among(filled_pad, cell_select(-1, 0)), rank_among(filled_pad, cell_select(-1, 1))]
    line_total = [count_among(filled_pad, cell_select(-1, 0)), count_among(filled_pad, cell_select(-1, 1))]
    corner_rank = {}
    corner_total = {}
    for along_x in (0, 1):
        for along_y in (0, 1):
            corner_rank[along_x, along_y] = rank_among(filled_pad, cell_select(along_x, along_y))
            corner_total[along_x, along_y] = count_among(filled_pad, cell_select(along_x, along_y))
    own_fill = shifted(filled_pad, 0, 0)
    own_slots = shifted(slot_rank, 0, 0)
    slot_index = jnp.arange(TILEB, dtype=jnp.int32)
    result = jnp.full((TILES_X, TILES_Y, TILEB, KTAPS), empty_row, jnp.int32)
    for cell_number in range(TILEB):
        cell_x, cell_y, cell_z = (cell_number % SIDE, cell_number // SIDE % SIDE, cell_number // (SIDE * SIDE))
        columns = []
        for move_x in (-1, 0, 1):
            for move_y in (-1, 0, 1):
                for move_z in (-1, 0, 1):
                    near_x, near_y, near_z = (cell_x + move_x, cell_y + move_y, cell_z + move_z)
                    if near_z < 0 or near_z >= ZLEV:
                        columns.append(jnp.full((TILES_X, TILES_Y), empty_row, jnp.int32))
                    else:
                        tile_x = -1 if near_x < 0 else 1 if near_x > SIDE - 1 else 0
                        tile_y = -1 if near_y < 0 else 1 if near_y > SIDE - 1 else 0
                        inner_cell = near_x - SIDE * tile_x + SIDE * (near_y - SIDE * tile_y) + SIDE * SIDE * near_z
                        present = shifted(filled_pad, tile_x, tile_y)[..., inner_cell]
                        if tile_y == 0:
                            if tile_x == 0:
                                row_value = shifted(slot_rank, 0, 0)[..., inner_cell]
                            elif tile_x < 0:
                                row_value = TILEB + shifted(face_rank[1], -1, 0)[..., inner_cell]
                            else:
                                row_value = TILEB + HX + shifted(face_rank[0], 1, 0)[..., inner_cell]
                        else:
                            line_side = 1 if tile_y < 0 else 0
                            base_row = TILEB + 2 * HX + (0 if tile_y < 0 else HY)
                            if tile_x == 0:
                                offset = shifted(line_rank[line_side], 0, tile_y)[..., inner_cell]
                            elif tile_x < 0:
                                offset = shifted(line_total[line_side], 0, tile_y) + shifted(corner_rank[1, line_side], -1, tile_y)[..., inner_cell]
                            else:
                                offset = shifted(line_total[line_side], 0, tile_y) + shifted(corner_total[1, line_side], -1, tile_y) + shifted(corner_rank[0, line_side], 1, tile_y)[..., inner_cell]
                            row_value = base_row + offset
                        columns.append(jnp.where(present > 0, row_value, empty_row).astype(jnp.int32))
        tap_rows = jnp.stack(columns, axis=-1)
        hit_table = own_fill[..., cell_number, None] * (own_slots[..., cell_number, None] == slot_index).astype(jnp.int32)
        result = result + hit_table[..., None] * (tap_rows[..., None, :] - empty_row)
    return result


def draw_features(key, part):
    key = jax.random.fold_in(key, 11)
    key_noise, key_tile, key_channel, key_offset = jax.random.split(key, 4)
    shape = (TILES_X, TILES_Y, TILEB, VOX, CH)
    across = jnp.arange(TILES_Y, dtype=jnp.float32) / max(TILES_Y - 1, 1)
    tile_spread = 10.0 ** (0.5 * jax.random.uniform(key_tile, (TILES_X, TILES_Y), jnp.float32) - 0.25)
    channel_scale = 10.0 ** (jax.random.uniform(key_channel, (CH,), jnp.float32) - 0.5)
    tile_offset = 0.5 * jax.random.normal(key_offset, (TILES_X, TILES_Y, 1, 1, CH), jnp.float32)
    noise = jax.random.normal(key_noise, shape, jnp.float32)
    rising = 3.0 ** across
    tile_scale = (rising[None, :] * tile_spread)[:, :, None, None, None]
    return ((noise * channel_scale + tile_offset) * tile_scale).astype(jnp.bfloat16)


def plant(values, key, low, top_value):
    longest = values.shape.index(max(values.shape))
    spots = []
    for shift in (0, 1):
        where = [jax.random.randint(jax.random.fold_in(key, axis), (), 0, length) for axis, length in enumerate(values.shape)]
        where[longest] = (where[longest] + shift) % values.shape[longest]
        spots.append(tuple(where))
    return values.at[spots[0]].set(low).at[spots[1]].set(top_value)


def block_scale(key, dims, cuts, low, high):
    gain = 1.0
    for dim, shards_of in cuts:
        steps = jax.random.uniform(jax.random.fold_in(jax.random.fold_in(key, 6), dim), (shards_of,), jnp.float32, low / len(cuts), high / len(cuts))
        gain = gain * jnp.repeat(jnp.exp(steps), dims[dim] // shards_of).reshape((-1,) + (1,) * (len(dims) - 1 - dim))
    return gain


def centred(key, dims, spread, limit, shards=(), kind=jnp.bfloat16):
    array = jax.random.normal(key, dims, jnp.float32) * spread
    if len(shards) > 0:
        array = block_scale(key, dims, shards, -0.22, 0.18) * array
    return jnp.clip(array, min=-limit, max=limit).astype(kind)


def setup_inputs(seed: int = 0) -> dict:
    arg_keys = jax.random.split(jax.random.key(seed), 11)
    features = draw_features(jax.random.fold_in(arg_keys[10], 71), 0)
    occupancy = plant((jax.random.randint(arg_keys[1], (TILES_X, TILES_Y, TILEB, VOX), 0, 2) < 1).astype(jnp.int32), jax.random.fold_in(arg_keys[1], 1), 0, 1)
    counts = draw_counts(jax.random.fold_in(arg_keys[10], 71), 0)
    kernel_map = draw_kernel_map(jax.random.fold_in(arg_keys[10], 71), 0)
    x_send = draw_x_send(jax.random.fold_in(arg_keys[10], 71), 0)
    y_send = draw_y_send(jax.random.fold_in(arg_keys[10], 71), 0)
    weight = centred(arg_keys[6], (KTAPS, CH, CH), (KTAPS * CH) ** -0.5, 0.109375)
    norm_gain = jnp.clip(1.0 + 0.1 * jax.random.normal(arg_keys[7], (CH,), jnp.float32), 0.5, 1.5)
    norm_shift = centred(arg_keys[8], (CH,), 0.5, 3.0, (), jnp.float32)
    cotangent = centred(arg_keys[9], (TILES_X, TILES_Y, TILEB, VOX, CH), 1.0, 6.0, ((0, 8), (1, 32)))
    return {"features": features, "occupancy": occupancy, "counts": counts, "kernel_map": kernel_map, "x_send": x_send, "y_send": y_send, "weight": weight, "norm_gain": norm_gain, "norm_shift": norm_shift, "cotangent": cotangent}


EPSILON = 1e-05

def tap_offsets():
    return [(move_x, move_y, move_z) for move_x in (-1, 0, 1) for move_y in (-1, 0, 1) for move_z in (-1, 0, 1)]

def span_of(offset, length):
    if offset < 0:
        return (length - 1, length)
    if offset == 0:
        return (0, length)
    return (0, 1)

def assemble(bricks_table, row_map):
    length = bricks_table.shape[1]
    planes = []
    for move_x in (-1, 0, 1):
        row_parts = []
        for move_y in (-1, 0, 1):
            cell_parts = []
            for move_z in (-1, 0, 1):
                tap_index = 9 * (move_x + 1) + 3 * (move_y + 1) + move_z + 1
                bounds = [span_of(move_x, length), span_of(move_y, length), span_of(move_z, length)]
                chosen = jnp.take(bricks_table, row_map[:, tap_index], axis=0)
                cell_parts.append(chosen[:, bounds[0][0]:bounds[0][1], bounds[1][0]:bounds[1][1], bounds[2][0]:bounds[2][1], :])
            row_parts.append(jnp.concatenate(cell_parts, axis=3))
        planes.append(jnp.concatenate(row_parts, axis=2))
    return jnp.concatenate(planes, axis=1)

def window(padded, anchor):
    length = padded.shape[1] - 2
    section = padded[:, anchor[0]:anchor[0] + length, anchor[1]:anchor[1] + length, anchor[2]:anchor[2] + length, :]
    return section.reshape(-1, padded.shape[-1])

def forward_conv(padded, weight):
    length = padded.shape[1] - 2
    summed = jnp.zeros((padded.shape[0] * length ** 3, weight.shape[2]), jnp.float32)
    for tap_index, offsets in enumerate(tap_offsets()):
        anchor = [1 + offset for offset in offsets]
        summed = summed + jnp.dot(window(padded, anchor), weight[tap_index], preferred_element_type=jnp.float32)
    return summed

def transposed_conv(padded, weight):
    length = padded.shape[1] - 2
    summed = jnp.zeros((padded.shape[0] * length ** 3, weight.shape[1]), jnp.float32)
    for tap_index, offsets in enumerate(tap_offsets()):
        anchor = [1 - offset for offset in offsets]
        summed = summed + lax.dot_general(window(padded, anchor), weight[tap_index], (((1,), (1,)), ((), ())), preferred_element_type=jnp.float32)
    return summed

def weight_terms(padded, grad_rows):
    terms = []
    for tap_index, offsets in enumerate(tap_offsets()):
        anchor = [1 + offset for offset in offsets]
        terms.append(lax.dot_general(window(padded, anchor), grad_rows, (((0,), (0,)), ((), ())), preferred_element_type=jnp.float32))
    return jnp.stack(terms)

def neighbour_rows(x_send, y_send, kernel_map, nbricks):
    tiles_x, tiles_y = (x_send.shape[0], x_send.shape[1])
    empty_index = tiles_x * tiles_y * nbricks
    own_rows = jnp.arange(tiles_x * tiles_y, dtype=jnp.int32).reshape(tiles_x, tiles_y, 1) * nbricks + jnp.arange(nbricks, dtype=jnp.int32)
    blank_row = jnp.full((tiles_x, tiles_y, 1), empty_index, jnp.int32)
    own_ext = jnp.concatenate((own_rows, blank_row), axis=2)
    to_lower = jnp.take_along_axis(own_ext, x_send[:, :, 0, :], axis=2)
    to_upper = jnp.take_along_axis(own_ext, x_send[:, :, 1, :], axis=2)
    edge_x = jnp.full((1, tiles_y, x_send.shape[3]), empty_index, jnp.int32)
    from_lower = jnp.concatenate((edge_x, to_upper[:-1]), axis=0)
    from_upper = jnp.concatenate((to_lower[1:], edge_x), axis=0)
    x_table = jnp.concatenate((own_rows, from_lower, from_upper, blank_row), axis=2)
    y_lower = jnp.take_along_axis(x_table, y_send[:, :, 0, :], axis=2)
    y_upper = jnp.take_along_axis(x_table, y_send[:, :, 1, :], axis=2)
    edge_y = jnp.full((tiles_x, 1, y_send.shape[3]), empty_index, jnp.int32)
    from_below = jnp.concatenate((edge_y, y_upper[:, :-1]), axis=1)
    from_above = jnp.concatenate((y_lower[:, 1:], edge_y), axis=1)
    full_table = jnp.concatenate((own_rows, from_lower, from_upper, from_below, from_above, blank_row), axis=2)
    flat_map = kernel_map.reshape(tiles_x, tiles_y, -1)
    return jnp.take_along_axis(full_table, flat_map, axis=2).reshape(tiles_x * tiles_y, nbricks, kernel_map.shape[3])

def reference(features, occupancy, counts, kernel_map, x_send, y_send, weight, norm_gain, norm_shift, cotangent):
    tiles_x, tiles_y, nbricks, voxels, channels = features.shape
    length = EDGE
    tile_count = tiles_x * tiles_y
    slot_index = jnp.arange(nbricks, dtype=jnp.int32)
    live_mask = occupancy.astype(jnp.float32) * (slot_index[None, None, :, None] < counts[:, :, None, None]).astype(jnp.float32)
    live_mask = live_mask.reshape(tile_count, nbricks * voxels, 1)
    inputs = features.reshape(tile_count, nbricks * voxels, channels) * live_mask.astype(jnp.bfloat16)
    neighbours = neighbour_rows(x_send, y_send, kernel_map, nbricks)
    blank_brick = jnp.zeros((1, length, length, length, channels), jnp.bfloat16)
    input_table = jnp.concatenate((inputs.reshape(-1, length, length, length, channels), blank_brick), axis=0)

    def forward_tile(row_map):
        return forward_conv(assemble(input_table, row_map), weight)
    conv_out = lax.map(forward_tile, neighbours)
    live_count = jnp.sum(live_mask)
    channel_mean = lax.optimization_barrier(jnp.sum(conv_out * live_mask, axis=(0, 1))) / live_count
    variance = lax.optimization_barrier(jnp.sum(conv_out * conv_out * live_mask, axis=(0, 1))) / live_count - channel_mean * channel_mean
    inverse_std = lax.rsqrt(variance + EPSILON)
    normed = (conv_out - channel_mean) * inverse_std
    pre_act = norm_gain * normed + norm_shift
    sigmoid_pre = jax.nn.sigmoid(pre_act)
    activations = (pre_act * sigmoid_pre * live_mask).astype(jnp.bfloat16)
    grad_act = cotangent.reshape(tile_count, -1, channels).astype(jnp.float32) * live_mask * sigmoid_pre * (1.0 + pre_act * (1.0 - sigmoid_pre))
    sum_grad = lax.optimization_barrier(jnp.sum(grad_act, axis=(0, 1)))
    sum_cross = lax.optimization_barrier(jnp.sum(grad_act * normed, axis=(0, 1)))
    grad_conv = (norm_gain * inverse_std * (grad_act - (sum_grad + normed * sum_cross) / live_count) * live_mask).astype(jnp.bfloat16)
    grad_table = jnp.concatenate((grad_conv.reshape(-1, length, length, length, channels), blank_brick), axis=0)

    def backward_tile(weight_acc, packed):
        row_map, tile_grad = packed
        weight_acc = weight_acc + weight_terms(assemble(input_table, row_map), tile_grad)
        input_grad = transposed_conv(assemble(grad_table, row_map), weight)
        return (weight_acc, input_grad)
    start_acc = jnp.zeros((weight.shape[0], channels, channels), jnp.float32)
    weight_total, input_grad = lax.scan(backward_tile, start_acc, (neighbours, grad_conv))
    grad_scale = lax.rsqrt(live_count)
    features_grad = (input_grad * live_mask).astype(jnp.bfloat16).reshape(features.shape)
    return (activations.reshape(features.shape), features_grad, weight_total * grad_scale, sum_cross * grad_scale, sum_grad * grad_scale)
```

```python
import functools

import jax
import jax.numpy as jnp
from jax import lax
from jax.experimental import pallas as pl
from jax.experimental.pallas import tpu as pltpu
from jax.sharding import PartitionSpec as P

EDGE = 8
PLANE = 64
VOX = 512
CH = 128
SLOTS = 4
HX = 2
HY = 4
EPSILON = 1e-05
F32 = jnp.float32
BF16 = jnp.bfloat16

VM = pl.BlockSpec(memory_space=pltpu.VMEM)
SM = pl.BlockSpec(memory_space=pltpu.SMEM)
LIMIT = 56 * 1024 * 1024


def params():
    return pltpu.CompilerParams(vmem_limit_bytes=LIMIT)


def cost(flops, moved):
    return pl.CostEstimate(flops=flops, bytes_accessed=moved, transcendentals=0)


def shape(dims, kind):
    return jax.ShapeDtypeStruct(dims, kind)


def pick_x(sends_ref, own_ref, low_ref, high_ref):
    for side, out_ref in ((0, low_ref), (1, high_ref)):
        for k in range(HX):
            row = sends_ref[side, k]
            brick = own_ref[jnp.minimum(row, SLOTS - 1)]
            out_ref[k] = jnp.where(row < SLOTS, brick, jnp.zeros_like(brick))


def prepare_kernel(counts_ref, sends_ref, feat_ref, occ_ref, own_ref, mask_ref, low_ref, high_ref):
    for s in range(SLOTS):
        live = (s < counts_ref[0, 0]).astype(F32)
        for k in range(VOX // CH):
            row = occ_ref[s : s + 1, k * CH : (k + 1) * CH].astype(F32) * live
            column = jnp.transpose(jnp.broadcast_to(row, (CH, CH)))
            rows = pl.ds(k * CH, CH)
            mask_ref[s, rows, :] = column.astype(BF16)
            own_ref[s, rows, :] = (feat_ref[s, rows, :].astype(F32) * column).astype(BF16)
    pick_x(sends_ref, own_ref, low_ref, high_ref)


def prepare(counts, sends_x, features, occupancy):
    return pl.pallas_call(
        prepare_kernel,
        out_shape=(
            shape((SLOTS, VOX, CH), BF16),
            shape((SLOTS, VOX, CH), BF16),
            shape((HX, VOX, CH), BF16),
            shape((HX, VOX, CH), BF16),
        ),
        in_specs=[SM, SM, VM, VM],
        out_specs=(VM, VM, VM, VM),
        compiler_params=params(),
        cost_estimate=cost(1 << 20, 2 << 20),
        name="prepare",
    )(counts, sends_x, features, occupancy)


def pick_y_kernel(sends_ref, own_ref, xl_ref, xu_ref, low_ref, high_ref):
    for side, out_ref in ((0, low_ref), (1, high_ref)):
        for k in range(HY):
            row = sends_ref[side, k]

            @pl.when(row < SLOTS)
            def _():
                out_ref[k] = own_ref[jnp.minimum(row, SLOTS - 1)]

            @pl.when((row >= SLOTS) & (row < SLOTS + HX))
            def _():
                out_ref[k] = xl_ref[jnp.clip(row - SLOTS, 0, HX - 1)]

            @pl.when((row >= SLOTS + HX) & (row < SLOTS + 2 * HX))
            def _():
                out_ref[k] = xu_ref[jnp.clip(row - SLOTS - HX, 0, HX - 1)]

            @pl.when(row >= SLOTS + 2 * HX)
            def _():
                out_ref[k] = jnp.zeros((VOX, CH), BF16)


def pick_y(sends_y, own, xl, xu):
    return pl.pallas_call(
        pick_y_kernel,
        out_shape=(shape((HY, VOX, CH), BF16), shape((HY, VOX, CH), BF16)),
        in_specs=[SM, VM, VM, VM],
        out_specs=(VM, VM),
        compiler_params=params(),
        cost_estimate=cost(1 << 20, 2 << 20),
        name="pick_y",
    )(sends_y, own, xl, xu)


def neighbours(low, high, axis):
    size = lax.axis_size(axis)
    up = [(i, i + 1) for i in range(size - 1)]
    down = [(j, i) for i, j in up]
    return lax.ppermute(high, axis, up), lax.ppermute(low, axis, down)


def fill_columns(map_ref, slot, table_ref, x9_ref):
    sub = lax.broadcasted_iota(jnp.int32, (EDGE + 2, EDGE, CH), 1)
    for a in range(-1, EDGE + 1):
        move = -1 if a < 0 else (1 if a >= EDGE else 0)
        base = (a % EDGE) * PLANE
        spans = []
        for r in (-1, 0, 1):
            tap = 9 * (move + 1) + r + 1
            before = table_ref[map_ref[slot, tap], base + 48 : base + 64, :].astype(F32)[8:]
            middle = table_ref[map_ref[slot, tap + 3], base : base + 64, :].astype(F32)
            after = table_ref[map_ref[slot, tap + 6], base : base + 16, :].astype(F32)[:8]
            spans.append(jnp.concatenate((before, middle, after), axis=0).reshape(EDGE + 2, EDGE, CH))
        low, centre, high = spans
        down = pltpu.roll(jnp.where(sub == EDGE - 1, low, centre), 1, 1)
        up = pltpu.roll(jnp.where(sub == 0, high, centre), EDGE - 1, 1)
        for r, source in ((-1, down), (0, centre), (1, up)):
            for q in (-1, 0, 1):
                rows = source[q + 1 : q + 1 + EDGE].reshape(PLANE, CH).astype(BF16)
                lane = (3 * (q + 1) + r + 1) * CH
                x9_ref[(a + 1) * PLANE : (a + 2) * PLANE, lane : lane + CH] = rows


def conv_kernel(map_ref, own_ref, xl_ref, xu_ref, yl_ref, yu_ref, w_ref, mask_ref, *rest, forward):
    slot = pl.program_id(0)
    if forward:
        out_ref, x9_out, stat_ref, table_ref = rest
        x9_ref = x9_out.at[0]
    else:
        out_ref, table_ref, x9_ref = rest

    @pl.when(slot == 0)
    def _():
        start = 0
        for ref in (own_ref, xl_ref, xu_ref, yl_ref, yu_ref):
            table_ref[start : start + ref.shape[0]] = ref[...]
            start += ref.shape[0]
        table_ref[start] = jnp.zeros((VOX, CH), BF16)
        if forward:
            stat_ref[...] = jnp.zeros_like(stat_ref)

    fill_columns(map_ref, slot, table_ref, x9_ref)
    total = None
    for p in range(3):
        term = jnp.dot(
            x9_ref[p * PLANE : p * PLANE + VOX, :], w_ref[p], preferred_element_type=F32
        )
        total = term if total is None else total + term
    mask = mask_ref[0].astype(F32)
    masked = total * mask
    if forward:
        out_ref[0] = total
        stat_ref[0:1] += jnp.sum(masked, axis=0, keepdims=True)
        stat_ref[1:2] += jnp.sum(masked * total, axis=0, keepdims=True)
        stat_ref[2:3] += jnp.sum(mask, axis=0, keepdims=True)
    else:
        out_ref[0] = masked.astype(BF16)


def conv(row_map, own, xl, xu, yl, yu, weight, mask, forward):
    brick = pl.BlockSpec((1, VOX, CH), lambda s: (s, 0, 0))
    whole = lambda *dims: pl.BlockSpec(dims, lambda s: (0,) * len(dims))
    scratch = [pltpu.VMEM((17, VOX, CH), BF16)]
    if forward:
        out_shape = (
            shape((SLOTS, VOX, CH), F32),
            shape((SLOTS, 10 * PLANE, 9 * CH), BF16),
            shape((8, CH), F32),
        )
        out_specs = (brick, pl.BlockSpec((1, 10 * PLANE, 9 * CH), lambda s: (s, 0, 0)), whole(8, CH))
    else:
        out_shape = shape((SLOTS, VOX, CH), BF16)
        out_specs = brick
        scratch.append(pltpu.VMEM((10 * PLANE, 9 * CH), BF16))
    return pl.pallas_call(
        functools.partial(conv_kernel, forward=forward),
        grid=(SLOTS,),
        out_shape=out_shape,
        in_specs=[
            SM,
            whole(SLOTS, VOX, CH),
            whole(HX, VOX, CH),
            whole(HX, VOX, CH),
            whole(HY, VOX, CH),
            whole(HY, VOX, CH),
            whole(3, 9 * CH, CH),
            brick,
        ],
        out_specs=out_specs,
        scratch_shapes=scratch,
        compiler_params=params(),
        cost_estimate=cost(1811939328, 12 << 20),
        name="forward_conv" if forward else "transposed_conv",
    )(row_map, own, xl, xu, yl, yu, weight, mask)


def norm_terms(stats, gain, shift):
    count = stats[2:3]
    mean = stats[0:1] / count
    variance = stats[1:2] / count - mean * mean
    return count, mean, lax.rsqrt(variance + EPSILON)


def act_kernel(stat_ref, conv_ref, cot_ref, mask_ref, gain_ref, shift_ref, act_ref, ga_ref, g_ref, sum_ref, norm_ref):
    slot = pl.program_id(0)
    count, mean, inverse = norm_terms(jnp.sum(stat_ref[...], axis=0), None, None)

    @pl.when(slot == 0)
    def _():
        sum_ref[...] = jnp.zeros_like(sum_ref)
        norm_ref[...] = jnp.concatenate((mean, inverse, count, jnp.zeros((5, CH), F32)), axis=0)

    mask = mask_ref[0].astype(F32)
    normed = (conv_ref[0] - mean) * inverse
    pre = gain_ref[...] * normed + shift_ref[...]
    sig = jax.nn.sigmoid(pre)
    act_ref[0] = (pre * sig * mask).astype(BF16)
    ga = cot_ref[0].astype(F32) * mask * sig * (1.0 + pre * (1.0 - sig))
    ga_ref[0] = ga
    sum_ref[0:1] += jnp.sum(ga, axis=0, keepdims=True)
    sum_ref[1:2] += jnp.sum(ga * normed, axis=0, keepdims=True)
    nm = normed * mask
    for k in range(VOX // CH):
        rows = slice(k * CH, (k + 1) * CH)
        g_ref[0, 0:CH, rows] = jnp.transpose(ga[rows]).astype(BF16)
        g_ref[0, CH : 2 * CH, rows] = jnp.transpose(nm[rows]).astype(BF16)
        g_ref[0, 2 * CH : 2 * CH + 16, rows] = jnp.transpose(mask[rows])[0:16].astype(BF16)


def act(stats, conv_out, cotangent, mask, gain, shift):
    brick = pl.BlockSpec((1, VOX, CH), lambda s: (s, 0, 0))
    whole = lambda *dims: pl.BlockSpec(dims, lambda s: (0,) * len(dims))
    return pl.pallas_call(
        act_kernel,
        grid=(SLOTS,),
        out_shape=(
            shape((SLOTS, VOX, CH), BF16),
            shape((SLOTS, VOX, CH), F32),
            shape((SLOTS, 2 * CH + 16, VOX), BF16),
            shape((8, CH), F32),
            shape((8, CH), F32),
        ),
        in_specs=[whole(*stats.shape), brick, brick, brick, whole(1, CH), whole(1, CH)],
        out_specs=(
            brick,
            brick,
            pl.BlockSpec((1, 2 * CH + 16, VOX), lambda s: (s, 0, 0)),
            whole(8, CH),
            whole(8, CH),
        ),
        compiler_params=params(),
        cost_estimate=cost(8 << 20, 5 << 20),
        name="activation",
    )(stats, conv_out, cotangent, mask, gain, shift)


def wgrad_kernel(g_ref, x9_ref, out_ref):
    slot = pl.program_id(0)
    for p in range(3):
        term = jnp.dot(
            g_ref[0], x9_ref[0, p * PLANE : p * PLANE + VOX, :], preferred_element_type=F32
        )

        @pl.when(slot == 0)
        def _():
            out_ref[p] = term

        @pl.when(slot > 0)
        def _():
            out_ref[p] += term


def wgrad(g, x9):
    return pl.pallas_call(
        wgrad_kernel,
        grid=(SLOTS,),
        out_shape=shape((3, 2 * CH + 16, 9 * CH), F32),
        in_specs=[
            pl.BlockSpec((1, 2 * CH + 16, VOX), lambda s: (s, 0, 0)),
            pl.BlockSpec((1, 10 * PLANE, 9 * CH), lambda s: (s, 0, 0)),
        ],
        out_specs=pl.BlockSpec((3, 2 * CH + 16, 9 * CH), lambda s: (0, 0, 0)),
        compiler_params=params(),
        cost_estimate=cost(2 * 1811939328, 12 << 20),
        name="weight_terms",
    )(g, x9)


def grad_kernel(sends_ref, sum_ref, norm_ref, gain_ref, conv_ref, ga_ref, mask_ref, out_ref, low_ref, high_ref, tot_ref):
    totals = jnp.sum(sum_ref[...], axis=0)
    mean, inverse, count = norm_ref[0:1], norm_ref[1:2], norm_ref[2:3]
    tot_ref[...] = totals
    factor = gain_ref[...] * inverse
    for s in range(SLOTS):
        normed = (conv_ref[s] - mean) * inverse
        inner = ga_ref[s] - (totals[0:1] + normed * totals[1:2]) / count
        out_ref[s] = (factor * inner * mask_ref[s].astype(F32)).astype(BF16)
    pick_x(sends_ref, out_ref, low_ref, high_ref)


def grad(sends_x, sums, norm, gain, conv_out, ga, mask):
    return pl.pallas_call(
        grad_kernel,
        out_shape=(
            shape((SLOTS, VOX, CH), BF16),
            shape((HX, VOX, CH), BF16),
            shape((HX, VOX, CH), BF16),
            shape((8, CH), F32),
        ),
        in_specs=[SM] + [VM] * 6,
        out_specs=(VM,) * 4,
        compiler_params=params(),
        cost_estimate=cost(4 << 20, 4 << 20),
        name="grad_conv",
    )(sends_x, sums, norm, gain, conv_out, ga, mask)


def column(row):
    return jnp.transpose(jnp.broadcast_to(row, (CH, CH)))


def combine_kernel(sum_ref, norm_ref, gain_ref, w_ref, out_ref):
    totals = jnp.sum(sum_ref[...], axis=0)
    inverse, count = norm_ref[1:2], norm_ref[2:3]
    factor = column(gain_ref[...] * inverse * lax.rsqrt(count))
    first = column(totals[0:1] / count)
    second = column(totals[1:2] / count)
    for p in range(3):
        for k in range(9):
            lanes = slice(k * CH, (k + 1) * CH)
            base = w_ref[p, 0:CH, lanes]
            cross = w_ref[p, CH : 2 * CH, lanes]
            ones = w_ref[p, 2 * CH : 2 * CH + 8, lanes][0:1]
            value = factor * (base - first * ones - second * cross)
            value = value.astype(BF16)
            for g in range(8):
                out_ref[g, 9 * p + k] = value[16 * g : 16 * (g + 1)]


def combine(sums, norm, gain, terms):
    return pl.pallas_call(
        combine_kernel,
        out_shape=shape((8, 27, 16, CH), BF16),
        in_specs=[VM] * 4,
        out_specs=VM,
        compiler_params=params(),
        cost_estimate=cost(4 << 20, 5 << 20),
        name="combine",
    )(sums, norm, gain, terms)


def finish_kernel(parts_ref, out_ref):
    for t in range(27):
        rows = jnp.concatenate([parts_ref[g, t].astype(F32) for g in range(8)], axis=0)
        out_ref[t] = jnp.transpose(rows)


def finish(parts):
    return pl.pallas_call(
        finish_kernel,
        out_shape=shape((27, CH, CH), F32),
        in_specs=[VM],
        out_specs=VM,
        compiler_params=params(),
        cost_estimate=cost(1 << 20, 3 << 20),
        name="finish",
    )(parts)


def spread(value, axis):
    size = lax.axis_size(axis)
    return lax.all_to_all(jnp.broadcast_to(value[None], (size,) + value.shape), axis, 0, 0)


def all_sum_parts(value):
    return spread(jnp.sum(spread(value, "gy"), axis=0), "gx")


def reduce_weight(local):
    parts = lax.all_to_all(local, "gx", 0, 0)
    mine = jnp.sum(parts.astype(F32), axis=0).astype(BF16)
    size = lax.axis_size("gy")
    mine = jnp.concatenate((mine, jnp.zeros((size - 27, 16, CH), BF16)), axis=0)
    parts = lax.all_to_all(mine, "gy", 0, 0)
    done = jnp.sum(parts.astype(F32), axis=0).astype(BF16)
    return spread(spread(done, "gy")[:27], "gx")


def shards(
    features,
    occupancy,
    counts,
    kernel_map,
    x_send,
    y_send,
    weight,
    norm_gain,
    norm_shift,
    cotangent,
):
    row_map, sends_x, sends_y = kernel_map[0, 0], x_send[0, 0], y_send[0, 0]
    gain, shift = norm_gain.reshape(1, CH), norm_shift.reshape(1, CH)
    own, mask, low, high = prepare(counts, sends_x, features[0, 0], occupancy[0, 0])
    xl, xu = neighbours(low, high, "gx")
    low, high = pick_y(sends_y, own, xl, xu)
    yl, yu = neighbours(low, high, "gy")
    conv_out, x9, stats = conv(
        row_map, own, xl, xu, yl, yu, weight.reshape(3, 9 * CH, CH), mask, True
    )
    stats = all_sum_parts(stats)
    activations, ga, g, sums, norm = act(stats, conv_out, cotangent[0, 0], mask, gain, shift)
    sums = all_sum_parts(sums)
    terms = wgrad(g, x9)
    local = combine(sums, norm, gain, terms)
    grads, low, high, totals = grad(sends_x, sums, norm, gain, conv_out, ga, mask)
    weight_grad = finish(reduce_weight(local))
    xl, xu = neighbours(low, high, "gx")
    low, high = pick_y(sends_y, grads, xl, xu)
    yl, yu = neighbours(low, high, "gy")
    turned = jnp.transpose(weight[::-1], (0, 2, 1)).reshape(3, 9 * CH, CH)
    features_grad = conv(row_map, grads, xl, xu, yl, yu, turned, mask, False)
    scale = lax.rsqrt(norm[2])
    return (
        activations[None, None],
        features_grad[None, None],
        weight_grad,
        totals[1] * scale,
        totals[0] * scale,
    )


def solution(mesh):
    tiles = P("gx", "gy", None, None, None)
    lists = P("gx", "gy", None, None)
    return jax.shard_map(
        shards,
        mesh=mesh,
        in_specs=(tiles, lists, P("gx", "gy"), lists, lists, lists, P(), P(), P(), tiles),
        out_specs=(tiles, tiles, P(), P(), P()),
        check_vma=False,
    )
```

```python
import functools

import jax
import jax.numpy as jnp
from jax import lax
from jax.experimental import pallas as pl
from jax.experimental.pallas import tpu as pltpu
from jax.sharding import PartitionSpec as P

EDGE = 8
PLANE = 64
VOX = 512
CH = 128
SLOTS = 4
HX = 2
HY = 4
EPSILON = 1e-05
F32 = jnp.float32
BF16 = jnp.bfloat16

VM = pl.BlockSpec(memory_space=pltpu.VMEM)
SM = pl.BlockSpec(memory_space=pltpu.SMEM)
MAIN = 224
EXTRA = 48
FACE_ROWS = HY * PLANE + 16
MIB = 1024 * 1024
CROSS = ("xh", "y", "xl")


def params(limit=20):
    return pltpu.CompilerParams(vmem_limit_bytes=limit * MIB)


def cost(flops, moved):
    return pl.CostEstimate(flops=flops, bytes_accessed=moved, transcendentals=0)


def shape(dims, kind):
    return jax.ShapeDtypeStruct(dims, kind)


def pick_x(sends_ref, own_ref, low_ref, high_ref, faces):
    for side, out_ref in ((0, low_ref), (1, high_ref)):
        start, stop = (0, VOX) if not faces else ((0, PLANE), (VOX - PLANE, VOX))[side]
        for k in range(HX):
            row = sends_ref[side, k]
            brick = own_ref[jnp.minimum(row, SLOTS - 1), start:stop, :]
            out_ref[k] = jnp.where(row < SLOTS, brick, jnp.zeros_like(brick))


def x_shapes(faces):
    send = shape((HX, PLANE if faces else VOX, CH), BF16)
    return (send, send)


def prepare_kernel(
    counts_ref, sends_ref, feat_ref, occ_ref, own_ref, mask_ref, low_ref, high_ref, *, faces
):
    for s in range(SLOTS):
        live = (s < counts_ref[0, 0]).astype(F32)
        for k in range(VOX // CH):
            row = occ_ref[s : s + 1, k * CH : (k + 1) * CH].astype(F32) * live
            column = jnp.transpose(jnp.broadcast_to(row, (CH, CH)))
            rows = pl.ds(k * CH, CH)
            mask_ref[s, rows, :] = column.astype(BF16)
            own_ref[s, rows, :] = (feat_ref[s, rows, :].astype(F32) * column).astype(BF16)
    pick_x(sends_ref, own_ref, low_ref, high_ref, faces)


def prepare(counts, sends_x, features, occupancy, faces):
    return pl.pallas_call(
        functools.partial(prepare_kernel, faces=faces),
        out_shape=(shape((SLOTS, VOX, CH), BF16),) * 2 + x_shapes(faces),
        in_specs=[SM, SM, VM, VM],
        out_specs=(VM, VM, VM, VM),
        compiler_params=params(),
        cost_estimate=cost(1 << 20, 2 << 20),
        name="prepare",
    )(counts, sends_x, features, occupancy)


def pick_y_kernel(sends_ref, own_ref, xl_ref, xu_ref, low_ref, high_ref):
    for side, out_ref in ((0, low_ref), (1, high_ref)):
        for k in range(HY):
            row = sends_ref[side, k]

            @pl.when(row < SLOTS)
            def _():
                out_ref[k] = own_ref[jnp.minimum(row, SLOTS - 1)]

            @pl.when((row >= SLOTS) & (row < SLOTS + HX))
            def _():
                out_ref[k] = xl_ref[jnp.clip(row - SLOTS, 0, HX - 1)]

            @pl.when((row >= SLOTS + HX) & (row < SLOTS + 2 * HX))
            def _():
                out_ref[k] = xu_ref[jnp.clip(row - SLOTS - HX, 0, HX - 1)]

            @pl.when(row >= SLOTS + 2 * HX)
            def _():
                out_ref[k] = jnp.zeros((VOX, CH), BF16)


def pick_y_faces_kernel(sends_ref, own_ref, xl_ref, xu_ref, low_ref, high_ref):
    lines = lax.broadcasted_iota(jnp.int32, (16, CH), 0)
    for side, out_ref in ((0, low_ref), (1, high_ref)):
        skip = 0 if side == 0 else PLANE - 16

        def edge(block):
            block = block.astype(F32)
            return block[:EDGE] if side == 0 else block[EDGE:]

        origin = jnp.zeros((16, CH), F32)
        for k in range(HY):
            row = sends_ref[side, k]
            rows = pl.ds(k * PLANE, PLANE)
            lower = (row >= SLOTS) & (row < SLOTS + HX)
            upper = (row >= SLOTS + HX) & (row < SLOTS + 2 * HX)
            code = jnp.where(lower, 1.0, jnp.where(upper, 2.0, 0.0))
            origin = jnp.where(lines == k, code, origin)

            @pl.when(row < SLOTS)
            def _():
                brick = jnp.minimum(row, SLOTS - 1)
                parts = [
                    edge(own_ref[brick, a * PLANE + skip : a * PLANE + skip + 16, :])
                    for a in range(EDGE)
                ]
                out_ref[rows, :] = jnp.concatenate(parts, axis=0).astype(BF16)

            @pl.when(lower)
            def _():
                part = edge(xl_ref[jnp.clip(row - SLOTS, 0, HX - 1), skip : skip + 16, :])
                empty = jnp.zeros((PLANE - EDGE, CH), F32)
                out_ref[rows, :] = jnp.concatenate((empty, part), axis=0).astype(BF16)

            @pl.when(upper)
            def _():
                part = edge(xu_ref[jnp.clip(row - SLOTS - HX, 0, HX - 1), skip : skip + 16, :])
                empty = jnp.zeros((PLANE - EDGE, CH), F32)
                out_ref[rows, :] = jnp.concatenate((part, empty), axis=0).astype(BF16)

            @pl.when(row >= SLOTS + 2 * HX)
            def _():
                out_ref[rows, :] = jnp.zeros((PLANE, CH), BF16)

        out_ref[HY * PLANE : FACE_ROWS, :] = origin.astype(BF16)


def pick_y(sends_y, own, xl, xu, faces):
    send = shape((FACE_ROWS, CH) if faces else (HY, VOX, CH), BF16)
    return pl.pallas_call(
        pick_y_faces_kernel if faces else pick_y_kernel,
        out_shape=(send, send),
        in_specs=[SM, VM, VM, VM],
        out_specs=(VM, VM),
        compiler_params=params(),
        cost_estimate=cost(1 << 20, 2 << 20),
        name="pick_y",
    )(sends_y, own, xl, xu)


def axis_size(axes):
    size = 1
    for axis in axes:
        size *= lax.axis_size(axis)
    return size


def neighbours(low, high, axis):
    size = axis_size(axis)
    up = [(i, i + 1) for i in range(size - 1)]
    down = [(j, i) for i, j in up]
    return lax.ppermute(high, axis, up), lax.ppermute(low, axis, down)


def fill_columns(map_ref, slot, table_ref, x9_ref):
    sub = lax.broadcasted_iota(jnp.int32, (EDGE + 2, EDGE, CH), 1)
    for a in range(-1, EDGE + 1):
        move = -1 if a < 0 else (1 if a >= EDGE else 0)
        base = (a % EDGE) * PLANE
        spans = []
        for r in (-1, 0, 1):
            tap = 9 * (move + 1) + r + 1
            before = table_ref[map_ref[slot, tap], base + 48 : base + 64, :].astype(F32)[8:]
            middle = table_ref[map_ref[slot, tap + 3], base : base + 64, :].astype(F32)
            after = table_ref[map_ref[slot, tap + 6], base : base + 16, :].astype(F32)[:8]
            spans.append(jnp.concatenate((before, middle, after), axis=0).reshape(EDGE + 2, EDGE, CH))
        low, centre, high = spans
        down = pltpu.roll(jnp.where(sub == EDGE - 1, low, centre), 1, 1)
        up = pltpu.roll(jnp.where(sub == 0, high, centre), EDGE - 1, 1)
        for r, source in ((-1, down), (0, centre), (1, up)):
            for q in (-1, 0, 1):
                rows = source[q + 1 : q + 1 + EDGE].reshape(PLANE, CH).astype(BF16)
                lane = (3 * (q + 1) + r + 1) * CH
                x9_ref[(a + 1) * PLANE : (a + 2) * PLANE, lane : lane + CH] = rows


def fill_whole(table_ref, refs):
    start = 0
    for ref in refs:
        table_ref[start : start + ref.shape[0]] = ref[...]
        start += ref.shape[0]


def fill_faces(table_ref, refs):
    own_ref, xl_ref, xu_ref, yl_ref, yu_ref = refs
    table_ref[0:SLOTS] = own_ref[...]
    for k in range(HX):
        table_ref[SLOTS + k, VOX - PLANE : VOX, :] = xl_ref[k]
        table_ref[SLOTS + HX + k, 0:PLANE, :] = xu_ref[k]
    empty = jnp.zeros((EDGE, CH), F32)
    first = SLOTS + 2 * HX
    for k in range(HY):
        low = yl_ref[k * PLANE : (k + 1) * PLANE, :].astype(F32)
        high = yu_ref[k * PLANE : (k + 1) * PLANE, :].astype(F32)
        for a in range(EDGE):
            part = slice(a * EDGE, (a + 1) * EDGE)
            base = a * PLANE
            table_ref[first + k, base + 48 : base + 64, :] = jnp.concatenate(
                (empty, low[part]), axis=0
            ).astype(BF16)
            table_ref[first + HY + k, base : base + 16, :] = jnp.concatenate(
                (high[part], empty), axis=0
            ).astype(BF16)


def count_misfits(rows, yl_ref, yu_ref):
    lane = lax.broadcasted_iota(jnp.int32, rows.shape, 1)
    within = lane - jnp.where(lane >= 9, 9, 0) - jnp.where(lane >= 18, 9, 0)
    not_down, not_up = lane >= 9, lane < 18
    bad = (rows >= SLOTS) & (rows < SLOTS + HX) & not_down
    bad = bad | ((rows >= SLOTS + HX) & (rows < SLOTS + 2 * HX) & not_up)
    for start, ref, wrong in (
        (SLOTS + 2 * HX, yl_ref, within >= 3),
        (SLOTS + 2 * HX + HY, yu_ref, within < 6),
    ):
        origin = ref[HY * PLANE : FACE_ROWS, :].astype(F32)
        for k in range(HY):
            code = jnp.broadcast_to(origin[k : k + 1, 0 : rows.shape[1]], rows.shape)
            fault = wrong | ((code == 1.0) & not_down) | ((code == 2.0) & not_up)
            bad = bad | ((rows == start + k) & fault)
    return jnp.sum(jnp.where(bad, 1.0, 0.0))


def conv_kernel(
    map_ref, rows_ref, own_ref, xl_ref, xu_ref, yl_ref, yu_ref, w_ref, mask_ref, *rest, forward, faces
):
    slot = pl.program_id(0)
    if forward:
        out_ref, x9_out, stat_ref, table_ref = rest
        x9_ref = x9_out.at[0]
    else:
        out_ref, table_ref, x9_ref = rest

    @pl.when(slot == 0)
    def _():
        fill = fill_faces if faces else fill_whole
        fill(table_ref, (own_ref, xl_ref, xu_ref, yl_ref, yu_ref))
        table_ref[16] = jnp.zeros((VOX, CH), BF16)
        if forward:
            stat_ref[...] = jnp.zeros_like(stat_ref)
            if faces:
                stat_ref[3:4] = jnp.broadcast_to(
                    count_misfits(rows_ref[...], yl_ref, yu_ref), (1, CH)
                )

    fill_columns(map_ref, slot, table_ref, x9_ref)
    total = None
    for p in range(3):
        term = jnp.dot(
            x9_ref[p * PLANE : p * PLANE + VOX, :], w_ref[p], preferred_element_type=F32
        )
        total = term if total is None else total + term
    mask = mask_ref[0].astype(F32)
    masked = total * mask
    if forward:
        out_ref[0] = total
        stat_ref[0:1] += jnp.sum(masked, axis=0, keepdims=True)
        stat_ref[1:2] += jnp.sum(masked * total, axis=0, keepdims=True)
        stat_ref[2:3] += jnp.sum(mask, axis=0, keepdims=True)
    else:
        out_ref[0] = masked.astype(BF16)


def whole(*dims):
    return pl.BlockSpec(dims, lambda s: (0,) * len(dims))


def conv(row_map, own, xl, xu, yl, yu, weight, mask, forward, faces):
    brick = pl.BlockSpec((1, VOX, CH), lambda s: (s, 0, 0))
    scratch = [pltpu.VMEM((17, VOX, CH), BF16)]
    if forward:
        out_shape = (
            shape((SLOTS, VOX, CH), F32),
            shape((SLOTS, 10 * PLANE, 9 * CH), BF16),
            shape((8, CH), F32),
        )
        out_specs = (brick, pl.BlockSpec((1, 10 * PLANE, 9 * CH), lambda s: (s, 0, 0)), whole(8, CH))
    else:
        out_shape = shape((SLOTS, VOX, CH), BF16)
        out_specs = brick
        scratch.append(pltpu.VMEM((10 * PLANE, 9 * CH), BF16))
    return pl.pallas_call(
        functools.partial(conv_kernel, forward=forward, faces=faces),
        grid=(SLOTS,),
        out_shape=out_shape,
        in_specs=[
            SM,
            whole(*row_map.shape),
            whole(*own.shape),
            whole(*xl.shape),
            whole(*xu.shape),
            whole(*yl.shape),
            whole(*yu.shape),
            whole(3, 9 * CH, CH),
            brick,
        ],
        out_specs=out_specs,
        scratch_shapes=scratch,
        compiler_params=params(24),
        cost_estimate=cost(1811939328, 12 << 20),
        name="forward_conv" if forward else "transposed_conv",
    )(row_map, row_map, own, xl, xu, yl, yu, weight, mask)


def norm_terms(stats):
    count = stats[2:3]
    mean = stats[0:1] / count
    variance = stats[1:2] / count - mean * mean
    return count, mean, lax.rsqrt(variance + EPSILON)


def act_kernel(stat_ref, conv_ref, cot_ref, mask_ref, gain_ref, shift_ref, act_ref, ga_ref, g_ref, sum_ref, norm_ref):
    slot = pl.program_id(0)
    count, mean, inverse = norm_terms(jnp.sum(stat_ref[...], axis=0))

    @pl.when(slot == 0)
    def _():
        sum_ref[...] = jnp.zeros_like(sum_ref)
        norm_ref[...] = jnp.concatenate((mean, inverse, count, jnp.zeros((5, CH), F32)), axis=0)

    mask = mask_ref[0].astype(F32)
    normed = (conv_ref[0] - mean) * inverse
    pre = gain_ref[...] * normed + shift_ref[...]
    sig = jax.nn.sigmoid(pre)
    act_ref[0] = (pre * sig * mask).astype(BF16)
    ga = cot_ref[0].astype(F32) * mask * sig * (1.0 + pre * (1.0 - sig))
    ga_ref[0] = ga
    sum_ref[0:1] += jnp.sum(ga, axis=0, keepdims=True)
    sum_ref[1:2] += jnp.sum(ga * normed, axis=0, keepdims=True)
    nm = normed * mask
    for k in range(VOX // CH):
        rows = slice(k * CH, (k + 1) * CH)
        g_ref[0, 0:CH, rows] = jnp.transpose(ga[rows]).astype(BF16)
        g_ref[0, CH : 2 * CH, rows] = jnp.transpose(nm[rows]).astype(BF16)
        g_ref[0, 2 * CH : 2 * CH + 16, rows] = jnp.transpose(mask[rows])[0:16].astype(BF16)


def act(stats, conv_out, cotangent, mask, gain, shift):
    brick = pl.BlockSpec((1, VOX, CH), lambda s: (s, 0, 0))
    return pl.pallas_call(
        act_kernel,
        grid=(SLOTS,),
        out_shape=(
            shape((SLOTS, VOX, CH), BF16),
            shape((SLOTS, VOX, CH), F32),
            shape((SLOTS, 2 * CH + 16, VOX), BF16),
            shape((8, CH), F32),
            shape((8, CH), F32),
        ),
        in_specs=[whole(*stats.shape), brick, brick, brick, whole(1, CH), whole(1, CH)],
        out_specs=(
            brick,
            brick,
            pl.BlockSpec((1, 2 * CH + 16, VOX), lambda s: (s, 0, 0)),
            whole(8, CH),
            whole(8, CH),
        ),
        compiler_params=params(),
        cost_estimate=cost(8 << 20, 5 << 20),
        name="activation",
    )(stats, conv_out, cotangent, mask, gain, shift)


def split(value, pieces):
    parts = []
    for _ in range(pieces):
        part = value.astype(BF16).astype(F32)
        parts.append(part)
        value = value - part
    return parts


def pack(ones, sums):
    parts = split(ones, 2) + split(sums[0:1], 3) + split(sums[1:2], 3)
    used = sum(part.shape[0] for part in parts)
    rows = -(-used // 16) * 16
    if used < rows:
        parts.append(jnp.zeros((rows - used, CH), F32))
    return jnp.concatenate(parts, axis=0).astype(BF16)


def unpack(rows, taps):
    ones = rows[0:taps] + rows[taps : 2 * taps]
    at = 2 * taps
    first = rows[at : at + 1] + rows[at + 1 : at + 2] + rows[at + 2 : at + 3]
    second = rows[at + 3 : at + 4] + rows[at + 4 : at + 5] + rows[at + 5 : at + 6]
    return ones, jnp.concatenate((first, second), axis=0)


def wgrad_kernel(core_ref, g_ref, x9_ref, sum_ref, keep_ref, send_ref, full_ref):
    ones = [None] * 27
    for p in range(3):
        for q in range(3):
            lanes = slice(3 * q * CH, 3 * (q + 1) * CH)
            total = None
            for s in range(SLOTS):
                term = jnp.dot(
                    g_ref[s],
                    x9_ref[s, p * PLANE : p * PLANE + VOX, lanes],
                    preferred_element_type=F32,
                )
                total = term if total is None else total + term
            for r in range(3):
                t = 9 * p + 3 * q + r
                tap = total[:, r * CH : (r + 1) * CH]
                ones[t] = tap[2 * CH : 2 * CH + 1]
                for half in (0, 1):
                    i = t - 13 * half
                    if 0 <= i < 14:
                        for k in range(16):
                            pair = jnp.concatenate(
                                (tap[8 * k : 8 * k + 8], tap[CH + 8 * k : CH + 8 * k + 8]), axis=0
                            )
                            row = k * MAIN + i * 16
                            full_ref[half, row : row + 16, :] = pair.astype(BF16)
    for half in (0, 1):
        rows = jnp.concatenate(ones[13 * half : 13 * half + 14], axis=0)
        full_ref[half, 16 * MAIN : 16 * MAIN + EXTRA, :] = pack(rows, sum_ref[0:2])
    core = core_ref[0]
    keep_ref[...] = full_ref[core]
    send_ref[...] = full_ref[1 - core]


def wgrad(core, g, x9, sums):
    rows = 16 * MAIN + EXTRA
    return pl.pallas_call(
        wgrad_kernel,
        out_shape=(shape((rows, CH), BF16), shape((rows, CH), BF16)),
        in_specs=[SM, VM, VM, VM],
        out_specs=(VM, VM),
        scratch_shapes=[pltpu.VMEM((2, rows, CH), BF16)],
        compiler_params=params(24),
        cost_estimate=cost(2 * 1811939328, 12 << 20),
        name="weight_terms",
    )(core, g, x9, sums)


def join_kernel(keep_ref, got_ref, out_ref):
    for k in range(16):
        rows = slice(k * MAIN, (k + 1) * MAIN)
        out_ref[k, 0:MAIN, :] = (keep_ref[rows, :].astype(F32) + got_ref[rows, :].astype(F32)).astype(BF16)
    rows = slice(16 * MAIN, 16 * MAIN + EXTRA)
    ones, sums = unpack(keep_ref[rows, :].astype(F32), 14)
    more_ones, more_sums = unpack(got_ref[rows, :].astype(F32), 14)
    extra = pack(ones + more_ones, sums + more_sums)
    for k in range(16):
        out_ref[k, MAIN : MAIN + EXTRA, :] = extra


def join(keep, got):
    return pl.pallas_call(
        join_kernel,
        out_shape=shape((16, MAIN + EXTRA, CH), BF16),
        in_specs=[VM, VM],
        out_specs=VM,
        compiler_params=params(),
        cost_estimate=cost(1 << 20, 3 << 20),
        name="join",
    )(keep, got)


def middle_kernel(parts_ref, out_ref):
    extra = None
    for k in range(16):
        ones, sums = unpack(parts_ref[k, MAIN : MAIN + EXTRA, :].astype(F32), 14)
        extra = (ones, sums) if extra is None else (extra[0] + ones, extra[1] + sums)
    for z in range(8):
        if z < 7:
            total = None
            for k in range(16):
                term = parts_ref[k, 32 * z : 32 * (z + 1), :].astype(F32)
                total = term if total is None else total + term
            ones = extra[0][2 * z : 2 * z + 2]
        else:
            total, ones = jnp.zeros((32, CH), F32), jnp.zeros((2, CH), F32)
        out_ref[z, 0:32, :] = total.astype(BF16)
        out_ref[z, 32:48, :] = pack(ones, extra[1])


def middle(parts):
    return pl.pallas_call(
        middle_kernel,
        out_shape=shape((8, 48, CH), BF16),
        in_specs=[VM],
        out_specs=VM,
        compiler_params=params(),
        cost_estimate=cost(1 << 20, 2 << 20),
        name="middle",
    )(parts)


def column(row):
    return jnp.transpose(jnp.broadcast_to(row, (CH, CH)))


def combine_kernel(block_ref, parts_ref, norm_ref, gain_ref, out_ref, tot_ref, gg_ref, sg_ref, coef_ref):
    main, sums, ones = None, None, None
    for z in range(8):
        term = parts_ref[z, 0:32, :].astype(F32)
        term_ones, term_sums = unpack(parts_ref[z, 32:48, :].astype(F32), 2)
        main = term if main is None else main + term
        ones = term_ones if ones is None else ones + term_ones
        sums = term_sums if sums is None else sums + term_sums
    inverse, count = norm_ref[1:2], norm_ref[2:3]
    scale = lax.rsqrt(count)
    tot_ref[...] = jnp.concatenate((sums, jnp.zeros((6, CH), F32)), axis=0)
    sg_ref[...] = sums[0:1] * scale
    gg_ref[...] = sums[1:2] * scale
    coef_ref[0] = column(gain_ref[...] * inverse * scale)
    coef_ref[1] = column(sums[0:1] / count)
    coef_ref[2] = column(sums[1:2] / count)
    mine = pl.ds(pl.multiple_of(block_ref[0] * 8, 8), 8)
    factor, first, second = coef_ref[0, mine, :], coef_ref[1, mine, :], coef_ref[2, mine, :]
    values = []
    for i in range(2):
        base, cross = main[16 * i : 16 * i + 8], main[16 * i + 8 : 16 * i + 16]
        values.append(factor * (base - first * ones[i : i + 1] - second * cross))
    out_ref[...] = jnp.concatenate(values, axis=0).astype(BF16)


def combine(block, parts, norm, gain):
    return pl.pallas_call(
        combine_kernel,
        out_shape=(shape((16, CH), BF16), shape((8, CH), F32), shape((1, CH), F32), shape((1, CH), F32)),
        in_specs=[SM] + [VM] * 3,
        out_specs=(VM,) * 4,
        scratch_shapes=[pltpu.VMEM((3, CH, CH), F32)],
        compiler_params=params(),
        cost_estimate=cost(1 << 20, 1 << 20),
        name="combine",
    )(block, parts, norm, gain)


def grad_kernel(
    sends_ref, tot_ref, norm_ref, gain_ref, conv_ref, ga_ref, mask_ref, out_ref, low_ref, high_ref, *, faces
):
    mean, inverse, count = norm_ref[0:1], norm_ref[1:2], norm_ref[2:3]
    factor = gain_ref[...] * inverse
    for s in range(SLOTS):
        normed = (conv_ref[s] - mean) * inverse
        inner = ga_ref[s] - (tot_ref[0:1] + normed * tot_ref[1:2]) / count
        out_ref[s] = (factor * inner * mask_ref[s].astype(F32)).astype(BF16)
    pick_x(sends_ref, out_ref, low_ref, high_ref, faces)


def grad(sends_x, totals, norm, gain, conv_out, ga, mask, faces):
    return pl.pallas_call(
        functools.partial(grad_kernel, faces=faces),
        out_shape=(shape((SLOTS, VOX, CH), BF16),) + x_shapes(faces),
        in_specs=[SM] + [VM] * 6,
        out_specs=(VM,) * 3,
        compiler_params=params(),
        cost_estimate=cost(4 << 20, 4 << 20),
        name="grad_conv",
    )(sends_x, totals, norm, gain, conv_out, ga, mask)


def finish_kernel(core_ref, mine_ref, other_ref, out_ref):
    for half in (0, 1):
        here = core_ref[0] == half
        for z in range(7):
            pairs = []
            for k in range(16):
                rows = slice(16 * z, 16 * (z + 1))
                pairs.append(jnp.where(here, mine_ref[k, rows, :], other_ref[k, rows, :]).astype(F32))
            for i in range(2):
                tap = 13 * half + 2 * z + i
                if half == 1 and tap == 13:
                    continue
                rows = jnp.concatenate([pair[8 * i : 8 * i + 8] for pair in pairs], axis=0)
                out_ref[tap] = jnp.transpose(rows)


def finish(core, mine, other):
    return pl.pallas_call(
        finish_kernel,
        out_shape=shape((27, CH, CH), F32),
        in_specs=[SM, VM, VM],
        out_specs=VM,
        compiler_params=params(),
        cost_estimate=cost(1 << 20, 3 << 20),
        name="finish",
    )(core, mine, other)


def spread(value, axes):
    size = axis_size(axes)
    return lax.all_to_all(jnp.broadcast_to(value[None], (size,) + value.shape), axes, 0, 0)


def all_sum_parts(value):
    return spread(jnp.sum(spread(value, ("z", "c")), axis=0), CROSS)


def swap(value):
    return lax.ppermute(value, "c", [(0, 1), (1, 0)])


def halo(own, low, high, sends_y, faces):
    xl, xu = neighbours(low, high, ("xh", "y"))
    low, high = pick_y(sends_y, own, xl, xu, faces)
    yl, yu = neighbours(low, high, ("xl", "z", "c"))
    return own, xl, xu, yl, yu


def shards(
    features,
    occupancy,
    counts,
    kernel_map,
    x_send,
    y_send,
    weight,
    norm_gain,
    norm_shift,
    cotangent,
):
    row_map, sends_x, sends_y = kernel_map[0, 0], x_send[0, 0], y_send[0, 0]
    gain, shift = norm_gain.reshape(1, CH), norm_shift.reshape(1, CH)
    core = lax.axis_index("c").reshape(1)
    block = lax.axis_index(CROSS).reshape(1)
    ahead = weight.reshape(3, 9 * CH, CH)
    turned = jnp.transpose(weight[::-1], (0, 2, 1)).reshape(3, 9 * CH, CH)

    def first(faces):
        own, mask, low, high = prepare(counts, sends_x, features[0, 0], occupancy[0, 0], faces)
        table = halo(own, low, high, sends_y, faces)
        conv_out, x9, stats = conv(row_map, *table, ahead, mask, True, faces)
        return conv_out, x9, mask, all_sum_parts(stats)

    def second(conv_out, x9, mask, stats, faces):
        activations, ga, g, sums, norm = act(stats, conv_out, cotangent[0, 0], mask, gain, shift)
        keep, send = wgrad(core, g, x9, sums)
        parts = lax.all_to_all(join(keep, swap(send)), CROSS, 0, 0)
        parts = lax.all_to_all(middle(parts), "z", 0, 0)
        value, totals, gain_grad, shift_grad = combine(block, parts, norm, gain)
        grads, low, high = grad(sends_x, totals, norm, gain, conv_out, ga, mask, faces)
        mine = spread(value, ("z",)).reshape(8 * 16, CH)[: 7 * 16]
        mine = spread(mine, CROSS)
        weight_grad = finish(core, mine, swap(mine))
        table = halo(grads, low, high, sends_y, faces)
        features_grad = conv(row_map, *table, turned, mask, False, faces)
        return activations, features_grad, weight_grad, gain_grad, shift_grad

    state = first(True)
    misfits = jnp.sum(state[3][:, 3, 0])
    activations, features_grad, weight_grad, gain_grad, shift_grad = lax.cond(
        misfits > 0,
        lambda *_: second(*first(False), False),
        lambda *given: second(*given, True),
        *state,
    )
    return (
        activations[None, None],
        features_grad[None, None],
        weight_grad,
        gain_grad.reshape(CH),
        shift_grad.reshape(CH),
    )


def solution(mesh):
    fine = jax.sharding.Mesh(mesh.devices.reshape(2, 4, 2, 8, 2), ("xh", "y", "xl", "z", "c"))
    gx, gy = ("xh", "y"), ("xl", "z", "c")
    tiles = P(gx, gy, None, None, None)
    lists = P(gx, gy, None, None)
    return jax.shard_map(
        shards,
        mesh=fine,
        in_specs=(tiles, lists, P(gx, gy), lists, lists, lists, P(), P(), P(), tiles),
        out_specs=(tiles, tiles, P(), P(), P()),
        check_vma=False,
    )
```

```python
import functools

import jax
import jax.numpy as jnp
from jax import lax
from jax.experimental import pallas as pl
from jax.experimental.pallas import tpu as pltpu
from jax.sharding import PartitionSpec as P

EDGE = 8
PLANE = 64
VOX = 512
CH = 128
SLOTS = 4
HX = 2
HY = 4
EPSILON = 1e-05
F32 = jnp.float32
BF16 = jnp.bfloat16

VM = pl.BlockSpec(memory_space=pltpu.VMEM)
SM = pl.BlockSpec(memory_space=pltpu.SMEM)
MAIN = 224
EXTRA = 48
FACE_ROWS = HY * PLANE + 16
MIB = 1024 * 1024
CROSS = ("xh", "y", "xl")


def params(limit=20):
    return pltpu.CompilerParams(vmem_limit_bytes=limit * MIB)


def cost(flops, moved):
    return pl.CostEstimate(flops=flops, bytes_accessed=moved, transcendentals=0)


def shape(dims, kind):
    return jax.ShapeDtypeStruct(dims, kind)


def pick_x(sends_ref, own_ref, low_ref, high_ref, faces):
    for side, out_ref in ((0, low_ref), (1, high_ref)):
        start, stop = (0, VOX) if not faces else ((0, PLANE), (VOX - PLANE, VOX))[side]
        for k in range(HX):
            row = sends_ref[side, k]
            brick = own_ref[jnp.minimum(row, SLOTS - 1), start:stop, :]
            out_ref[k] = jnp.where(row < SLOTS, brick, jnp.zeros_like(brick))


def x_shapes(faces):
    send = shape((HX, PLANE if faces else VOX, CH), BF16)
    return (send, send)


def prepare_kernel(
    counts_ref, sends_ref, feat_ref, occ_ref, own_ref, mask_ref, low_ref, high_ref, *, faces
):
    for s in range(SLOTS):
        live = (s < counts_ref[0, 0]).astype(F32)
        for k in range(VOX // CH):
            row = occ_ref[s : s + 1, k * CH : (k + 1) * CH].astype(F32) * live
            column = jnp.transpose(jnp.broadcast_to(row, (CH, CH)))
            rows = pl.ds(k * CH, CH)
            mask_ref[s, rows, :] = column.astype(BF16)
            own_ref[s, rows, :] = (feat_ref[s, rows, :].astype(F32) * column).astype(BF16)
    pick_x(sends_ref, own_ref, low_ref, high_ref, faces)


def prepare(counts, sends_x, features, occupancy, faces):
    return pl.pallas_call(
        functools.partial(prepare_kernel, faces=faces),
        out_shape=(shape((SLOTS, VOX, CH), BF16),) * 2 + x_shapes(faces),
        in_specs=[SM, SM, VM, VM],
        out_specs=(VM, VM, VM, VM),
        compiler_params=params(),
        cost_estimate=cost(1 << 20, 2 << 20),
        name="prepare",
    )(counts, sends_x, features, occupancy)


def pick_y_kernel(sends_ref, own_ref, xl_ref, xu_ref, low_ref, high_ref):
    for side, out_ref in ((0, low_ref), (1, high_ref)):
        for k in range(HY):
            row = sends_ref[side, k]

            @pl.when(row < SLOTS)
            def _():
                out_ref[k] = own_ref[jnp.minimum(row, SLOTS - 1)]

            @pl.when((row >= SLOTS) & (row < SLOTS + HX))
            def _():
                out_ref[k] = xl_ref[jnp.clip(row - SLOTS, 0, HX - 1)]

            @pl.when((row >= SLOTS + HX) & (row < SLOTS + 2 * HX))
            def _():
                out_ref[k] = xu_ref[jnp.clip(row - SLOTS - HX, 0, HX - 1)]

            @pl.when(row >= SLOTS + 2 * HX)
            def _():
                out_ref[k] = jnp.zeros((VOX, CH), BF16)


def pick_y_faces_kernel(sends_ref, own_ref, xl_ref, xu_ref, low_ref, high_ref):
    lines = lax.broadcasted_iota(jnp.int32, (16, CH), 0)
    for side, out_ref in ((0, low_ref), (1, high_ref)):
        skip = 0 if side == 0 else PLANE - 16

        def edge(block):
            block = block.astype(F32)
            return block[:EDGE] if side == 0 else block[EDGE:]

        origin = jnp.zeros((16, CH), F32)
        for k in range(HY):
            row = sends_ref[side, k]
            rows = pl.ds(k * PLANE, PLANE)
            lower = (row >= SLOTS) & (row < SLOTS + HX)
            upper = (row >= SLOTS + HX) & (row < SLOTS + 2 * HX)
            code = jnp.where(lower, 1.0, jnp.where(upper, 2.0, 0.0))
            origin = jnp.where(lines == k, code, origin)

            @pl.when(row < SLOTS)
            def _():
                brick = jnp.minimum(row, SLOTS - 1)
                parts = [
                    edge(own_ref[brick, a * PLANE + skip : a * PLANE + skip + 16, :])
                    for a in range(EDGE)
                ]
                out_ref[rows, :] = jnp.concatenate(parts, axis=0).astype(BF16)

            @pl.when(lower)
            def _():
                part = edge(xl_ref[jnp.clip(row - SLOTS, 0, HX - 1), skip : skip + 16, :])
                empty = jnp.zeros((PLANE - EDGE, CH), F32)
                out_ref[rows, :] = jnp.concatenate((empty, part), axis=0).astype(BF16)

            @pl.when(upper)
            def _():
                part = edge(xu_ref[jnp.clip(row - SLOTS - HX, 0, HX - 1), skip : skip + 16, :])
                empty = jnp.zeros((PLANE - EDGE, CH), F32)
                out_ref[rows, :] = jnp.concatenate((part, empty), axis=0).astype(BF16)

            @pl.when(row >= SLOTS + 2 * HX)
            def _():
                out_ref[rows, :] = jnp.zeros((PLANE, CH), BF16)

        out_ref[HY * PLANE : FACE_ROWS, :] = origin.astype(BF16)


def pick_y(sends_y, own, xl, xu, faces):
    send = shape((FACE_ROWS, CH) if faces else (HY, VOX, CH), BF16)
    return pl.pallas_call(
        pick_y_faces_kernel if faces else pick_y_kernel,
        out_shape=(send, send),
        in_specs=[SM, VM, VM, VM],
        out_specs=(VM, VM),
        compiler_params=params(),
        cost_estimate=cost(1 << 20, 2 << 20),
        name="pick_y",
    )(sends_y, own, xl, xu)


def axis_size(axes):
    size = 1
    for axis in axes:
        size *= lax.axis_size(axis)
    return size


def neighbours(low, high, axis):
    size = axis_size(axis)
    up = [(i, i + 1) for i in range(size - 1)]
    down = [(j, i) for i, j in up]
    return lax.ppermute(high, axis, up), lax.ppermute(low, axis, down)


def fill_columns(map_ref, slot, table_ref, x9_ref):
    sub = lax.broadcasted_iota(jnp.int32, (EDGE + 2, EDGE, CH), 1)
    for a in range(-1, EDGE + 1):
        move = -1 if a < 0 else (1 if a >= EDGE else 0)
        base = (a % EDGE) * PLANE
        spans = []
        for r in (-1, 0, 1):
            tap = 9 * (move + 1) + r + 1
            before = table_ref[map_ref[slot, tap], base + 48 : base + 64, :].astype(F32)[8:]
            middle = table_ref[map_ref[slot, tap + 3], base : base + 64, :].astype(F32)
            after = table_ref[map_ref[slot, tap + 6], base : base + 16, :].astype(F32)[:8]
            spans.append(jnp.concatenate((before, middle, after), axis=0).reshape(EDGE + 2, EDGE, CH))
        low, centre, high = spans
        down = pltpu.roll(jnp.where(sub == EDGE - 1, low, centre), 1, 1)
        up = pltpu.roll(jnp.where(sub == 0, high, centre), EDGE - 1, 1)
        for r, source in ((-1, down), (0, centre), (1, up)):
            for q in (-1, 0, 1):
                rows = source[q + 1 : q + 1 + EDGE].reshape(PLANE, CH).astype(BF16)
                lane = (3 * (q + 1) + r + 1) * CH
                x9_ref[(a + 1) * PLANE : (a + 2) * PLANE, lane : lane + CH] = rows


def fill_whole(table_ref, refs):
    start = 0
    for ref in refs:
        table_ref[start : start + ref.shape[0]] = ref[...]
        start += ref.shape[0]


def fill_faces(table_ref, refs):
    own_ref, xl_ref, xu_ref, yl_ref, yu_ref = refs
    table_ref[0:SLOTS] = own_ref[...]
    for k in range(HX):
        table_ref[SLOTS + k, VOX - PLANE : VOX, :] = xl_ref[k]
        table_ref[SLOTS + HX + k, 0:PLANE, :] = xu_ref[k]
    empty = jnp.zeros((EDGE, CH), F32)
    first = SLOTS + 2 * HX
    for k in range(HY):
        low = yl_ref[k * PLANE : (k + 1) * PLANE, :].astype(F32)
        high = yu_ref[k * PLANE : (k + 1) * PLANE, :].astype(F32)
        for a in range(EDGE):
            part = slice(a * EDGE, (a + 1) * EDGE)
            base = a * PLANE
            table_ref[first + k, base + 48 : base + 64, :] = jnp.concatenate(
                (empty, low[part]), axis=0
            ).astype(BF16)
            table_ref[first + HY + k, base : base + 16, :] = jnp.concatenate(
                (high[part], empty), axis=0
            ).astype(BF16)


def count_misfits(rows, yl_ref, yu_ref):
    lane = lax.broadcasted_iota(jnp.int32, rows.shape, 1)
    within = lane - jnp.where(lane >= 9, 9, 0) - jnp.where(lane >= 18, 9, 0)
    not_down, not_up = lane >= 9, lane < 18
    bad = (rows >= SLOTS) & (rows < SLOTS + HX) & not_down
    bad = bad | ((rows >= SLOTS + HX) & (rows < SLOTS + 2 * HX) & not_up)
    for start, ref, wrong in (
        (SLOTS + 2 * HX, yl_ref, within >= 3),
        (SLOTS + 2 * HX + HY, yu_ref, within < 6),
    ):
        origin = ref[HY * PLANE : FACE_ROWS, :].astype(F32)
        for k in range(HY):
            code = jnp.broadcast_to(origin[k : k + 1, 0 : rows.shape[1]], rows.shape)
            fault = wrong | ((code == 1.0) & not_down) | ((code == 2.0) & not_up)
            bad = bad | ((rows == start + k) & fault)
    return jnp.sum(jnp.where(bad, 1.0, 0.0))


def conv_kernel(
    map_ref, rows_ref, own_ref, xl_ref, xu_ref, yl_ref, yu_ref, w_ref, mask_ref, *rest, forward, faces
):
    slot = pl.program_id(0)
    if forward:
        out_ref, x9_out, stat_ref, table_ref = rest
        x9_ref = x9_out.at[0]
    else:
        out_ref, table_ref, x9_ref = rest

    @pl.when(slot == 0)
    def _():
        fill = fill_faces if faces else fill_whole
        fill(table_ref, (own_ref, xl_ref, xu_ref, yl_ref, yu_ref))
        table_ref[16] = jnp.zeros((VOX, CH), BF16)
        if forward:
            stat_ref[...] = jnp.zeros_like(stat_ref)
            if faces:
                stat_ref[3:4] = jnp.broadcast_to(
                    count_misfits(rows_ref[...], yl_ref, yu_ref), (1, CH)
                )

    fill_columns(map_ref, slot, table_ref, x9_ref)
    total = None
    for p in range(3):
        term = jnp.dot(
            x9_ref[p * PLANE : p * PLANE + VOX, :], w_ref[p], preferred_element_type=F32
        )
        total = term if total is None else total + term
    mask = mask_ref[0].astype(F32)
    masked = total * mask
    if forward:
        out_ref[0] = total
        stat_ref[0:1] += jnp.sum(masked, axis=0, keepdims=True)
        stat_ref[1:2] += jnp.sum(masked * total, axis=0, keepdims=True)
        stat_ref[2:3] += jnp.sum(mask, axis=0, keepdims=True)
    else:
        out_ref[0] = masked.astype(BF16)


def whole(*dims):
    return pl.BlockSpec(dims, lambda s: (0,) * len(dims))


def conv(row_map, own, xl, xu, yl, yu, weight, mask, forward, faces):
    brick = pl.BlockSpec((1, VOX, CH), lambda s: (s, 0, 0))
    scratch = [pltpu.VMEM((17, VOX, CH), BF16)]
    if forward:
        out_shape = (
            shape((SLOTS, VOX, CH), F32),
            shape((SLOTS, 10 * PLANE, 9 * CH), BF16),
            shape((8, CH), F32),
        )
        out_specs = (brick, pl.BlockSpec((1, 10 * PLANE, 9 * CH), lambda s: (s, 0, 0)), whole(8, CH))
    else:
        out_shape = shape((SLOTS, VOX, CH), BF16)
        out_specs = brick
        scratch.append(pltpu.VMEM((10 * PLANE, 9 * CH), BF16))
    return pl.pallas_call(
        functools.partial(conv_kernel, forward=forward, faces=faces),
        grid=(SLOTS,),
        out_shape=out_shape,
        in_specs=[
            SM,
            whole(*row_map.shape),
            whole(*own.shape),
            whole(*xl.shape),
            whole(*xu.shape),
            whole(*yl.shape),
            whole(*yu.shape),
            whole(3, 9 * CH, CH),
            brick,
        ],
        out_specs=out_specs,
        scratch_shapes=scratch,
        compiler_params=params(24),
        cost_estimate=cost(6000000000, 12 << 20),
        name="forward_conv" if forward else "transposed_conv",
    )(row_map, row_map, own, xl, xu, yl, yu, weight, mask)


def norm_terms(stats):
    count = stats[2:3]
    mean = stats[0:1] / count
    variance = stats[1:2] / count - mean * mean
    return count, mean, lax.rsqrt(variance + EPSILON)


def act_kernel(stat_ref, conv_ref, cot_ref, mask_ref, gain_ref, shift_ref, act_ref, ga_ref, g_ref, sum_ref, norm_ref):
    slot = pl.program_id(0)
    count, mean, inverse = norm_terms(jnp.sum(stat_ref[...], axis=0))

    @pl.when(slot == 0)
    def _():
        sum_ref[...] = jnp.zeros_like(sum_ref)
        norm_ref[...] = jnp.concatenate((mean, inverse, count, jnp.zeros((5, CH), F32)), axis=0)

    mask = mask_ref[0].astype(F32)
    normed = (conv_ref[0] - mean) * inverse
    pre = gain_ref[...] * normed + shift_ref[...]
    sig = jax.nn.sigmoid(pre)
    act_ref[0] = (pre * sig * mask).astype(BF16)
    ga = cot_ref[0].astype(F32) * mask * sig * (1.0 + pre * (1.0 - sig))
    ga_ref[0] = ga
    sum_ref[0:1] += jnp.sum(ga, axis=0, keepdims=True)
    sum_ref[1:2] += jnp.sum(ga * normed, axis=0, keepdims=True)
    nm = normed * mask
    for k in range(VOX // CH):
        rows = slice(k * CH, (k + 1) * CH)
        g_ref[0, 0:CH, rows] = jnp.transpose(ga[rows]).astype(BF16)
        g_ref[0, CH : 2 * CH, rows] = jnp.transpose(nm[rows]).astype(BF16)
        g_ref[0, 2 * CH : 2 * CH + 16, rows] = jnp.transpose(mask[rows])[0:16].astype(BF16)


def act(stats, conv_out, cotangent, mask, gain, shift):
    brick = pl.BlockSpec((1, VOX, CH), lambda s: (s, 0, 0))
    return pl.pallas_call(
        act_kernel,
        grid=(SLOTS,),
        out_shape=(
            shape((SLOTS, VOX, CH), BF16),
            shape((SLOTS, VOX, CH), F32),
            shape((SLOTS, 2 * CH + 16, VOX), BF16),
            shape((8, CH), F32),
            shape((8, CH), F32),
        ),
        in_specs=[whole(*stats.shape), brick, brick, brick, whole(1, CH), whole(1, CH)],
        out_specs=(
            brick,
            brick,
            pl.BlockSpec((1, 2 * CH + 16, VOX), lambda s: (s, 0, 0)),
            whole(8, CH),
            whole(8, CH),
        ),
        compiler_params=params(),
        cost_estimate=cost(8 << 20, 5 << 20),
        name="activation",
    )(stats, conv_out, cotangent, mask, gain, shift)


def split(value, pieces):
    parts = []
    for _ in range(pieces):
        part = value.astype(BF16).astype(F32)
        parts.append(part)
        value = value - part
    return parts


def pack(ones, sums):
    parts = split(ones, 2) + split(sums[0:1], 3) + split(sums[1:2], 3)
    used = sum(part.shape[0] for part in parts)
    rows = -(-used // 16) * 16
    if used < rows:
        parts.append(jnp.zeros((rows - used, CH), F32))
    return jnp.concatenate(parts, axis=0).astype(BF16)


def unpack(rows, taps):
    ones = rows[0:taps] + rows[taps : 2 * taps]
    at = 2 * taps
    first = rows[at : at + 1] + rows[at + 1 : at + 2] + rows[at + 2 : at + 3]
    second = rows[at + 3 : at + 4] + rows[at + 4 : at + 5] + rows[at + 5 : at + 6]
    return ones, jnp.concatenate((first, second), axis=0)


def wgrad_kernel(core_ref, g_ref, x9_ref, sum_ref, keep_ref, send_ref, hold_ref):
    ones = [None] * 27
    for p in range(3):
        for q in range(3):
            lanes = slice(3 * q * CH, 3 * (q + 1) * CH)
            total = None
            for s in range(SLOTS):
                term = jnp.dot(
                    g_ref[s],
                    x9_ref[s, p * PLANE : p * PLANE + VOX, lanes],
                    preferred_element_type=F32,
                )
                total = term if total is None else total + term
            for r in range(3):
                t = 9 * p + 3 * q + r
                tap = total[:, r * CH : (r + 1) * CH]
                ones[t] = tap[2 * CH : 2 * CH + 1]
                for half in (0, 1):
                    i = t - 13 * half
                    if 0 <= i < 14:
                        for k in range(16):
                            pair = jnp.concatenate(
                                (tap[8 * k : 8 * k + 8], tap[CH + 8 * k : CH + 8 * k + 8]), axis=0
                            )
                            row = k * MAIN + i * 16
                            hold_ref[half, row : row + 16, :] = pair
    for half in (0, 1):
        rows = jnp.concatenate(ones[13 * half : 13 * half + 14], axis=0)
        hold_ref[half, 16 * MAIN : 16 * MAIN + EXTRA, :] = pack(rows, sum_ref[0:2]).astype(F32)
    core = core_ref[0]
    keep_ref[...] = hold_ref[core]
    send_ref[...] = hold_ref[1 - core].astype(BF16)


def wgrad(core, g, x9, sums):
    rows = 16 * MAIN + EXTRA
    return pl.pallas_call(
        wgrad_kernel,
        out_shape=(shape((rows, CH), F32), shape((rows, CH), BF16)),
        in_specs=[SM, VM, VM, VM],
        out_specs=(VM, VM),
        scratch_shapes=[pltpu.VMEM((2, rows, CH), F32)],
        compiler_params=params(24),
        cost_estimate=cost(2 * 1811939328, 12 << 20),
        name="weight_terms",
    )(core, g, x9, sums)


def join_kernel(keep_ref, got_ref, out_ref):
    for k in range(16):
        rows = slice(k * MAIN, (k + 1) * MAIN)
        out_ref[k, 0:MAIN, :] = (keep_ref[rows, :] + got_ref[rows, :].astype(F32)).astype(BF16)
    rows = slice(16 * MAIN, 16 * MAIN + EXTRA)
    ones, sums = unpack(keep_ref[rows, :], 14)
    more_ones, more_sums = unpack(got_ref[rows, :].astype(F32), 14)
    extra = pack(ones + more_ones, sums + more_sums)
    for k in range(16):
        out_ref[k, MAIN : MAIN + EXTRA, :] = extra


def join(keep, got):
    return pl.pallas_call(
        join_kernel,
        out_shape=shape((16, MAIN + EXTRA, CH), BF16),
        in_specs=[VM, VM],
        out_specs=VM,
        compiler_params=params(),
        cost_estimate=cost(1 << 20, 3 << 20),
        name="join",
    )(keep, got)


def middle_kernel(parts_ref, out_ref):
    extra = None
    for k in range(16):
        ones, sums = unpack(parts_ref[k, MAIN : MAIN + EXTRA, :].astype(F32), 14)
        extra = (ones, sums) if extra is None else (extra[0] + ones, extra[1] + sums)
    for z in range(8):
        if z < 7:
            total = None
            for k in range(16):
                term = parts_ref[k, 32 * z : 32 * (z + 1), :].astype(F32)
                total = term if total is None else total + term
            ones = extra[0][2 * z : 2 * z + 2]
        else:
            total, ones = jnp.zeros((32, CH), F32), jnp.zeros((2, CH), F32)
        out_ref[z] = jnp.concatenate((total, ones, extra[1], jnp.zeros((4, CH), F32)), axis=0)


def middle(parts):
    return pl.pallas_call(
        middle_kernel,
        out_shape=shape((8, 40, CH), F32),
        in_specs=[VM],
        out_specs=VM,
        compiler_params=params(),
        cost_estimate=cost(1 << 20, 2 << 20),
        name="middle",
    )(parts)


def column(row):
    return jnp.transpose(jnp.broadcast_to(row, (CH, CH)))


def combine_kernel(block_ref, parts_ref, norm_ref, gain_ref, out_ref, tot_ref, gg_ref, sg_ref, coef_ref):
    total = jnp.sum(parts_ref[...], axis=0)
    main, ones, sums = total[0:32], total[32:34], total[34:36]
    inverse, count = norm_ref[1:2], norm_ref[2:3]
    scale = lax.rsqrt(count)
    tot_ref[...] = jnp.concatenate((sums, jnp.zeros((6, CH), F32)), axis=0)
    sg_ref[...] = sums[0:1] * scale
    gg_ref[...] = sums[1:2] * scale
    coef_ref[0] = column(gain_ref[...] * inverse * scale)
    coef_ref[1] = column(sums[0:1] / count)
    coef_ref[2] = column(sums[1:2] / count)
    mine = pl.ds(pl.multiple_of(block_ref[0] * 8, 8), 8)
    factor, first, second = coef_ref[0, mine, :], coef_ref[1, mine, :], coef_ref[2, mine, :]
    values = []
    for i in range(2):
        base, cross = main[16 * i : 16 * i + 8], main[16 * i + 8 : 16 * i + 16]
        values.append(factor * (base - first * ones[i : i + 1] - second * cross))
    out_ref[...] = jnp.concatenate(values, axis=0).astype(BF16)


def combine(block, parts, norm, gain):
    return pl.pallas_call(
        combine_kernel,
        out_shape=(shape((16, CH), BF16), shape((8, CH), F32), shape((1, CH), F32), shape((1, CH), F32)),
        in_specs=[SM] + [VM] * 3,
        out_specs=(VM,) * 4,
        scratch_shapes=[pltpu.VMEM((3, CH, CH), F32)],
        compiler_params=params(),
        cost_estimate=cost(1 << 20, 1 << 20),
        name="combine",
    )(block, parts, norm, gain)


def grad_kernel(
    sends_ref, tot_ref, norm_ref, gain_ref, conv_ref, ga_ref, mask_ref, out_ref, low_ref, high_ref, *, faces
):
    mean, inverse, count = norm_ref[0:1], norm_ref[1:2], norm_ref[2:3]
    factor = gain_ref[...] * inverse
    for s in range(SLOTS):
        normed = (conv_ref[s] - mean) * inverse
        inner = ga_ref[s] - (tot_ref[0:1] + normed * tot_ref[1:2]) / count
        out_ref[s] = (factor * inner * mask_ref[s].astype(F32)).astype(BF16)
    pick_x(sends_ref, out_ref, low_ref, high_ref, faces)


def grad(sends_x, totals, norm, gain, conv_out, ga, mask, faces):
    return pl.pallas_call(
        functools.partial(grad_kernel, faces=faces),
        out_shape=(shape((SLOTS, VOX, CH), BF16),) + x_shapes(faces),
        in_specs=[SM] + [VM] * 6,
        out_specs=(VM,) * 3,
        compiler_params=params(),
        cost_estimate=cost(4 << 20, 4 << 20),
        name="grad_conv",
    )(sends_x, totals, norm, gain, conv_out, ga, mask)


def finish_kernel(core_ref, mine_ref, other_ref, out_ref):
    for half in (0, 1):
        here = core_ref[0] == half
        for z in range(7):
            pairs = []
            for k in range(16):
                rows = slice(16 * z, 16 * (z + 1))
                pairs.append(jnp.where(here, mine_ref[k, rows, :], other_ref[k, rows, :]).astype(F32))
            for i in range(2):
                tap = 13 * half + 2 * z + i
                if half == 1 and tap == 13:
                    continue
                rows = jnp.concatenate([pair[8 * i : 8 * i + 8] for pair in pairs], axis=0)
                out_ref[tap] = jnp.transpose(rows)


def finish(core, mine, other):
    return pl.pallas_call(
        finish_kernel,
        out_shape=shape((27, CH, CH), F32),
        in_specs=[SM, VM, VM],
        out_specs=VM,
        compiler_params=params(),
        cost_estimate=cost(1 << 20, 3 << 20),
        name="finish",
    )(core, mine, other)


def spread(value, axes):
    size = axis_size(axes)
    return lax.all_to_all(jnp.broadcast_to(value[None], (size,) + value.shape), axes, 0, 0)


def all_sum_parts(value):
    return spread(jnp.sum(spread(value, ("z", "c")), axis=0), CROSS)


def swap(value):
    return lax.ppermute(value, "c", [(0, 1), (1, 0)])


def halo(own, low, high, sends_y, faces):
    xl, xu = neighbours(low, high, ("xh", "y"))
    low, high = pick_y(sends_y, own, xl, xu, faces)
    yl, yu = neighbours(low, high, ("xl", "z", "c"))
    return own, xl, xu, yl, yu


def shards(
    features,
    occupancy,
    counts,
    kernel_map,
    x_send,
    y_send,
    weight,
    norm_gain,
    norm_shift,
    cotangent,
):
    row_map, sends_x, sends_y = kernel_map[0, 0], x_send[0, 0], y_send[0, 0]
    gain, shift = norm_gain.reshape(1, CH), norm_shift.reshape(1, CH)
    core = lax.axis_index("c").reshape(1)
    block = lax.axis_index(CROSS).reshape(1)
    ahead = weight.reshape(3, 9 * CH, CH)
    turned = jnp.transpose(weight[::-1], (0, 2, 1)).reshape(3, 9 * CH, CH)

    def first(faces):
        own, mask, low, high = prepare(counts, sends_x, features[0, 0], occupancy[0, 0], faces)
        table = halo(own, low, high, sends_y, faces)
        conv_out, x9, stats = conv(row_map, *table, ahead, mask, True, faces)
        return conv_out, x9, mask, all_sum_parts(stats)

    def second(conv_out, x9, mask, stats, faces):
        activations, ga, g, sums, norm = act(stats, conv_out, cotangent[0, 0], mask, gain, shift)
        keep, send = wgrad(core, g, x9, sums)
        parts = lax.all_to_all(join(keep, swap(send)), CROSS, 0, 0)
        parts = lax.all_to_all(middle(parts), "z", 0, 0)
        value, totals, gain_grad, shift_grad = combine(block, parts, norm, gain)
        grads, low, high = grad(sends_x, totals, norm, gain, conv_out, ga, mask, faces)
        value, low, high = lax.optimization_barrier((value, low, high))
        xl, xu = neighbours(low, high, ("xh", "y"))
        mine = spread(value, ("z",)).reshape(8 * 16, CH)[: 7 * 16]
        low, high = pick_y(sends_y, grads, xl, xu, faces)
        mine, low, high = lax.optimization_barrier((mine, low, high))
        yl, yu = neighbours(low, high, ("xl", "z", "c"))
        mine = spread(mine, CROSS)
        features_grad = conv(row_map, grads, xl, xu, yl, yu, turned, mask, False, faces)
        mine, features_grad = lax.optimization_barrier((mine, features_grad))
        weight_grad = finish(core, mine, swap(mine))
        return activations, features_grad, weight_grad, gain_grad, shift_grad

    state = first(True)
    misfits = jnp.sum(state[3][:, 3, 0])
    activations, features_grad, weight_grad, gain_grad, shift_grad = lax.cond(
        misfits > 0,
        lambda *_: second(*first(False), False),
        lambda *given: second(*given, True),
        *state,
    )
    return (
        activations[None, None],
        features_grad[None, None],
        weight_grad,
        gain_grad.reshape(CH),
        shift_grad.reshape(CH),
    )


def solution(mesh):
    fine = jax.sharding.Mesh(mesh.devices.reshape(2, 4, 2, 8, 2), ("xh", "y", "xl", "z", "c"))
    gx, gy = ("xh", "y"), ("xl", "z", "c")
    tiles = P(gx, gy, None, None, None)
    lists = P(gx, gy, None, None)
    return jax.shard_map(
        shards,
        mesh=fine,
        in_specs=(tiles, lists, P(gx, gy), lists, lists, lists, P(), P(), P(), tiles),
        out_specs=(tiles, tiles, P(), P(), P()),
        check_vma=False,
    )
```

```python
import functools

import jax
import jax.numpy as jnp
from jax import lax
from jax.experimental import pallas as pl
from jax.experimental.pallas import tpu as pltpu
from jax.sharding import PartitionSpec as P

EDGE = 8
PLANE = 64
VOX = 512
CH = 128
SLOTS = 4
HX = 2
HY = 4
EPSILON = 1e-05
F32 = jnp.float32
BF16 = jnp.bfloat16

VM = pl.BlockSpec(memory_space=pltpu.VMEM)
SM = pl.BlockSpec(memory_space=pltpu.SMEM)
MAIN = 224
EXTRA = 48
FACE_ROWS = HY * PLANE + 16
MIB = 1024 * 1024
CROSS = ("xh", "y", "xl")


def params(limit=20):
    return pltpu.CompilerParams(vmem_limit_bytes=limit * MIB)


def cost(flops, moved):
    return pl.CostEstimate(flops=flops, bytes_accessed=moved, transcendentals=0)


def shape(dims, kind):
    return jax.ShapeDtypeStruct(dims, kind)


def pick_x(sends_ref, own_ref, low_ref, high_ref, faces):
    for side, out_ref in ((0, low_ref), (1, high_ref)):
        start, stop = (0, VOX) if not faces else ((0, PLANE), (VOX - PLANE, VOX))[side]
        for k in range(HX):
            row = sends_ref[side, k]
            brick = own_ref[jnp.minimum(row, SLOTS - 1), start:stop, :]
            out_ref[k] = jnp.where(row < SLOTS, brick, jnp.zeros_like(brick))


def x_shapes(faces):
    send = shape((HX, PLANE if faces else VOX, CH), BF16)
    return (send, send)


def prepare_kernel(
    counts_ref, sends_ref, feat_ref, occ_ref, own_ref, mask_ref, low_ref, high_ref, *, faces
):
    for s in range(SLOTS):
        live = (s < counts_ref[0, 0]).astype(F32)
        for k in range(VOX // CH):
            row = occ_ref[s : s + 1, k * CH : (k + 1) * CH].astype(F32) * live
            column = jnp.transpose(jnp.broadcast_to(row, (CH, CH)))
            rows = pl.ds(k * CH, CH)
            mask_ref[s, rows, :] = column.astype(BF16)
            own_ref[s, rows, :] = (feat_ref[s, rows, :].astype(F32) * column).astype(BF16)
    pick_x(sends_ref, own_ref, low_ref, high_ref, faces)


def prepare(counts, sends_x, features, occupancy, faces):
    return pl.pallas_call(
        functools.partial(prepare_kernel, faces=faces),
        out_shape=(shape((SLOTS, VOX, CH), BF16),) * 2 + x_shapes(faces),
        in_specs=[SM, SM, VM, VM],
        out_specs=(VM, VM, VM, VM),
        compiler_params=params(),
        cost_estimate=cost(1 << 20, 2 << 20),
        name="prepare",
    )(counts, sends_x, features, occupancy)


def pick_y_kernel(sends_ref, own_ref, xl_ref, xu_ref, low_ref, high_ref):
    for side, out_ref in ((0, low_ref), (1, high_ref)):
        for k in range(HY):
            row = sends_ref[side, k]

            @pl.when(row < SLOTS)
            def _():
                out_ref[k] = own_ref[jnp.minimum(row, SLOTS - 1)]

            @pl.when((row >= SLOTS) & (row < SLOTS + HX))
            def _():
                out_ref[k] = xl_ref[jnp.clip(row - SLOTS, 0, HX - 1)]

            @pl.when((row >= SLOTS + HX) & (row < SLOTS + 2 * HX))
            def _():
                out_ref[k] = xu_ref[jnp.clip(row - SLOTS - HX, 0, HX - 1)]

            @pl.when(row >= SLOTS + 2 * HX)
            def _():
                out_ref[k] = jnp.zeros((VOX, CH), BF16)


def pick_y_faces_kernel(sends_ref, own_ref, xl_ref, xu_ref, low_ref, high_ref):
    lines = lax.broadcasted_iota(jnp.int32, (16, CH), 0)
    for side, out_ref in ((0, low_ref), (1, high_ref)):
        skip = 0 if side == 0 else PLANE - 16

        def edge(block):
            block = block.astype(F32)
            return block[:EDGE] if side == 0 else block[EDGE:]

        origin = jnp.zeros((16, CH), F32)
        for k in range(HY):
            row = sends_ref[side, k]
            rows = pl.ds(k * PLANE, PLANE)
            lower = (row >= SLOTS) & (row < SLOTS + HX)
            upper = (row >= SLOTS + HX) & (row < SLOTS + 2 * HX)
            code = jnp.where(lower, 1.0, jnp.where(upper, 2.0, 0.0))
            origin = jnp.where(lines == k, code, origin)

            @pl.when(row < SLOTS)
            def _():
                brick = jnp.minimum(row, SLOTS - 1)
                parts = [
                    edge(own_ref[brick, a * PLANE + skip : a * PLANE + skip + 16, :])
                    for a in range(EDGE)
                ]
                out_ref[rows, :] = jnp.concatenate(parts, axis=0).astype(BF16)

            @pl.when(lower)
            def _():
                part = edge(xl_ref[jnp.clip(row - SLOTS, 0, HX - 1), skip : skip + 16, :])
                empty = jnp.zeros((PLANE - EDGE, CH), F32)
                out_ref[rows, :] = jnp.concatenate((empty, part), axis=0).astype(BF16)

            @pl.when(upper)
            def _():
                part = edge(xu_ref[jnp.clip(row - SLOTS - HX, 0, HX - 1), skip : skip + 16, :])
                empty = jnp.zeros((PLANE - EDGE, CH), F32)
                out_ref[rows, :] = jnp.concatenate((part, empty), axis=0).astype(BF16)

            @pl.when(row >= SLOTS + 2 * HX)
            def _():
                out_ref[rows, :] = jnp.zeros((PLANE, CH), BF16)

        out_ref[HY * PLANE : FACE_ROWS, :] = origin.astype(BF16)


def pick_y(sends_y, own, xl, xu, faces):
    send = shape((FACE_ROWS, CH) if faces else (HY, VOX, CH), BF16)
    return pl.pallas_call(
        pick_y_faces_kernel if faces else pick_y_kernel,
        out_shape=(send, send),
        in_specs=[SM, VM, VM, VM],
        out_specs=(VM, VM),
        compiler_params=params(),
        cost_estimate=cost(1 << 20, 2 << 20),
        name="pick_y",
    )(sends_y, own, xl, xu)


def axis_size(axes):
    size = 1
    for axis in axes:
        size *= lax.axis_size(axis)
    return size


def neighbours(low, high, axis):
    size = axis_size(axis)
    up = [(i, i + 1) for i in range(size - 1)]
    down = [(j, i) for i, j in up]
    return lax.ppermute(high, axis, up), lax.ppermute(low, axis, down)


def fill_columns(map_ref, slot, table_ref, x9_ref):
    sub = lax.broadcasted_iota(jnp.int32, (EDGE + 2, EDGE, CH), 1)
    for a in range(-1, EDGE + 1):
        move = -1 if a < 0 else (1 if a >= EDGE else 0)
        base = (a % EDGE) * PLANE
        spans = []
        for r in (-1, 0, 1):
            tap = 9 * (move + 1) + r + 1
            before = table_ref[map_ref[slot, tap], base + 48 : base + 64, :].astype(F32)[8:]
            middle = table_ref[map_ref[slot, tap + 3], base : base + 64, :].astype(F32)
            after = table_ref[map_ref[slot, tap + 6], base : base + 16, :].astype(F32)[:8]
            spans.append(jnp.concatenate((before, middle, after), axis=0).reshape(EDGE + 2, EDGE, CH))
        low, centre, high = spans
        down = pltpu.roll(jnp.where(sub == EDGE - 1, low, centre), 1, 1)
        up = pltpu.roll(jnp.where(sub == 0, high, centre), EDGE - 1, 1)
        for r, source in ((-1, down), (0, centre), (1, up)):
            for q in (-1, 0, 1):
                rows = source[q + 1 : q + 1 + EDGE].reshape(PLANE, CH).astype(BF16)
                lane = (3 * (q + 1) + r + 1) * CH
                x9_ref[(a + 1) * PLANE : (a + 2) * PLANE, lane : lane + CH] = rows


def fill_whole(table_ref, refs):
    start = 0
    for ref in refs:
        table_ref[start : start + ref.shape[0]] = ref[...]
        start += ref.shape[0]


def fill_faces(table_ref, refs):
    own_ref, xl_ref, xu_ref, yl_ref, yu_ref = refs
    table_ref[0:SLOTS] = own_ref[...]
    for k in range(HX):
        table_ref[SLOTS + k, VOX - PLANE : VOX, :] = xl_ref[k]
        table_ref[SLOTS + HX + k, 0:PLANE, :] = xu_ref[k]
    empty = jnp.zeros((EDGE, CH), F32)
    first = SLOTS + 2 * HX
    for k in range(HY):
        low = yl_ref[k * PLANE : (k + 1) * PLANE, :].astype(F32)
        high = yu_ref[k * PLANE : (k + 1) * PLANE, :].astype(F32)
        for a in range(EDGE):
            part = slice(a * EDGE, (a + 1) * EDGE)
            base = a * PLANE
            table_ref[first + k, base + 48 : base + 64, :] = jnp.concatenate(
                (empty, low[part]), axis=0
            ).astype(BF16)
            table_ref[first + HY + k, base : base + 16, :] = jnp.concatenate(
                (high[part], empty), axis=0
            ).astype(BF16)


def count_misfits(rows, yl_ref, yu_ref):
    lane = lax.broadcasted_iota(jnp.int32, rows.shape, 1)
    within = lane - jnp.where(lane >= 9, 9, 0) - jnp.where(lane >= 18, 9, 0)
    not_down, not_up = lane >= 9, lane < 18
    bad = (rows >= SLOTS) & (rows < SLOTS + HX) & not_down
    bad = bad | ((rows >= SLOTS + HX) & (rows < SLOTS + 2 * HX) & not_up)
    for start, ref, wrong in (
        (SLOTS + 2 * HX, yl_ref, within >= 3),
        (SLOTS + 2 * HX + HY, yu_ref, within < 6),
    ):
        origin = ref[HY * PLANE : FACE_ROWS, :].astype(F32)
        for k in range(HY):
            code = jnp.broadcast_to(origin[k : k + 1, 0 : rows.shape[1]], rows.shape)
            fault = wrong | ((code == 1.0) & not_down) | ((code == 2.0) & not_up)
            bad = bad | ((rows == start + k) & fault)
    return jnp.sum(jnp.where(bad, 1.0, 0.0))


def conv_kernel(
    map_ref, rows_ref, own_ref, xl_ref, xu_ref, yl_ref, yu_ref, w_ref, mask_ref, *rest, forward, faces
):
    if forward:
        out_ref, x9_out, stat_ref, table_ref, x9_ref, sems = rest
    else:
        out_ref, table_ref, x9_ref = rest
    fill = fill_faces if faces else fill_whole
    fill(table_ref, (own_ref, xl_ref, xu_ref, yl_ref, yu_ref))
    table_ref[16] = jnp.zeros((VOX, CH), BF16)
    sums = [jnp.zeros((1, CH), F32)] * 3
    copies = []

    def columns(slot):
        fill_columns(map_ref, slot, table_ref, x9_ref.at[slot])
        if forward:
            copies.append(pltpu.make_async_copy(x9_ref.at[slot], x9_out.at[slot], sems.at[slot]))
            copies[-1].start()

    columns(0)
    for slot in range(SLOTS):
        if slot + 1 < SLOTS:
            columns(slot + 1)
        total = None
        for p in range(3):
            term = jnp.dot(
                x9_ref[slot, p * PLANE : p * PLANE + VOX, :], w_ref[p], preferred_element_type=F32
            )
            total = term if total is None else total + term
        mask = mask_ref[slot].astype(F32)
        masked = total * mask
        if forward:
            out_ref[slot] = total
            terms = (masked, masked * total, mask)
            sums = [s + jnp.sum(term, axis=0, keepdims=True) for s, term in zip(sums, terms)]
        else:
            out_ref[slot] = masked.astype(BF16)
    if forward:
        misfits = count_misfits(rows_ref[...], yl_ref, yu_ref) if faces else 0.0
        sums.append(jnp.broadcast_to(misfits, (1, CH)))
        stat_ref[...] = jnp.concatenate(sums + [jnp.zeros((4, CH), F32)], axis=0)
    for copy in copies:
        copy.wait()


def whole(*dims):
    return pl.BlockSpec(dims, lambda s: (0,) * len(dims))


def conv(row_map, own, xl, xu, yl, yu, weight, mask, forward, faces):
    columns = (SLOTS, 10 * PLANE, 9 * CH)
    scratch = [pltpu.VMEM((17, VOX, CH), BF16), pltpu.VMEM(columns, BF16)]
    if forward:
        out_shape = (shape((SLOTS, VOX, CH), F32), shape(columns, BF16), shape((8, CH), F32))
        out_specs = (VM, pl.BlockSpec(memory_space=pl.ANY), VM)
        scratch.append(pltpu.SemaphoreType.DMA((SLOTS,)))
    else:
        out_shape = shape((SLOTS, VOX, CH), BF16)
        out_specs = VM
    return pl.pallas_call(
        functools.partial(conv_kernel, forward=forward, faces=faces),
        out_shape=out_shape,
        in_specs=[SM] + [VM] * 8,
        out_specs=out_specs,
        scratch_shapes=scratch,
        compiler_params=params(28),
        cost_estimate=cost(6000000000, 12 << 20),
        name="forward_conv" if forward else "transposed_conv",
    )(row_map, row_map, own, xl, xu, yl, yu, weight, mask)


def norm_terms(stats):
    count = stats[2:3]
    mean = stats[0:1] / count
    variance = stats[1:2] / count - mean * mean
    return count, mean, lax.rsqrt(variance + EPSILON)


def activate(slot, stats, cot_ref, conv_ref, mask_ref, gain_ref, shift_ref, act_ref, ga_ref, g_ref):
    count, mean, inverse = stats
    mask = mask_ref[slot].astype(F32)
    normed = (conv_ref[slot] - mean) * inverse
    pre = gain_ref[...] * normed + shift_ref[...]
    sig = jax.nn.sigmoid(pre)
    act_ref[slot] = (pre * sig * mask).astype(BF16)
    ga = cot_ref[slot].astype(F32) * mask * sig * (1.0 + pre * (1.0 - sig))
    ga_ref[slot] = ga
    nm = normed * mask
    for k in range(VOX // CH):
        rows = slice(k * CH, (k + 1) * CH)
        g_ref[slot, 0:CH, rows] = jnp.transpose(ga[rows]).astype(BF16)
        g_ref[slot, CH : 2 * CH, rows] = jnp.transpose(nm[rows]).astype(BF16)
        g_ref[slot, 2 * CH : 2 * CH + 16, rows] = jnp.transpose(mask[rows])[0:16].astype(BF16)
    sums = (jnp.sum(ga, axis=0, keepdims=True), jnp.sum(ga * normed, axis=0, keepdims=True))
    return jnp.concatenate(sums, axis=0)


def split(value, pieces):
    parts = []
    for _ in range(pieces):
        part = value.astype(BF16).astype(F32)
        parts.append(part)
        value = value - part
    return parts


def pack(ones, sums):
    parts = split(ones, 2) + split(sums[0:1], 3) + split(sums[1:2], 3)
    used = sum(part.shape[0] for part in parts)
    rows = -(-used // 16) * 16
    if used < rows:
        parts.append(jnp.zeros((rows - used, CH), F32))
    return jnp.concatenate(parts, axis=0).astype(BF16)


def unpack(rows, taps):
    ones = rows[0:taps] + rows[taps : 2 * taps]
    at = 2 * taps
    first = rows[at : at + 1] + rows[at + 1 : at + 2] + rows[at + 2 : at + 3]
    second = rows[at + 3 : at + 4] + rows[at + 4 : at + 5] + rows[at + 5 : at + 6]
    return ones, jnp.concatenate((first, second), axis=0)


def wgrad_kernel(
    core_ref, stat_ref, conv_ref, cot_ref, mask_ref, gain_ref, shift_ref, x9_hbm,
    act_ref, ga_ref, norm_ref, keep_ref, send_ref, g_ref, x9_ref, hold_ref, sems,
):
    copies = [
        pltpu.make_async_copy(x9_hbm.at[s], x9_ref.at[s], sems.at[s]) for s in range(SLOTS)
    ]
    for copy in copies:
        copy.start()
    stats = norm_terms(jnp.sum(stat_ref[...], axis=0))
    count, mean, inverse = stats
    norm_ref[...] = jnp.concatenate((mean, inverse, count, jnp.zeros((5, CH), F32)), axis=0)
    sums = jnp.zeros((2, CH), F32)
    for s in range(SLOTS):
        sums = sums + activate(
            s, stats, cot_ref, conv_ref, mask_ref, gain_ref, shift_ref, act_ref, ga_ref, g_ref
        )
    for copy in copies:
        copy.wait()
    ones = [None] * 27
    for p in range(3):
        for q in range(0, 9, 2):
            width = min(2, 9 - q)
            lanes = slice(q * CH, (q + width) * CH)
            total = None
            for s in range(SLOTS):
                term = jnp.dot(
                    g_ref[s],
                    x9_ref[s, p * PLANE : p * PLANE + VOX, lanes],
                    preferred_element_type=F32,
                )
                total = term if total is None else total + term
            for r in range(width):
                t = 9 * p + q + r
                tap = total[:, r * CH : (r + 1) * CH]
                ones[t] = tap[2 * CH : 2 * CH + 1]
                for half in (0, 1):
                    i = t - 13 * half
                    if 0 <= i < 14:
                        for k in range(16):
                            pair = jnp.concatenate(
                                (tap[8 * k : 8 * k + 8], tap[CH + 8 * k : CH + 8 * k + 8]), axis=0
                            )
                            row = k * MAIN + i * 16
                            hold_ref[half, row : row + 16, :] = pair
    for half in (0, 1):
        rows = jnp.concatenate(ones[13 * half : 13 * half + 14], axis=0)
        hold_ref[half, 16 * MAIN : 16 * MAIN + EXTRA, :] = pack(rows, sums).astype(F32)
    core = core_ref[0]
    keep_ref[...] = hold_ref[core]
    send_ref[...] = hold_ref[1 - core].astype(BF16)


def wgrad(core, stats, conv_out, cotangent, mask, gain, shift, x9):
    rows = 16 * MAIN + EXTRA
    return pl.pallas_call(
        wgrad_kernel,
        out_shape=(
            shape((SLOTS, VOX, CH), BF16),
            shape((SLOTS, VOX, CH), F32),
            shape((8, CH), F32),
            shape((rows, CH), F32),
            shape((rows, CH), BF16),
        ),
        in_specs=[SM] + [VM] * 6 + [pl.BlockSpec(memory_space=pl.ANY)],
        out_specs=(VM,) * 5,
        scratch_shapes=[
            pltpu.VMEM((SLOTS, 2 * CH + 16, VOX), BF16),
            pltpu.VMEM((SLOTS, 10 * PLANE, 9 * CH), BF16),
            pltpu.VMEM((2, rows, CH), F32),
            pltpu.SemaphoreType.DMA((SLOTS,)),
        ],
        compiler_params=params(28),
        cost_estimate=cost(6000000000, 12 << 20),
        name="weight_terms",
    )(core, stats, conv_out, cotangent, mask, gain, shift, x9)


def join_kernel(keep_ref, got_ref, out_ref):
    for k in range(16):
        rows = slice(k * MAIN, (k + 1) * MAIN)
        out_ref[k, 0:MAIN, :] = (keep_ref[rows, :] + got_ref[rows, :].astype(F32)).astype(BF16)
    rows = slice(16 * MAIN, 16 * MAIN + EXTRA)
    ones, sums = unpack(keep_ref[rows, :], 14)
    more_ones, more_sums = unpack(got_ref[rows, :].astype(F32), 14)
    extra = pack(ones + more_ones, sums + more_sums)
    for k in range(16):
        out_ref[k, MAIN : MAIN + EXTRA, :] = extra


def join(keep, got):
    return pl.pallas_call(
        join_kernel,
        out_shape=shape((16, MAIN + EXTRA, CH), BF16),
        in_specs=[VM, VM],
        out_specs=VM,
        compiler_params=params(),
        cost_estimate=cost(1 << 20, 3 << 20),
        name="join",
    )(keep, got)


def middle_kernel(parts_ref, out_ref):
    extra = None
    for k in range(16):
        ones, sums = unpack(parts_ref[k, MAIN : MAIN + EXTRA, :].astype(F32), 14)
        extra = (ones, sums) if extra is None else (extra[0] + ones, extra[1] + sums)
    for z in range(8):
        if z < 7:
            total = None
            for k in range(16):
                term = parts_ref[k, 32 * z : 32 * (z + 1), :].astype(F32)
                total = term if total is None else total + term
            ones = extra[0][2 * z : 2 * z + 2]
        else:
            total, ones = jnp.zeros((32, CH), F32), jnp.zeros((2, CH), F32)
        out_ref[z] = jnp.concatenate((total, ones, extra[1], jnp.zeros((4, CH), F32)), axis=0)


def middle(parts):
    return pl.pallas_call(
        middle_kernel,
        out_shape=shape((8, 40, CH), F32),
        in_specs=[VM],
        out_specs=VM,
        compiler_params=params(),
        cost_estimate=cost(1 << 20, 2 << 20),
        name="middle",
    )(parts)


def column(row):
    return jnp.transpose(jnp.broadcast_to(row, (CH, CH)))


def combine_kernel(block_ref, parts_ref, norm_ref, gain_ref, out_ref, gg_ref, sg_ref, coef_ref):
    total = jnp.sum(parts_ref[...], axis=0)
    main, ones, sums = total[0:32], total[32:34], total[34:36]
    inverse, count = norm_ref[1:2], norm_ref[2:3]
    scale = lax.rsqrt(count)
    sg_ref[...] = sums[0:1] * scale
    gg_ref[...] = sums[1:2] * scale
    coef_ref[0] = column(gain_ref[...] * inverse * scale)
    coef_ref[1] = column(sums[0:1] / count)
    coef_ref[2] = column(sums[1:2] / count)
    mine = pl.ds(pl.multiple_of(block_ref[0] * 8, 8), 8)
    factor, first, second = coef_ref[0, mine, :], coef_ref[1, mine, :], coef_ref[2, mine, :]
    values = []
    for i in range(2):
        base, cross = main[16 * i : 16 * i + 8], main[16 * i + 8 : 16 * i + 16]
        values.append(factor * (base - first * ones[i : i + 1] - second * cross))
    out_ref[...] = jnp.concatenate(values, axis=0).astype(BF16)


def combine(block, parts, norm, gain):
    return pl.pallas_call(
        combine_kernel,
        out_shape=(shape((16, CH), BF16), shape((1, CH), F32), shape((1, CH), F32)),
        in_specs=[SM] + [VM] * 3,
        out_specs=(VM,) * 3,
        scratch_shapes=[pltpu.VMEM((3, CH, CH), F32)],
        compiler_params=params(),
        cost_estimate=cost(1 << 20, 1 << 20),
        name="combine",
    )(block, parts, norm, gain)


def grad_kernel(
    sends_ref, parts_ref, norm_ref, gain_ref, conv_ref, ga_ref, mask_ref, out_ref, low_ref, high_ref, *, faces
):
    totals = jnp.sum(parts_ref[...], axis=0)[34:36]
    mean, inverse, count = norm_ref[0:1], norm_ref[1:2], norm_ref[2:3]
    factor = gain_ref[...] * inverse
    for s in range(SLOTS):
        normed = (conv_ref[s] - mean) * inverse
        inner = ga_ref[s] - (totals[0:1] + normed * totals[1:2]) / count
        out_ref[s] = (factor * inner * mask_ref[s].astype(F32)).astype(BF16)
    pick_x(sends_ref, out_ref, low_ref, high_ref, faces)


def grad(sends_x, parts, norm, gain, conv_out, ga, mask, faces):
    return pl.pallas_call(
        functools.partial(grad_kernel, faces=faces),
        out_shape=(shape((SLOTS, VOX, CH), BF16),) + x_shapes(faces),
        in_specs=[SM] + [VM] * 6,
        out_specs=(VM,) * 3,
        compiler_params=params(),
        cost_estimate=cost(4 << 20, 4 << 20),
        name="grad_conv",
    )(sends_x, parts, norm, gain, conv_out, ga, mask)


def finish_kernel(core_ref, mine_ref, other_ref, out_ref):
    for half in (0, 1):
        here = core_ref[0] == half
        for z in range(7):
            pairs = []
            for k in range(16):
                rows = slice(16 * z, 16 * (z + 1))
                pairs.append(jnp.where(here, mine_ref[k, rows, :], other_ref[k, rows, :]).astype(F32))
            for i in range(2):
                tap = 13 * half + 2 * z + i
                if half == 1 and tap == 13:
                    continue
                rows = jnp.concatenate([pair[8 * i : 8 * i + 8] for pair in pairs], axis=0)
                out_ref[tap] = jnp.transpose(rows)


def finish(core, mine, other):
    return pl.pallas_call(
        finish_kernel,
        out_shape=shape((27, CH, CH), F32),
        in_specs=[SM, VM, VM],
        out_specs=VM,
        compiler_params=params(),
        cost_estimate=cost(1 << 20, 3 << 20),
        name="finish",
    )(core, mine, other)


def spread(value, axes):
    size = axis_size(axes)
    return lax.all_to_all(jnp.broadcast_to(value[None], (size,) + value.shape), axes, 0, 0)


def all_sum_parts(value):
    return spread(jnp.sum(spread(value, ("z", "c")), axis=0), CROSS)


def swap(value):
    return lax.ppermute(value, "c", [(0, 1), (1, 0)])


def turn_kernel(w_ref, out_ref):
    for t in range(27):
        rows = slice((t % 9) * CH, (t % 9 + 1) * CH)
        out_ref[t // 9, rows, :] = jnp.transpose(w_ref[26 - t].astype(F32)).astype(BF16)


def turn(weight):
    return pl.pallas_call(
        turn_kernel,
        out_shape=shape((3, 9 * CH, CH), BF16),
        in_specs=[VM],
        out_specs=VM,
        compiler_params=params(),
        cost_estimate=cost(1 << 20, 2 << 20),
        name="turn",
    )(weight)


def shards(
    features,
    occupancy,
    counts,
    kernel_map,
    x_send,
    y_send,
    weight,
    norm_gain,
    norm_shift,
    cotangent,
):
    row_map, sends_x, sends_y = kernel_map[0, 0], x_send[0, 0], y_send[0, 0]
    gain, shift = norm_gain.reshape(1, CH), norm_shift.reshape(1, CH)
    core = lax.axis_index("c").reshape(1)
    block = lax.axis_index(CROSS).reshape(1)
    ahead = weight.reshape(3, 9 * CH, CH)

    def first(faces):
        own, mask, low, high = prepare(counts, sends_x, features[0, 0], occupancy[0, 0], faces)
        later, low, high = lax.optimization_barrier((weight, low, high))
        xl, xu = neighbours(low, high, ("xh", "y"))
        xl, xu, turned = lax.optimization_barrier((xl, xu, turn(later)))
        low, high = pick_y(sends_y, own, xl, xu, faces)
        yl, yu = neighbours(low, high, ("xl", "z", "c"))
        conv_out, x9, stats = conv(row_map, own, xl, xu, yl, yu, ahead, mask, True, faces)
        return conv_out, x9, mask, turned, all_sum_parts(stats)

    def second(conv_out, x9, mask, turned, stats, faces):
        activations, ga, norm, keep, send = wgrad(
            core, stats, conv_out, cotangent[0, 0], mask, gain, shift, x9
        )
        parts = lax.all_to_all(join(keep, swap(send)), CROSS, 0, 0)
        parts = lax.all_to_all(middle(parts), "z", 0, 0)
        grads, low, high = grad(sends_x, parts, norm, gain, conv_out, ga, mask, faces)
        xl, xu = neighbours(low, high, ("xh", "y"))
        parts, xl, xu = lax.optimization_barrier((parts, xl, xu))
        value, gain_grad, shift_grad = combine(block, parts, norm, gain)
        mine = spread(value, ("z",)).reshape(8 * 16, CH)[: 7 * 16]
        low, high = pick_y(sends_y, grads, xl, xu, faces)
        mine, low, high = lax.optimization_barrier((mine, low, high))
        yl, yu = neighbours(low, high, ("xl", "z", "c"))
        mine = spread(mine, CROSS)
        features_grad = conv(row_map, grads, xl, xu, yl, yu, turned, mask, False, faces)
        mine, features_grad = lax.optimization_barrier((mine, features_grad))
        weight_grad = finish(core, mine, swap(mine))
        return activations, features_grad, weight_grad, gain_grad, shift_grad

    state = first(True)
    misfits = jnp.sum(state[4][:, 3, 0])
    activations, features_grad, weight_grad, gain_grad, shift_grad = lax.cond(
        misfits > 0,
        lambda *_: second(*first(False), False),
        lambda *given: second(*given, True),
        *state,
    )
    return (
        activations[None, None],
        features_grad[None, None],
        weight_grad,
        gain_grad.reshape(CH),
        shift_grad.reshape(CH),
    )


def solution(mesh):
    fine = jax.sharding.Mesh(mesh.devices.reshape(2, 4, 2, 8, 2), ("xh", "y", "xl", "z", "c"))
    gx, gy = ("xh", "y"), ("xl", "z", "c")
    tiles = P(gx, gy, None, None, None)
    lists = P(gx, gy, None, None)
    return jax.shard_map(
        shards,
        mesh=fine,
        in_specs=(tiles, lists, P(gx, gy), lists, lists, lists, P(), P(), P(), tiles),
        out_specs=(tiles, tiles, P(), P(), P()),
        check_vma=False,
    )
```

```python
import functools

import jax
import jax.numpy as jnp
from jax import lax
from jax.experimental import pallas as pl
from jax.experimental.pallas import tpu as pltpu
from jax.sharding import PartitionSpec as P

EDGE = 8
PLANE = 64
VOX = 512
CH = 128
SLOTS = 4
HX = 2
HY = 4
EPSILON = 1e-05
F32 = jnp.float32
BF16 = jnp.bfloat16

VM = pl.BlockSpec(memory_space=pltpu.VMEM)
SM = pl.BlockSpec(memory_space=pltpu.SMEM)
MAIN = 224
EXTRA = 48
FACE_ROWS = HY * PLANE + 16
MIB = 1024 * 1024
CROSS = ("xh", "y", "xl")


def params(limit=20):
    return pltpu.CompilerParams(vmem_limit_bytes=limit * MIB)


def cost(flops, moved):
    return pl.CostEstimate(flops=flops, bytes_accessed=moved, transcendentals=0)


def shape(dims, kind):
    return jax.ShapeDtypeStruct(dims, kind)


def pick_x(sends_ref, own_ref, low_ref, high_ref, faces):
    for side, out_ref in ((0, low_ref), (1, high_ref)):
        start, stop = (0, VOX) if not faces else ((0, PLANE), (VOX - PLANE, VOX))[side]
        for k in range(HX):
            row = sends_ref[side, k]
            brick = own_ref[jnp.minimum(row, SLOTS - 1), start:stop, :]
            out_ref[k] = jnp.where(row < SLOTS, brick, jnp.zeros_like(brick))


def x_shapes(faces):
    send = shape((HX, PLANE if faces else VOX, CH), BF16)
    return (send, send)


def prepare_kernel(
    counts_ref, sends_ref, feat_ref, occ_ref, own_ref, mask_ref, low_ref, high_ref, *, faces
):
    for s in range(SLOTS):
        live = (s < counts_ref[0, 0]).astype(F32)
        for k in range(VOX // CH):
            row = occ_ref[s : s + 1, k * CH : (k + 1) * CH].astype(F32) * live
            column = jnp.transpose(jnp.broadcast_to(row, (CH, CH)))
            rows = pl.ds(k * CH, CH)
            mask_ref[s, rows, :] = column.astype(BF16)
            own_ref[s, rows, :] = (feat_ref[s, rows, :].astype(F32) * column).astype(BF16)
    pick_x(sends_ref, own_ref, low_ref, high_ref, faces)


def prepare(counts, sends_x, features, occupancy, faces):
    return pl.pallas_call(
        functools.partial(prepare_kernel, faces=faces),
        out_shape=(shape((SLOTS, VOX, CH), BF16),) * 2 + x_shapes(faces),
        in_specs=[SM, SM, VM, VM],
        out_specs=(VM, VM, VM, VM),
        compiler_params=params(),
        cost_estimate=cost(1 << 20, 2 << 20),
        name="prepare",
    )(counts, sends_x, features, occupancy)


def pick_y_kernel(sends_ref, own_ref, xl_ref, xu_ref, low_ref, high_ref):
    for side, out_ref in ((0, low_ref), (1, high_ref)):
        for k in range(HY):
            row = sends_ref[side, k]

            @pl.when(row < SLOTS)
            def _():
                out_ref[k] = own_ref[jnp.minimum(row, SLOTS - 1)]

            @pl.when((row >= SLOTS) & (row < SLOTS + HX))
            def _():
                out_ref[k] = xl_ref[jnp.clip(row - SLOTS, 0, HX - 1)]

            @pl.when((row >= SLOTS + HX) & (row < SLOTS + 2 * HX))
            def _():
                out_ref[k] = xu_ref[jnp.clip(row - SLOTS - HX, 0, HX - 1)]

            @pl.when(row >= SLOTS + 2 * HX)
            def _():
                out_ref[k] = jnp.zeros((VOX, CH), BF16)


def pick_y_faces_kernel(sends_ref, own_ref, xl_ref, xu_ref, low_ref, high_ref):
    lines = lax.broadcasted_iota(jnp.int32, (16, CH), 0)
    for side, out_ref in ((0, low_ref), (1, high_ref)):
        skip = 0 if side == 0 else PLANE - 16

        def edge(block):
            block = block.astype(F32)
            return block[:EDGE] if side == 0 else block[EDGE:]

        origin = jnp.zeros((16, CH), F32)
        for k in range(HY):
            row = sends_ref[side, k]
            rows = pl.ds(k * PLANE, PLANE)
            lower = (row >= SLOTS) & (row < SLOTS + HX)
            upper = (row >= SLOTS + HX) & (row < SLOTS + 2 * HX)
            code = jnp.where(lower, 1.0, jnp.where(upper, 2.0, 0.0))
            origin = jnp.where(lines == k, code, origin)

            @pl.when(row < SLOTS)
            def _():
                brick = jnp.minimum(row, SLOTS - 1)
                parts = [
                    edge(own_ref[brick, a * PLANE + skip : a * PLANE + skip + 16, :])
                    for a in range(EDGE)
                ]
                out_ref[rows, :] = jnp.concatenate(parts, axis=0).astype(BF16)

            @pl.when(lower)
            def _():
                part = edge(xl_ref[jnp.clip(row - SLOTS, 0, HX - 1), skip : skip + 16, :])
                empty = jnp.zeros((PLANE - EDGE, CH), F32)
                out_ref[rows, :] = jnp.concatenate((empty, part), axis=0).astype(BF16)

            @pl.when(upper)
            def _():
                part = edge(xu_ref[jnp.clip(row - SLOTS - HX, 0, HX - 1), skip : skip + 16, :])
                empty = jnp.zeros((PLANE - EDGE, CH), F32)
                out_ref[rows, :] = jnp.concatenate((part, empty), axis=0).astype(BF16)

            @pl.when(row >= SLOTS + 2 * HX)
            def _():
                out_ref[rows, :] = jnp.zeros((PLANE, CH), BF16)

        out_ref[HY * PLANE : FACE_ROWS, :] = origin.astype(BF16)


def pick_y(sends_y, own, xl, xu, faces):
    send = shape((FACE_ROWS, CH) if faces else (HY, VOX, CH), BF16)
    return pl.pallas_call(
        pick_y_faces_kernel if faces else pick_y_kernel,
        out_shape=(send, send),
        in_specs=[SM, VM, VM, VM],
        out_specs=(VM, VM),
        compiler_params=params(),
        cost_estimate=cost(1 << 20, 2 << 20),
        name="pick_y",
    )(sends_y, own, xl, xu)


def axis_size(axes):
    size = 1
    for axis in axes:
        size *= lax.axis_size(axis)
    return size


def neighbours(low, high, axis):
    size = axis_size(axis)
    up = [(i, i + 1) for i in range(size - 1)]
    down = [(j, i) for i, j in up]
    return lax.ppermute(high, axis, up), lax.ppermute(low, axis, down)


def fill_columns(map_ref, slot, table_ref, x9_ref):
    sub = lax.broadcasted_iota(jnp.int32, (EDGE + 2, EDGE, CH), 1)
    for a in range(-1, EDGE + 1):
        move = -1 if a < 0 else (1 if a >= EDGE else 0)
        base = (a % EDGE) * PLANE
        spans = []
        for r in (-1, 0, 1):
            tap = 9 * (move + 1) + r + 1
            before = table_ref[map_ref[slot, tap], base + 48 : base + 64, :].astype(F32)[8:]
            middle = table_ref[map_ref[slot, tap + 3], base : base + 64, :].astype(F32)
            after = table_ref[map_ref[slot, tap + 6], base : base + 16, :].astype(F32)[:8]
            spans.append(jnp.concatenate((before, middle, after), axis=0).reshape(EDGE + 2, EDGE, CH))
        low, centre, high = spans
        down = pltpu.roll(jnp.where(sub == EDGE - 1, low, centre), 1, 1)
        up = pltpu.roll(jnp.where(sub == 0, high, centre), EDGE - 1, 1)
        for r, source in ((-1, down), (0, centre), (1, up)):
            for q in (-1, 0, 1):
                rows = source[q + 1 : q + 1 + EDGE].reshape(PLANE, CH).astype(BF16)
                lane = (3 * (q + 1) + r + 1) * CH
                x9_ref[(a + 1) * PLANE : (a + 2) * PLANE, lane : lane + CH] = rows


def fill_whole(table_ref, refs):
    start = 0
    for ref in refs:
        table_ref[start : start + ref.shape[0]] = ref[...]
        start += ref.shape[0]


def fill_faces(table_ref, refs):
    own_ref, xl_ref, xu_ref, yl_ref, yu_ref = refs
    table_ref[0:SLOTS] = own_ref[...]
    for k in range(HX):
        table_ref[SLOTS + k, VOX - PLANE : VOX, :] = xl_ref[k]
        table_ref[SLOTS + HX + k, 0:PLANE, :] = xu_ref[k]
    empty = jnp.zeros((EDGE, CH), F32)
    first = SLOTS + 2 * HX
    for k in range(HY):
        low = yl_ref[k * PLANE : (k + 1) * PLANE, :].astype(F32)
        high = yu_ref[k * PLANE : (k + 1) * PLANE, :].astype(F32)
        for a in range(EDGE):
            part = slice(a * EDGE, (a + 1) * EDGE)
            base = a * PLANE
            table_ref[first + k, base + 48 : base + 64, :] = jnp.concatenate(
                (empty, low[part]), axis=0
            ).astype(BF16)
            table_ref[first + HY + k, base : base + 16, :] = jnp.concatenate(
                (high[part], empty), axis=0
            ).astype(BF16)


def count_misfits(rows, yl_ref, yu_ref):
    lane = lax.broadcasted_iota(jnp.int32, rows.shape, 1)
    within = lane - jnp.where(lane >= 9, 9, 0) - jnp.where(lane >= 18, 9, 0)
    not_down, not_up = lane >= 9, lane < 18
    bad = (rows >= SLOTS) & (rows < SLOTS + HX) & not_down
    bad = bad | ((rows >= SLOTS + HX) & (rows < SLOTS + 2 * HX) & not_up)
    for start, ref, wrong in (
        (SLOTS + 2 * HX, yl_ref, within >= 3),
        (SLOTS + 2 * HX + HY, yu_ref, within < 6),
    ):
        origin = ref[HY * PLANE : FACE_ROWS, :].astype(F32)
        for k in range(HY):
            code = jnp.broadcast_to(origin[k : k + 1, 0 : rows.shape[1]], rows.shape)
            fault = wrong | ((code == 1.0) & not_down) | ((code == 2.0) & not_up)
            bad = bad | ((rows == start + k) & fault)
    return jnp.sum(jnp.where(bad, 1.0, 0.0))


def conv_kernel(
    map_ref, rows_ref, own_ref, xl_ref, xu_ref, yl_ref, yu_ref, w_ref, mask_ref,
    out_ref, x9_out, stat_ref, table_ref, x9_ref, sems,
):
    fill_faces(table_ref, (own_ref, xl_ref, xu_ref, yl_ref, yu_ref))
    table_ref[16] = jnp.zeros((VOX, CH), BF16)
    sums = [jnp.zeros((1, CH), F32)] * 3
    copies = []

    def columns(slot):
        fill_columns(map_ref, slot, table_ref, x9_ref.at[slot])
        copies.append(pltpu.make_async_copy(x9_ref.at[slot], x9_out.at[slot], sems.at[slot]))
        copies[-1].start()

    columns(0)
    for slot in range(SLOTS):
        if slot + 1 < SLOTS:
            columns(slot + 1)
        total = None
        for p in range(3):
            term = jnp.dot(
                x9_ref[slot, p * PLANE : p * PLANE + VOX, :], w_ref[p], preferred_element_type=F32
            )
            total = term if total is None else total + term
        mask = mask_ref[slot].astype(F32)
        masked = total * mask
        out_ref[slot] = total
        terms = (masked, masked * total, mask)
        sums = [s + jnp.sum(term, axis=0, keepdims=True) for s, term in zip(sums, terms)]
    misfits = count_misfits(rows_ref[...], yl_ref, yu_ref)
    sums.append(jnp.broadcast_to(misfits, (1, CH)))
    stat_ref[...] = jnp.concatenate(sums + [jnp.zeros((4, CH), F32)], axis=0)
    for copy in copies:
        copy.wait()


def conv(row_map, own, xl, xu, yl, yu, weight, mask):
    columns = (SLOTS, 10 * PLANE, 9 * CH)
    return pl.pallas_call(
        conv_kernel,
        out_shape=(shape((SLOTS, VOX, CH), F32), shape(columns, BF16), shape((8, CH), F32)),
        in_specs=[SM] + [VM] * 8,
        out_specs=(VM, pl.BlockSpec(memory_space=pl.ANY), VM),
        scratch_shapes=[
            pltpu.VMEM((17, VOX, CH), BF16),
            pltpu.VMEM(columns, BF16),
            pltpu.SemaphoreType.DMA((SLOTS,)),
        ],
        compiler_params=params(28),
        cost_estimate=cost(6000000000, 12 << 20),
        name="forward_conv",
    )(row_map, row_map, own, xl, xu, yl, yu, weight, mask)


def step_kernel(
    map_ref, rows_ref, own_ref, xl_ref, xu_ref, yl_ref, yu_ref, w_ref, mask_ref, *rest, forward, faces
):
    slot = pl.program_id(0)
    if forward:
        out_ref, x9_out, stat_ref, table_ref = rest
        x9_ref = x9_out.at[0]
    else:
        out_ref, table_ref, x9_ref = rest

    @pl.when(slot == 0)
    def _():
        fill = fill_faces if faces else fill_whole
        fill(table_ref, (own_ref, xl_ref, xu_ref, yl_ref, yu_ref))
        table_ref[16] = jnp.zeros((VOX, CH), BF16)
        if forward:
            stat_ref[...] = jnp.zeros_like(stat_ref)
            if faces:
                stat_ref[3:4] = jnp.broadcast_to(
                    count_misfits(rows_ref[...], yl_ref, yu_ref), (1, CH)
                )

    fill_columns(map_ref, slot, table_ref, x9_ref)
    total = None
    for p in range(3):
        term = jnp.dot(
            x9_ref[p * PLANE : p * PLANE + VOX, :], w_ref[p], preferred_element_type=F32
        )
        total = term if total is None else total + term
    mask = mask_ref[0].astype(F32)
    masked = total * mask
    if forward:
        out_ref[0] = total
        stat_ref[0:1] += jnp.sum(masked, axis=0, keepdims=True)
        stat_ref[1:2] += jnp.sum(masked * total, axis=0, keepdims=True)
        stat_ref[2:3] += jnp.sum(mask, axis=0, keepdims=True)
    else:
        out_ref[0] = masked.astype(BF16)


def whole(*dims):
    return pl.BlockSpec(dims, lambda s: (0,) * len(dims))


def conv_steps(row_map, own, xl, xu, yl, yu, weight, mask, forward, faces):
    brick = pl.BlockSpec((1, VOX, CH), lambda s: (s, 0, 0))
    scratch = [pltpu.VMEM((17, VOX, CH), BF16)]
    if forward:
        out_shape = (
            shape((SLOTS, VOX, CH), F32),
            shape((SLOTS, 10 * PLANE, 9 * CH), BF16),
            shape((8, CH), F32),
        )
        out_specs = (brick, pl.BlockSpec((1, 10 * PLANE, 9 * CH), lambda s: (s, 0, 0)), whole(8, CH))
    else:
        out_shape = shape((SLOTS, VOX, CH), BF16)
        out_specs = brick
        scratch.append(pltpu.VMEM((10 * PLANE, 9 * CH), BF16))
    return pl.pallas_call(
        functools.partial(step_kernel, forward=forward, faces=faces),
        grid=(SLOTS,),
        out_shape=out_shape,
        in_specs=[
            SM,
            whole(*row_map.shape),
            whole(*own.shape),
            whole(*xl.shape),
            whole(*xu.shape),
            whole(*yl.shape),
            whole(*yu.shape),
            whole(3, 9 * CH, CH),
            brick,
        ],
        out_specs=out_specs,
        scratch_shapes=scratch,
        compiler_params=params(24),
        cost_estimate=cost(6000000000, 12 << 20),
        name="forward_steps" if forward else "transposed_conv",
    )(row_map, row_map, own, xl, xu, yl, yu, weight, mask)


def norm_terms(stats):
    count = stats[2:3]
    mean = stats[0:1] / count
    variance = stats[1:2] / count - mean * mean
    return count, mean, lax.rsqrt(variance + EPSILON)


def activate(slot, stats, cot_ref, conv_ref, mask_ref, gain_ref, shift_ref, act_ref, ga_ref, g_ref):
    count, mean, inverse = stats
    mask = mask_ref[slot].astype(F32)
    normed = (conv_ref[slot] - mean) * inverse
    pre = gain_ref[...] * normed + shift_ref[...]
    sig = jax.nn.sigmoid(pre)
    act_ref[slot] = (pre * sig * mask).astype(BF16)
    ga = cot_ref[slot].astype(F32) * mask * sig * (1.0 + pre * (1.0 - sig))
    ga_ref[slot] = ga
    nm = normed * mask
    for k in range(VOX // CH):
        rows = slice(k * CH, (k + 1) * CH)
        g_ref[slot, 0:CH, rows] = jnp.transpose(ga[rows]).astype(BF16)
        g_ref[slot, CH : 2 * CH, rows] = jnp.transpose(nm[rows]).astype(BF16)
        g_ref[slot, 2 * CH : 2 * CH + 16, rows] = jnp.transpose(mask[rows])[0:16].astype(BF16)
    sums = (jnp.sum(ga, axis=0, keepdims=True), jnp.sum(ga * normed, axis=0, keepdims=True))
    return jnp.concatenate(sums, axis=0)


def split(value, pieces):
    parts = []
    for _ in range(pieces):
        part = value.astype(BF16).astype(F32)
        parts.append(part)
        value = value - part
    return parts


def pack(ones, sums):
    parts = split(ones, 2) + split(sums[0:1], 3) + split(sums[1:2], 3)
    used = sum(part.shape[0] for part in parts)
    rows = -(-used // 16) * 16
    if used < rows:
        parts.append(jnp.zeros((rows - used, CH), F32))
    return jnp.concatenate(parts, axis=0).astype(BF16)


def unpack(rows, taps):
    ones = rows[0:taps] + rows[taps : 2 * taps]
    at = 2 * taps
    first = rows[at : at + 1] + rows[at + 1 : at + 2] + rows[at + 2 : at + 3]
    second = rows[at + 3 : at + 4] + rows[at + 4 : at + 5] + rows[at + 5 : at + 6]
    return ones, jnp.concatenate((first, second), axis=0)


def wgrad_kernel(
    core_ref, stat_ref, conv_ref, cot_ref, mask_ref, gain_ref, shift_ref, x9_hbm,
    act_ref, ga_ref, norm_ref, keep_ref, send_ref, g_ref, x9_ref, hold_ref, sems, *, unroll
):
    copies = [
        pltpu.make_async_copy(x9_hbm.at[s], x9_ref.at[s], sems.at[s]) for s in range(SLOTS)
    ]
    for copy in copies:
        copy.start()
    stats = norm_terms(jnp.sum(stat_ref[...], axis=0))
    count, mean, inverse = stats
    norm_ref[...] = jnp.concatenate((mean, inverse, count, jnp.zeros((5, CH), F32)), axis=0)

    def add_sums(s, sums):
        return sums + activate(
            s, stats, cot_ref, conv_ref, mask_ref, gain_ref, shift_ref, act_ref, ga_ref, g_ref
        )

    sums = lax.fori_loop(0, SLOTS, add_sums, jnp.zeros((2, CH), F32), unroll=unroll)
    for copy in copies:
        copy.wait()
    ones = [None] * 27
    for p in range(3):
        for q in range(0, 9, 2):
            width = min(2, 9 - q)
            lanes = slice(q * CH, (q + width) * CH)

            def add_term(s, total):
                rows = slice(p * PLANE, p * PLANE + VOX)
                return total + jnp.dot(
                    g_ref[s], x9_ref[s, rows, lanes], preferred_element_type=F32
                )

            if unroll:
                total = None
                for s in range(SLOTS):
                    total = add_term(s, 0.0 if total is None else total)
            else:
                empty = jnp.zeros((2 * CH + 16, width * CH), F32)
                total = lax.fori_loop(0, SLOTS, add_term, empty)
            for r in range(width):
                t = 9 * p + q + r
                tap = total[:, r * CH : (r + 1) * CH]
                ones[t] = tap[2 * CH : 2 * CH + 1]
                for half in (0, 1):
                    i = t - 13 * half
                    if 0 <= i < 14:
                        for k in range(16):
                            pair = jnp.concatenate(
                                (tap[8 * k : 8 * k + 8], tap[CH + 8 * k : CH + 8 * k + 8]), axis=0
                            )
                            row = k * MAIN + i * 16
                            hold_ref[half, row : row + 16, :] = pair
    for half in (0, 1):
        rows = jnp.concatenate(ones[13 * half : 13 * half + 14], axis=0)
        hold_ref[half, 16 * MAIN : 16 * MAIN + EXTRA, :] = pack(rows, sums).astype(F32)
    core = core_ref[0]
    keep_ref[...] = hold_ref[core]
    send_ref[...] = hold_ref[1 - core].astype(BF16)


def wgrad(core, stats, conv_out, cotangent, mask, gain, shift, x9, unroll):
    rows = 16 * MAIN + EXTRA
    return pl.pallas_call(
        functools.partial(wgrad_kernel, unroll=unroll),
        out_shape=(
            shape((SLOTS, VOX, CH), BF16),
            shape((SLOTS, VOX, CH), F32),
            shape((8, CH), F32),
            shape((rows, CH), F32),
            shape((rows, CH), BF16),
        ),
        in_specs=[SM] + [VM] * 6 + [pl.BlockSpec(memory_space=pl.ANY)],
        out_specs=(VM,) * 5,
        scratch_shapes=[
            pltpu.VMEM((SLOTS, 2 * CH + 16, VOX), BF16),
            pltpu.VMEM((SLOTS, 10 * PLANE, 9 * CH), BF16),
            pltpu.VMEM((2, rows, CH), F32),
            pltpu.SemaphoreType.DMA((SLOTS,)),
        ],
        compiler_params=params(28),
        cost_estimate=cost(6000000000, 12 << 20),
        name="weight_terms",
    )(core, stats, conv_out, cotangent, mask, gain, shift, x9)


def join_kernel(keep_ref, got_ref, out_ref):
    for k in range(16):
        rows = slice(k * MAIN, (k + 1) * MAIN)
        out_ref[k, 0:MAIN, :] = (keep_ref[rows, :] + got_ref[rows, :].astype(F32)).astype(BF16)
    rows = slice(16 * MAIN, 16 * MAIN + EXTRA)
    ones, sums = unpack(keep_ref[rows, :], 14)
    more_ones, more_sums = unpack(got_ref[rows, :].astype(F32), 14)
    extra = pack(ones + more_ones, sums + more_sums)
    for k in range(16):
        out_ref[k, MAIN : MAIN + EXTRA, :] = extra


def join(keep, got):
    return pl.pallas_call(
        join_kernel,
        out_shape=shape((16, MAIN + EXTRA, CH), BF16),
        in_specs=[VM, VM],
        out_specs=VM,
        compiler_params=params(),
        cost_estimate=cost(1 << 20, 3 << 20),
        name="join",
    )(keep, got)


def middle_kernel(parts_ref, out_ref):
    extra = None
    for k in range(16):
        ones, sums = unpack(parts_ref[k, MAIN : MAIN + EXTRA, :].astype(F32), 14)
        extra = (ones, sums) if extra is None else (extra[0] + ones, extra[1] + sums)
    for z in range(8):
        if z < 7:
            total = None
            for k in range(16):
                term = parts_ref[k, 32 * z : 32 * (z + 1), :].astype(F32)
                total = term if total is None else total + term
            ones = extra[0][2 * z : 2 * z + 2]
        else:
            total, ones = jnp.zeros((32, CH), F32), jnp.zeros((2, CH), F32)
        out_ref[z] = jnp.concatenate((total, ones, extra[1], jnp.zeros((4, CH), F32)), axis=0)


def middle(parts):
    return pl.pallas_call(
        middle_kernel,
        out_shape=shape((8, 40, CH), F32),
        in_specs=[VM],
        out_specs=VM,
        compiler_params=params(),
        cost_estimate=cost(1 << 20, 2 << 20),
        name="middle",
    )(parts)


def column(row):
    return jnp.transpose(jnp.broadcast_to(row, (CH, CH)))


def combine_kernel(block_ref, parts_ref, norm_ref, gain_ref, out_ref, gg_ref, sg_ref, coef_ref):
    total = jnp.sum(parts_ref[...], axis=0)
    main, ones, sums = total[0:32], total[32:34], total[34:36]
    inverse, count = norm_ref[1:2], norm_ref[2:3]
    scale = lax.rsqrt(count)
    sg_ref[...] = sums[0:1] * scale
    gg_ref[...] = sums[1:2] * scale
    coef_ref[0] = column(gain_ref[...] * inverse * scale)
    coef_ref[1] = column(sums[0:1] / count)
    coef_ref[2] = column(sums[1:2] / count)
    mine = pl.ds(pl.multiple_of(block_ref[0] * 8, 8), 8)
    factor, first, second = coef_ref[0, mine, :], coef_ref[1, mine, :], coef_ref[2, mine, :]
    values = []
    for i in range(2):
        base, cross = main[16 * i : 16 * i + 8], main[16 * i + 8 : 16 * i + 16]
        values.append(factor * (base - first * ones[i : i + 1] - second * cross))
    out_ref[...] = jnp.concatenate(values, axis=0).astype(BF16)


def combine(block, parts, norm, gain):
    return pl.pallas_call(
        combine_kernel,
        out_shape=(shape((16, CH), BF16), shape((1, CH), F32), shape((1, CH), F32)),
        in_specs=[SM] + [VM] * 3,
        out_specs=(VM,) * 3,
        scratch_shapes=[pltpu.VMEM((3, CH, CH), F32)],
        compiler_params=params(),
        cost_estimate=cost(1 << 20, 1 << 20),
        name="combine",
    )(block, parts, norm, gain)


def grad_kernel(
    sends_ref, parts_ref, norm_ref, gain_ref, conv_ref, ga_ref, mask_ref, out_ref, low_ref, high_ref, *, faces
):
    totals = jnp.sum(parts_ref[...], axis=0)[34:36]
    mean, inverse, count = norm_ref[0:1], norm_ref[1:2], norm_ref[2:3]
    factor = gain_ref[...] * inverse
    for s in range(SLOTS):
        normed = (conv_ref[s] - mean) * inverse
        inner = ga_ref[s] - (totals[0:1] + normed * totals[1:2]) / count
        out_ref[s] = (factor * inner * mask_ref[s].astype(F32)).astype(BF16)
    pick_x(sends_ref, out_ref, low_ref, high_ref, faces)


def grad(sends_x, parts, norm, gain, conv_out, ga, mask, faces):
    return pl.pallas_call(
        functools.partial(grad_kernel, faces=faces),
        out_shape=(shape((SLOTS, VOX, CH), BF16),) + x_shapes(faces),
        in_specs=[SM] + [VM] * 6,
        out_specs=(VM,) * 3,
        compiler_params=params(),
        cost_estimate=cost(4 << 20, 4 << 20),
        name="grad_conv",
    )(sends_x, parts, norm, gain, conv_out, ga, mask)


def finish_kernel(core_ref, mine_ref, other_ref, out_ref):
    for half in (0, 1):
        here = core_ref[0] == half
        for z in range(7):
            pairs = []
            for k in range(16):
                rows = slice(16 * z, 16 * (z + 1))
                pairs.append(jnp.where(here, mine_ref[k, rows, :], other_ref[k, rows, :]).astype(F32))
            for i in range(2):
                tap = 13 * half + 2 * z + i
                if half == 1 and tap == 13:
                    continue
                rows = jnp.concatenate([pair[8 * i : 8 * i + 8] for pair in pairs], axis=0)
                out_ref[tap] = jnp.transpose(rows)


def finish(core, mine, other):
    return pl.pallas_call(
        finish_kernel,
        out_shape=shape((27, CH, CH), F32),
        in_specs=[SM, VM, VM],
        out_specs=VM,
        compiler_params=params(),
        cost_estimate=cost(1 << 20, 3 << 20),
        name="finish",
    )(core, mine, other)


def spread(value, axes):
    size = axis_size(axes)
    return lax.all_to_all(jnp.broadcast_to(value[None], (size,) + value.shape), axes, 0, 0)


def all_sum_parts(value):
    return spread(jnp.sum(spread(value, ("z", "c")), axis=0), CROSS)


def swap(value):
    return lax.ppermute(value, "c", [(0, 1), (1, 0)])


def turn_kernel(w_ref, out_ref):
    for t in range(27):
        rows = slice((t % 9) * CH, (t % 9 + 1) * CH)
        out_ref[t // 9, rows, :] = jnp.transpose(w_ref[26 - t].astype(F32)).astype(BF16)


def turn(weight):
    return pl.pallas_call(
        turn_kernel,
        out_shape=shape((3, 9 * CH, CH), BF16),
        in_specs=[VM],
        out_specs=VM,
        compiler_params=params(),
        cost_estimate=cost(1 << 20, 2 << 20),
        name="turn",
    )(weight)


def shards(
    features,
    occupancy,
    counts,
    kernel_map,
    x_send,
    y_send,
    weight,
    norm_gain,
    norm_shift,
    cotangent,
):
    row_map, sends_x, sends_y = kernel_map[0, 0], x_send[0, 0], y_send[0, 0]
    gain, shift = norm_gain.reshape(1, CH), norm_shift.reshape(1, CH)
    core = lax.axis_index("c").reshape(1)
    block = lax.axis_index(CROSS).reshape(1)
    ahead = weight.reshape(3, 9 * CH, CH)

    def first(faces):
        own, mask, low, high = prepare(counts, sends_x, features[0, 0], occupancy[0, 0], faces)
        later, low, high = lax.optimization_barrier((weight, low, high))
        xl, xu = neighbours(low, high, ("xh", "y"))
        xl, xu, turned = lax.optimization_barrier((xl, xu, turn(later)))
        low, high = pick_y(sends_y, own, xl, xu, faces)
        yl, yu = neighbours(low, high, ("xl", "z", "c"))
        table = (row_map, own, xl, xu, yl, yu, ahead, mask)
        conv_out, x9, stats = conv(*table) if faces else conv_steps(*table, True, False)
        return conv_out, x9, mask, turned, all_sum_parts(stats)

    def second(conv_out, x9, mask, turned, stats, faces):
        activations, ga, norm, keep, send = wgrad(
            core, stats, conv_out, cotangent[0, 0], mask, gain, shift, x9, faces
        )
        parts = lax.all_to_all(join(keep, swap(send)), CROSS, 0, 0)
        parts = lax.all_to_all(middle(parts), "z", 0, 0)
        grads, low, high = grad(sends_x, parts, norm, gain, conv_out, ga, mask, faces)
        parts, low, high = lax.optimization_barrier((parts, low, high))
        xl, xu = neighbours(low, high, ("xh", "y"))
        value, gain_grad, shift_grad = combine(block, parts, norm, gain)
        mine = spread(value, ("z",)).reshape(8 * 16, CH)[: 7 * 16]
        low, high = pick_y(sends_y, grads, xl, xu, faces)
        mine, low, high = lax.optimization_barrier((mine, low, high))
        yl, yu = neighbours(low, high, ("xl", "z", "c"))
        mine = spread(mine, CROSS)
        features_grad = conv_steps(row_map, grads, xl, xu, yl, yu, turned, mask, False, faces)
        mine, features_grad = lax.optimization_barrier((mine, features_grad))
        weight_grad = finish(core, mine, swap(mine))
        return activations, features_grad, weight_grad, gain_grad, shift_grad

    state = first(True)
    misfits = jnp.sum(state[4][:, 3, 0])
    activations, features_grad, weight_grad, gain_grad, shift_grad = lax.cond(
        misfits > 0,
        lambda *_: second(*first(False), False),
        lambda *given: second(*given, True),
        *state,
    )
    return (
        activations[None, None],
        features_grad[None, None],
        weight_grad,
        gain_grad.reshape(CH),
        shift_grad.reshape(CH),
    )


def solution(mesh):
    fine = jax.sharding.Mesh(mesh.devices.reshape(2, 4, 2, 8, 2), ("xh", "y", "xl", "z", "c"))
    gx, gy = ("xh", "y"), ("xl", "z", "c")
    tiles = P(gx, gy, None, None, None)
    lists = P(gx, gy, None, None)
    return jax.shard_map(
        shards,
        mesh=fine,
        in_specs=(tiles, lists, P(gx, gy), lists, lists, lists, P(), P(), P(), tiles),
        out_specs=(tiles, tiles, P(), P(), P()),
        check_vma=False,
    )
```

```python
import functools

import jax
import jax.numpy as jnp
from jax import lax
from jax.experimental import pallas as pl
from jax.experimental.pallas import tpu as pltpu
from jax.sharding import PartitionSpec as P

EDGE = 8
PLANE = 64
VOX = 512
CH = 128
SLOTS = 4
HX = 2
HY = 4
EPSILON = 1e-05
F32 = jnp.float32
BF16 = jnp.bfloat16

VM = pl.BlockSpec(memory_space=pltpu.VMEM)
SM = pl.BlockSpec(memory_space=pltpu.SMEM)
MAIN = 224
EXTRA = 48
FACE_ROWS = HY * PLANE + 16
MIB = 1024 * 1024
CROSS = ("xh", "y", "xl")


def params(limit=20):
    return pltpu.CompilerParams(vmem_limit_bytes=limit * MIB)


def cost(flops, moved):
    return pl.CostEstimate(flops=flops, bytes_accessed=moved, transcendentals=0)


def shape(dims, kind):
    return jax.ShapeDtypeStruct(dims, kind)


def side_of(turn, odd):
    return odd if turn else 1 - odd


def lower_upper(odd, first, second):
    even = odd == 0
    return jnp.where(even, second, first), jnp.where(even, first, second)


def pick_x(place_ref, sends_ref, own_ref, first_ref, second_ref, faces):
    for turn, out_ref in ((0, first_ref), (1, second_ref)):
        side, rows = turn, slice(0, VOX)
        if faces:
            side = side_of(turn, place_ref[0])
            rows = pl.ds(pl.multiple_of(side * (VOX - PLANE), PLANE), PLANE)
        for k in range(HX):
            row = sends_ref[side, k]
            brick = own_ref[jnp.minimum(row, SLOTS - 1), rows, :]
            out_ref[k] = jnp.where(row < SLOTS, brick, jnp.zeros_like(brick))


def x_shapes(faces):
    send = shape((HX, PLANE if faces else VOX, CH), BF16)
    return (send, send)


def prepare_kernel(
    place_ref, counts_ref, sends_ref, feat_ref, occ_ref, own_ref, mask_ref, low_ref, high_ref, *, faces
):
    for s in range(SLOTS):
        live = (s < counts_ref[0, 0]).astype(F32)
        for k in range(VOX // CH):
            row = occ_ref[s : s + 1, k * CH : (k + 1) * CH].astype(F32) * live
            column = jnp.transpose(jnp.broadcast_to(row, (CH, CH)))
            rows = pl.ds(k * CH, CH)
            mask_ref[s, rows, :] = column.astype(BF16)
            own_ref[s, rows, :] = (feat_ref[s, rows, :].astype(F32) * column).astype(BF16)
    pick_x(place_ref, sends_ref, own_ref, low_ref, high_ref, faces)


def prepare(place, counts, sends_x, features, occupancy, faces):
    return pl.pallas_call(
        functools.partial(prepare_kernel, faces=faces),
        out_shape=(shape((SLOTS, VOX, CH), BF16),) * 2 + x_shapes(faces),
        in_specs=[SM, SM, SM, VM, VM],
        out_specs=(VM, VM, VM, VM),
        compiler_params=params(),
        cost_estimate=cost(1 << 20, 2 << 20),
        name="prepare",
    )(place, counts, sends_x, features, occupancy)


def pick_y_kernel(place_ref, sends_ref, own_ref, xl_ref, xu_ref, low_ref, high_ref):
    for side, out_ref in ((0, low_ref), (1, high_ref)):
        for k in range(HY):
            row = sends_ref[side, k]

            @pl.when(row < SLOTS)
            def _():
                out_ref[k] = own_ref[jnp.minimum(row, SLOTS - 1)]

            @pl.when((row >= SLOTS) & (row < SLOTS + HX))
            def _():
                out_ref[k] = xl_ref[jnp.clip(row - SLOTS, 0, HX - 1)]

            @pl.when((row >= SLOTS + HX) & (row < SLOTS + 2 * HX))
            def _():
                out_ref[k] = xu_ref[jnp.clip(row - SLOTS - HX, 0, HX - 1)]

            @pl.when(row >= SLOTS + 2 * HX)
            def _():
                out_ref[k] = jnp.zeros((VOX, CH), BF16)


def pick_y_faces_kernel(place_ref, sends_ref, own_ref, x1_ref, x2_ref, first_ref, second_ref):
    lines = lax.broadcasted_iota(jnp.int32, (16, CH), 0)
    odd = place_ref[0]
    for turn, out_ref in ((0, first_ref), (1, second_ref)):
        side = side_of(turn, place_ref[1])
        skip = side * (PLANE - 16)

        def piece(base):
            return pl.ds(pl.multiple_of(base + skip, 16), 16)

        def edge(block):
            block = block.astype(F32)
            return jnp.where(side == 0, block[:EDGE], block[EDGE:])

        origin = jnp.zeros((16, CH), F32)
        for k in range(HY):
            row = sends_ref[side, k]
            rows = pl.ds(k * PLANE, PLANE)
            lower = (row >= SLOTS) & (row < SLOTS + HX)
            upper = (row >= SLOTS + HX) & (row < SLOTS + 2 * HX)
            code = jnp.where(lower, 1.0, jnp.where(upper, 2.0, 0.0))
            origin = jnp.where(lines == k, code, origin)

            @pl.when(row < SLOTS)
            def _():
                brick = jnp.minimum(row, SLOTS - 1)
                parts = [edge(own_ref[brick, piece(a * PLANE), :]) for a in range(EDGE)]
                out_ref[rows, :] = jnp.concatenate(parts, axis=0).astype(BF16)

            @pl.when(lower | upper)
            def _():
                at = jnp.where(lower, row - SLOTS, row - SLOTS - HX)
                at = jnp.clip(at, 0, HX - 1)
                down, up = lower_upper(odd, x1_ref[at, piece(0), :], x2_ref[at, piece(0), :])
                part = edge(jnp.where(lower, down, up))
                empty = jnp.zeros((PLANE - 2 * EDGE, CH), F32)
                blank = jnp.zeros_like(part)
                front, back = jnp.where(lower, blank, part), jnp.where(lower, part, blank)
                out_ref[rows, :] = jnp.concatenate((front, empty, back), axis=0).astype(BF16)

            @pl.when(row >= SLOTS + 2 * HX)
            def _():
                out_ref[rows, :] = jnp.zeros((PLANE, CH), BF16)

        out_ref[HY * PLANE : FACE_ROWS, :] = origin.astype(BF16)


def pick_y(place, sends_y, own, xl, xu, faces):
    send = shape((FACE_ROWS, CH) if faces else (HY, VOX, CH), BF16)
    return pl.pallas_call(
        pick_y_faces_kernel if faces else pick_y_kernel,
        out_shape=(send, send),
        in_specs=[SM, SM, VM, VM, VM],
        out_specs=(VM, VM),
        compiler_params=params(),
        cost_estimate=cost(1 << 20, 2 << 20),
        name="pick_y",
    )(place, sends_y, own, xl, xu)


def axis_size(axes):
    size = 1
    for axis in axes:
        size *= lax.axis_size(axis)
    return size


def neighbours(first, second, axes, faces):
    size = axis_size(axes)
    if faces:
        pairs = [[(i, i + 1) for i in range(turn, size - 1, 2)] for turn in (0, 1)]
        one, two = [pair + [(j, i) for i, j in pair] for pair in pairs]
        return lax.ppermute(first, axes, one), lax.ppermute(second, axes, two)
    up = [(i, i + 1) for i in range(size - 1)]
    down = [(j, i) for i, j in up]
    return lax.ppermute(second, axes, up), lax.ppermute(first, axes, down)


def fill_plane(map_ref, slot, table_ref, x9_ref, move, base, row):
    sub = lax.broadcasted_iota(jnp.int32, (EDGE + 2, EDGE, CH), 1)
    spans = []
    for r in (-1, 0, 1):
        tap = 9 * (move + 1) + r + 1
        first, whole_plane, last = pl.ds(base + 48, 16), pl.ds(base, PLANE), pl.ds(base, 16)
        before = table_ref[map_ref[slot, tap], first, :].astype(F32)[8:]
        middle = table_ref[map_ref[slot, tap + 3], whole_plane, :].astype(F32)
        after = table_ref[map_ref[slot, tap + 6], last, :].astype(F32)[:8]
        spans.append(jnp.concatenate((before, middle, after), axis=0).reshape(EDGE + 2, EDGE, CH))
    low, centre, high = spans
    down = pltpu.roll(jnp.where(sub == EDGE - 1, low, centre), 1, 1)
    up = pltpu.roll(jnp.where(sub == 0, high, centre), EDGE - 1, 1)
    for r, source in ((-1, down), (0, centre), (1, up)):
        for q in (-1, 0, 1):
            rows = source[q + 1 : q + 1 + EDGE].reshape(PLANE, CH).astype(BF16)
            lane = (3 * (q + 1) + r + 1) * CH
            x9_ref[pl.ds(row, PLANE), lane : lane + CH] = rows


def fill_columns(map_ref, slot, table_ref, x9_ref, unroll=True):
    fill = functools.partial(fill_plane, map_ref, slot, table_ref, x9_ref)
    fill(-1, VOX - PLANE, 0)
    if unroll:
        for a in range(EDGE):
            fill(0, a * PLANE, (a + 1) * PLANE)
    else:

        def inner(a, carry):
            base = pl.multiple_of(a * PLANE, PLANE)
            fill(0, base, pl.multiple_of(base + PLANE, PLANE))
            return carry

        lax.fori_loop(0, EDGE, inner, 0)
    fill(1, 0, (EDGE + 1) * PLANE)


def fill_whole(place_ref, table_ref, refs):
    start = 0
    for ref in refs:
        table_ref[start : start + ref.shape[0]] = ref[...]
        start += ref.shape[0]


def fill_faces(place_ref, table_ref, refs):
    own_ref, x1_ref, x2_ref, y1_ref, y2_ref = refs
    table_ref[0:SLOTS] = own_ref[...]
    for k in range(HX):
        low, high = lower_upper(place_ref[0], x1_ref[k], x2_ref[k])
        table_ref[SLOTS + k, VOX - PLANE : VOX, :] = low
        table_ref[SLOTS + HX + k, 0:PLANE, :] = high
    empty = jnp.zeros((EDGE, CH), F32)
    first = SLOTS + 2 * HX
    for k in range(HY):
        rows = slice(k * PLANE, (k + 1) * PLANE)
        low, high = lower_upper(
            place_ref[1], y1_ref[rows, :].astype(F32), y2_ref[rows, :].astype(F32)
        )
        for a in range(EDGE):
            part = slice(a * EDGE, (a + 1) * EDGE)
            base = a * PLANE
            table_ref[first + k, base + 48 : base + 64, :] = jnp.concatenate(
                (empty, low[part]), axis=0
            ).astype(BF16)
            table_ref[first + HY + k, base : base + 16, :] = jnp.concatenate(
                (high[part], empty), axis=0
            ).astype(BF16)


def count_misfits(place_ref, rows, y1_ref, y2_ref):
    lane = lax.broadcasted_iota(jnp.int32, rows.shape, 1)
    within = lane - jnp.where(lane >= 9, 9, 0) - jnp.where(lane >= 18, 9, 0)
    not_down, not_up = lane >= 9, lane < 18
    bad = (rows >= SLOTS) & (rows < SLOTS + HX) & not_down
    bad = bad | ((rows >= SLOTS + HX) & (rows < SLOTS + 2 * HX) & not_up)
    marks = slice(HY * PLANE, FACE_ROWS)
    low, high = lower_upper(
        place_ref[1], y1_ref[marks, :].astype(F32), y2_ref[marks, :].astype(F32)
    )
    for start, origin, wrong in (
        (SLOTS + 2 * HX, low, within >= 3),
        (SLOTS + 2 * HX + HY, high, within < 6),
    ):
        for k in range(HY):
            code = jnp.broadcast_to(origin[k : k + 1, 0 : rows.shape[1]], rows.shape)
            fault = wrong | ((code == 1.0) & not_down) | ((code == 2.0) & not_up)
            bad = bad | ((rows == start + k) & fault)
    return jnp.sum(jnp.where(bad, 1.0, 0.0))


def conv_kernel(
    place_ref, map_ref, rows_ref, own_ref, xl_ref, xu_ref, yl_ref, yu_ref, w_ref, mask_ref,
    out_ref, x9_out, stat_ref, table_ref, x9_ref, sems,
):
    fill_faces(place_ref, table_ref, (own_ref, xl_ref, xu_ref, yl_ref, yu_ref))
    table_ref[16] = jnp.zeros((VOX, CH), BF16)
    sums = [jnp.zeros((1, CH), F32)] * 3
    copies = []

    def columns(slot):
        fill_columns(map_ref, slot, table_ref, x9_ref.at[slot])
        copies.append(pltpu.make_async_copy(x9_ref.at[slot], x9_out.at[slot], sems.at[slot]))
        copies[-1].start()

    columns(0)
    for slot in range(SLOTS):
        if slot + 1 < SLOTS:
            columns(slot + 1)
        total = None
        for p in range(3):
            term = jnp.dot(
                x9_ref[slot, p * PLANE : p * PLANE + VOX, :], w_ref[p], preferred_element_type=F32
            )
            total = term if total is None else total + term
        mask = mask_ref[slot].astype(F32)
        masked = total * mask
        out_ref[slot] = total
        terms = (masked, masked * total, mask)
        sums = [s + jnp.sum(term, axis=0, keepdims=True) for s, term in zip(sums, terms)]
    misfits = count_misfits(place_ref, rows_ref[...], yl_ref, yu_ref)
    sums.append(jnp.broadcast_to(misfits, (1, CH)))
    stat_ref[...] = jnp.concatenate(sums + [jnp.zeros((4, CH), F32)], axis=0)
    for copy in copies:
        copy.wait()


def conv(place, row_map, own, xl, xu, yl, yu, weight, mask):
    columns = (SLOTS, 10 * PLANE, 9 * CH)
    return pl.pallas_call(
        conv_kernel,
        out_shape=(shape((SLOTS, VOX, CH), F32), shape(columns, BF16), shape((8, CH), F32)),
        in_specs=[SM, SM] + [VM] * 8,
        out_specs=(VM, pl.BlockSpec(memory_space=pl.ANY), VM),
        scratch_shapes=[
            pltpu.VMEM((17, VOX, CH), BF16),
            pltpu.VMEM(columns, BF16),
            pltpu.SemaphoreType.DMA((SLOTS,)),
        ],
        compiler_params=params(28),
        cost_estimate=cost(6000000000, 12 << 20),
        name="forward_conv",
    )(place, row_map, row_map, own, xl, xu, yl, yu, weight, mask)


def step_kernel(
    place_ref, map_ref, rows_ref, own_ref, xl_ref, xu_ref, yl_ref, yu_ref, w_ref, mask_ref, *rest,
    forward, faces
):
    slot = pl.program_id(0)
    if forward:
        out_ref, x9_out, stat_ref, table_ref = rest
        x9_ref = x9_out.at[0]
    else:
        out_ref, table_ref, x9_ref = rest

    @pl.when(slot == 0)
    def _():
        fill = fill_faces if faces else fill_whole
        fill(place_ref, table_ref, (own_ref, xl_ref, xu_ref, yl_ref, yu_ref))
        table_ref[16] = jnp.zeros((VOX, CH), BF16)
        if forward:
            stat_ref[...] = jnp.zeros_like(stat_ref)

    fill_columns(map_ref, slot, table_ref, x9_ref, faces)
    total = None
    for p in range(3):
        term = jnp.dot(
            x9_ref[p * PLANE : p * PLANE + VOX, :], w_ref[p], preferred_element_type=F32
        )
        total = term if total is None else total + term
    mask = mask_ref[0].astype(F32)
    masked = total * mask
    if forward:
        out_ref[0] = total
        stat_ref[0:1] += jnp.sum(masked, axis=0, keepdims=True)
        stat_ref[1:2] += jnp.sum(masked * total, axis=0, keepdims=True)
        stat_ref[2:3] += jnp.sum(mask, axis=0, keepdims=True)
    else:
        out_ref[0] = masked.astype(BF16)


def whole(*dims):
    return pl.BlockSpec(dims, lambda s: (0,) * len(dims))


def conv_steps(place, row_map, own, xl, xu, yl, yu, weight, mask, forward, faces):
    brick = pl.BlockSpec((1, VOX, CH), lambda s: (s, 0, 0))
    scratch = [pltpu.VMEM((17, VOX, CH), BF16)]
    if forward:
        out_shape = (
            shape((SLOTS, VOX, CH), F32),
            shape((SLOTS, 10 * PLANE, 9 * CH), BF16),
            shape((8, CH), F32),
        )
        out_specs = (brick, pl.BlockSpec((1, 10 * PLANE, 9 * CH), lambda s: (s, 0, 0)), whole(8, CH))
    else:
        out_shape = shape((SLOTS, VOX, CH), BF16)
        out_specs = brick
        scratch.append(pltpu.VMEM((10 * PLANE, 9 * CH), BF16))
    return pl.pallas_call(
        functools.partial(step_kernel, forward=forward, faces=faces),
        grid=(SLOTS,),
        out_shape=out_shape,
        in_specs=[
            SM,
            SM,
            whole(*row_map.shape),
            whole(*own.shape),
            whole(*xl.shape),
            whole(*xu.shape),
            whole(*yl.shape),
            whole(*yu.shape),
            whole(3, 9 * CH, CH),
            brick,
        ],
        out_specs=out_specs,
        scratch_shapes=scratch,
        compiler_params=params(24),
        cost_estimate=cost(6000000000, 12 << 20),
        name="forward_steps" if forward else "transposed_conv",
    )(place, row_map, row_map, own, xl, xu, yl, yu, weight, mask)


def norm_terms(stats):
    count = stats[2:3]
    mean = stats[0:1] / count
    variance = stats[1:2] / count - mean * mean
    return count, mean, lax.rsqrt(variance + EPSILON)


def activate(slot, stats, cot_ref, conv_ref, mask_ref, gain_ref, shift_ref, act_ref, ga_ref, g_ref):
    count, mean, inverse = stats
    mask = mask_ref[slot].astype(F32)
    normed = (conv_ref[slot] - mean) * inverse
    pre = gain_ref[...] * normed + shift_ref[...]
    sig = jax.nn.sigmoid(pre)
    act_ref[slot] = (pre * sig * mask).astype(BF16)
    ga = cot_ref[slot].astype(F32) * mask * sig * (1.0 + pre * (1.0 - sig))
    ga_ref[slot] = ga
    nm = normed * mask
    for k in range(VOX // CH):
        rows = slice(k * CH, (k + 1) * CH)
        g_ref[slot, 0:CH, rows] = jnp.transpose(ga[rows]).astype(BF16)
        g_ref[slot, CH : 2 * CH, rows] = jnp.transpose(nm[rows]).astype(BF16)
        g_ref[slot, 2 * CH : 2 * CH + 16, rows] = jnp.transpose(mask[rows])[0:16].astype(BF16)
    sums = (jnp.sum(ga, axis=0, keepdims=True), jnp.sum(ga * normed, axis=0, keepdims=True))
    return jnp.concatenate(sums, axis=0)


def split(value, pieces):
    parts = []
    for _ in range(pieces):
        part = value.astype(BF16).astype(F32)
        parts.append(part)
        value = value - part
    return parts


def pack(ones, sums):
    parts = split(ones, 2) + split(sums[0:1], 3) + split(sums[1:2], 3)
    used = sum(part.shape[0] for part in parts)
    rows = -(-used // 16) * 16
    if used < rows:
        parts.append(jnp.zeros((rows - used, CH), F32))
    return jnp.concatenate(parts, axis=0).astype(BF16)


def unpack(rows, taps):
    ones = rows[0:taps] + rows[taps : 2 * taps]
    at = 2 * taps
    first = rows[at : at + 1] + rows[at + 1 : at + 2] + rows[at + 2 : at + 3]
    second = rows[at + 3 : at + 4] + rows[at + 4 : at + 5] + rows[at + 5 : at + 6]
    return ones, jnp.concatenate((first, second), axis=0)


def wgrad_kernel(
    place_ref, stat_ref, conv_ref, cot_ref, mask_ref, gain_ref, shift_ref, x9_hbm,
    act_ref, ga_ref, norm_ref, keep_ref, send_ref, g_ref, x9_ref, hold_ref, sems, *, unroll
):
    copies = [
        pltpu.make_async_copy(x9_hbm.at[s], x9_ref.at[s], sems.at[s]) for s in range(SLOTS)
    ]
    for copy in copies:
        copy.start()
    stats = norm_terms(jnp.sum(stat_ref[...], axis=0))
    count, mean, inverse = stats
    norm_ref[...] = jnp.concatenate((mean, inverse, count, jnp.zeros((5, CH), F32)), axis=0)

    def add_sums(s, sums):
        return sums + activate(
            s, stats, cot_ref, conv_ref, mask_ref, gain_ref, shift_ref, act_ref, ga_ref, g_ref
        )

    sums = lax.fori_loop(0, SLOTS, add_sums, jnp.zeros((2, CH), F32), unroll=unroll)
    for copy in copies:
        copy.wait()
    ones = [None] * 27
    for p in range(3):
        for q in range(0, 9, 2):
            width = min(2, 9 - q)
            lanes = slice(q * CH, (q + width) * CH)

            def add_term(s, total):
                rows = slice(p * PLANE, p * PLANE + VOX)
                return total + jnp.dot(
                    g_ref[s], x9_ref[s, rows, lanes], preferred_element_type=F32
                )

            if unroll:
                total = None
                for s in range(SLOTS):
                    total = add_term(s, 0.0 if total is None else total)
            else:
                empty = jnp.zeros((2 * CH + 16, width * CH), F32)
                total = lax.fori_loop(0, SLOTS, add_term, empty)
            for r in range(width):
                t = 9 * p + q + r
                tap = total[:, r * CH : (r + 1) * CH]
                ones[t] = tap[2 * CH : 2 * CH + 1]
                for half in (0, 1):
                    i = t - 13 * half
                    if 0 <= i < 14:
                        for k in range(16):
                            pair = jnp.concatenate(
                                (tap[8 * k : 8 * k + 8], tap[CH + 8 * k : CH + 8 * k + 8]), axis=0
                            )
                            row = k * MAIN + i * 16
                            hold_ref[half, row : row + 16, :] = pair
    for half in (0, 1):
        rows = jnp.concatenate(ones[13 * half : 13 * half + 14], axis=0)
        hold_ref[half, 16 * MAIN : 16 * MAIN + EXTRA, :] = pack(rows, sums).astype(F32)
    core = place_ref[1]
    keep_ref[...] = hold_ref[core]
    send_ref[...] = hold_ref[1 - core].astype(BF16)


def wgrad(place, stats, conv_out, cotangent, mask, gain, shift, x9, unroll):
    rows = 16 * MAIN + EXTRA
    return pl.pallas_call(
        functools.partial(wgrad_kernel, unroll=unroll),
        out_shape=(
            shape((SLOTS, VOX, CH), BF16),
            shape((SLOTS, VOX, CH), F32),
            shape((8, CH), F32),
            shape((rows, CH), F32),
            shape((rows, CH), BF16),
        ),
        in_specs=[SM] + [VM] * 6 + [pl.BlockSpec(memory_space=pl.ANY)],
        out_specs=(VM,) * 5,
        scratch_shapes=[
            pltpu.VMEM((SLOTS, 2 * CH + 16, VOX), BF16),
            pltpu.VMEM((SLOTS, 10 * PLANE, 9 * CH), BF16),
            pltpu.VMEM((2, rows, CH), F32),
            pltpu.SemaphoreType.DMA((SLOTS,)),
        ],
        compiler_params=params(28),
        cost_estimate=cost(6000000000, 12 << 20),
        name="weight_terms",
    )(place, stats, conv_out, cotangent, mask, gain, shift, x9)


def join_kernel(keep_ref, got_ref, out_ref):
    for k in range(16):
        rows = slice(k * MAIN, (k + 1) * MAIN)
        out_ref[k, 0:MAIN, :] = (keep_ref[rows, :] + got_ref[rows, :].astype(F32)).astype(BF16)
    rows = slice(16 * MAIN, 16 * MAIN + EXTRA)
    ones, sums = unpack(keep_ref[rows, :], 14)
    more_ones, more_sums = unpack(got_ref[rows, :].astype(F32), 14)
    extra = pack(ones + more_ones, sums + more_sums)
    for k in range(16):
        out_ref[k, MAIN : MAIN + EXTRA, :] = extra


def join(keep, got):
    return pl.pallas_call(
        join_kernel,
        out_shape=shape((16, MAIN + EXTRA, CH), BF16),
        in_specs=[VM, VM],
        out_specs=VM,
        compiler_params=params(),
        cost_estimate=cost(1 << 20, 3 << 20),
        name="join",
    )(keep, got)


def middle_kernel(parts_ref, out_ref):
    extra = None
    for k in range(16):
        ones, sums = unpack(parts_ref[k, MAIN : MAIN + EXTRA, :].astype(F32), 14)
        extra = (ones, sums) if extra is None else (extra[0] + ones, extra[1] + sums)
    for z in range(8):
        if z < 7:
            total = None
            for k in range(16):
                term = parts_ref[k, 32 * z : 32 * (z + 1), :].astype(F32)
                total = term if total is None else total + term
            ones = extra[0][2 * z : 2 * z + 2]
        else:
            total, ones = jnp.zeros((32, CH), F32), jnp.zeros((2, CH), F32)
        out_ref[z] = jnp.concatenate((total, ones, extra[1], jnp.zeros((4, CH), F32)), axis=0)


def middle(parts):
    return pl.pallas_call(
        middle_kernel,
        out_shape=shape((8, 40, CH), F32),
        in_specs=[VM],
        out_specs=VM,
        compiler_params=params(),
        cost_estimate=cost(1 << 20, 2 << 20),
        name="middle",
    )(parts)


def column(row):
    return jnp.transpose(jnp.broadcast_to(row, (CH, CH)))


def combine_kernel(place_ref, parts_ref, norm_ref, gain_ref, out_ref, gg_ref, sg_ref, coef_ref):
    total = jnp.sum(parts_ref[...], axis=0)
    main, ones, sums = total[0:32], total[32:34], total[34:36]
    inverse, count = norm_ref[1:2], norm_ref[2:3]
    scale = lax.rsqrt(count)
    sg_ref[...] = sums[0:1] * scale
    gg_ref[...] = sums[1:2] * scale
    coef_ref[0] = column(gain_ref[...] * inverse * scale)
    coef_ref[1] = column(sums[0:1] / count)
    coef_ref[2] = column(sums[1:2] / count)
    mine = pl.ds(pl.multiple_of(place_ref[2] * 8, 8), 8)
    factor, first, second = coef_ref[0, mine, :], coef_ref[1, mine, :], coef_ref[2, mine, :]
    values = []
    for i in range(2):
        base, cross = main[16 * i : 16 * i + 8], main[16 * i + 8 : 16 * i + 16]
        values.append(factor * (base - first * ones[i : i + 1] - second * cross))
    value = jnp.concatenate(values, axis=0).astype(BF16)
    for z in range(8):
        out_ref[z] = value


def combine(place, parts, norm, gain):
    return pl.pallas_call(
        combine_kernel,
        out_shape=(shape((8, 16, CH), BF16), shape((1, CH), F32), shape((1, CH), F32)),
        in_specs=[SM] + [VM] * 3,
        out_specs=(VM,) * 3,
        scratch_shapes=[pltpu.VMEM((3, CH, CH), F32)],
        compiler_params=params(),
        cost_estimate=cost(1 << 20, 1 << 20),
        name="combine",
    )(place, parts, norm, gain)


def grad_kernel(
    place_ref, sends_ref, parts_ref, norm_ref, gain_ref, conv_ref, ga_ref, mask_ref, out_ref, low_ref, high_ref, *, faces
):
    totals = jnp.sum(parts_ref[...], axis=0)[34:36]
    mean, inverse, count = norm_ref[0:1], norm_ref[1:2], norm_ref[2:3]
    factor = gain_ref[...] * inverse
    for s in range(SLOTS):
        normed = (conv_ref[s] - mean) * inverse
        inner = ga_ref[s] - (totals[0:1] + normed * totals[1:2]) / count
        out_ref[s] = (factor * inner * mask_ref[s].astype(F32)).astype(BF16)
    pick_x(place_ref, sends_ref, out_ref, low_ref, high_ref, faces)


def grad(place, sends_x, parts, norm, gain, conv_out, ga, mask, faces):
    return pl.pallas_call(
        functools.partial(grad_kernel, faces=faces),
        out_shape=(shape((SLOTS, VOX, CH), BF16),) + x_shapes(faces),
        in_specs=[SM, SM] + [VM] * 6,
        out_specs=(VM,) * 3,
        compiler_params=params(),
        cost_estimate=cost(4 << 20, 4 << 20),
        name="grad_conv",
    )(place, sends_x, parts, norm, gain, conv_out, ga, mask)


def finish_kernel(place_ref, mine_ref, other_ref, out_ref):
    for half in (0, 1):
        here = place_ref[1] == half
        for z in range(7):
            pairs = []
            for k in range(16):
                rows = slice(16 * z, 16 * (z + 1))
                pairs.append(jnp.where(here, mine_ref[k, rows, :], other_ref[k, rows, :]).astype(F32))
            for i in range(2):
                tap = 13 * half + 2 * z + i
                if half == 1 and tap == 13:
                    continue
                rows = jnp.concatenate([pair[8 * i : 8 * i + 8] for pair in pairs], axis=0)
                out_ref[tap] = jnp.transpose(rows)


def finish(place, mine, other):
    return pl.pallas_call(
        finish_kernel,
        out_shape=shape((27, CH, CH), F32),
        in_specs=[SM, VM, VM],
        out_specs=VM,
        compiler_params=params(),
        cost_estimate=cost(1 << 20, 3 << 20),
        name="finish",
    )(place, mine, other)


def spread(value, axes):
    size = axis_size(axes)
    return lax.all_to_all(jnp.broadcast_to(value[None], (size,) + value.shape), axes, 0, 0)


def all_sum_parts(value):
    return spread(jnp.sum(spread(value, ("z", "c")), axis=0), CROSS)


def swap(value):
    return lax.ppermute(value, "c", [(0, 1), (1, 0)])


def turn_kernel(w_ref, out_ref):
    for t in range(27):
        rows = slice((t % 9) * CH, (t % 9 + 1) * CH)
        out_ref[t // 9, rows, :] = jnp.transpose(w_ref[26 - t].astype(F32)).astype(BF16)


def turn(weight):
    return pl.pallas_call(
        turn_kernel,
        out_shape=shape((3, 9 * CH, CH), BF16),
        in_specs=[VM],
        out_specs=VM,
        compiler_params=params(),
        cost_estimate=cost(1 << 20, 2 << 20),
        name="turn",
    )(weight)


def shards(
    features,
    occupancy,
    counts,
    kernel_map,
    x_send,
    y_send,
    weight,
    norm_gain,
    norm_shift,
    cotangent,
):
    row_map, sends_x, sends_y = kernel_map[0, 0], x_send[0, 0], y_send[0, 0]
    gain, shift = norm_gain.reshape(1, CH), norm_shift.reshape(1, CH)
    place = jnp.stack((lax.axis_index("y") % 2, lax.axis_index("c"), lax.axis_index(CROSS)))
    ahead = weight.reshape(3, 9 * CH, CH)

    def first(faces):
        own, mask, low, high = prepare(place, counts, sends_x, features[0, 0], occupancy[0, 0], faces)
        later, low, high = lax.optimization_barrier((weight, low, high))
        xl, xu = neighbours(low, high, ("xh", "y"), faces)
        xl, xu, turned = lax.optimization_barrier((xl, xu, turn(later)))
        low, high = pick_y(place, sends_y, own, xl, xu, faces)
        yl, yu = neighbours(low, high, ("xl", "z", "c"), faces)
        table = (place, row_map, own, xl, xu, yl, yu, ahead, mask)
        conv_out, x9, stats = conv(*table) if faces else conv_steps(*table, True, False)
        return conv_out, x9, mask, turned, all_sum_parts(stats)

    def second(conv_out, x9, mask, turned, stats, faces):
        activations, ga, norm, keep, send = wgrad(
            place, stats, conv_out, cotangent[0, 0], mask, gain, shift, x9, faces
        )
        parts = lax.all_to_all(join(keep, swap(send)), CROSS, 0, 0)
        parts = lax.all_to_all(middle(parts), "z", 0, 0)
        grads, low, high = grad(place, sends_x, parts, norm, gain, conv_out, ga, mask, faces)
        parts, low, high = lax.optimization_barrier((parts, low, high))
        xl, xu = neighbours(low, high, ("xh", "y"), faces)
        value, gain_grad, shift_grad = combine(place, parts, norm, gain)
        mine = lax.all_to_all(value, "z", 0, 0).reshape(8 * 16, CH)[: 7 * 16]
        low, high = pick_y(place, sends_y, grads, xl, xu, faces)
        mine, low, high = lax.optimization_barrier((mine, low, high))
        yl, yu = neighbours(low, high, ("xl", "z", "c"), faces)
        mine = spread(mine, CROSS)
        features_grad = conv_steps(place, row_map, grads, xl, xu, yl, yu, turned, mask, False, faces)
        mine, features_grad = lax.optimization_barrier((mine, features_grad))
        weight_grad = finish(place, mine, swap(mine))
        return activations, features_grad, weight_grad, gain_grad, shift_grad

    state = first(True)
    misfits = jnp.sum(state[4][:, 3, 0])
    activations, features_grad, weight_grad, gain_grad, shift_grad = lax.cond(
        misfits > 0,
        lambda *_: second(*first(False), False),
        lambda *given: second(*given, True),
        *state,
    )
    return (
        activations[None, None],
        features_grad[None, None],
        weight_grad,
        gain_grad.reshape(CH),
        shift_grad.reshape(CH),
    )


def solution(mesh):
    fine = jax.sharding.Mesh(mesh.devices.reshape(2, 4, 2, 8, 2), ("xh", "y", "xl", "z", "c"))
    gx, gy = ("xh", "y"), ("xl", "z", "c")
    tiles = P(gx, gy, None, None, None)
    lists = P(gx, gy, None, None)
    return jax.shard_map(
        shards,
        mesh=fine,
        in_specs=(tiles, lists, P(gx, gy), lists, lists, lists, P(), P(), P(), tiles),
        out_specs=(tiles, tiles, P(), P(), P()),
        check_vma=False,
    )
```

```python
import functools

import jax
import jax.numpy as jnp
from jax import lax
from jax.experimental import pallas as pl
from jax.experimental.pallas import tpu as pltpu
from jax.sharding import PartitionSpec as P

EDGE = 8
PLANE = 64
VOX = 512
CH = 128
SLOTS = 4
HX = 2
HY = 4
EPSILON = 1e-05
F32 = jnp.float32
BF16 = jnp.bfloat16

VM = pl.BlockSpec(memory_space=pltpu.VMEM)
SM = pl.BlockSpec(memory_space=pltpu.SMEM)
MAIN = 224
EXTRA = 48
FACE_ROWS = HY * PLANE + 16
MIB = 1024 * 1024
CROSS = ("xh", "y", "xl")


def params(limit=20):
    return pltpu.CompilerParams(vmem_limit_bytes=limit * MIB)


def cost(flops, moved):
    return pl.CostEstimate(flops=flops, bytes_accessed=moved, transcendentals=0)


def shape(dims, kind):
    return jax.ShapeDtypeStruct(dims, kind)


def side_of(turn, odd):
    return 1 - odd if turn else odd


def lower_upper(odd, first, second):
    even = odd == 0
    return jnp.where(even, first, second), jnp.where(even, second, first)


def pick_x(place_ref, sends_ref, own_ref, first_ref, second_ref, faces):
    for turn, out_ref in ((0, first_ref), (1, second_ref)):
        side, rows = turn, slice(0, VOX)
        if faces:
            side = side_of(turn, place_ref[0])
            rows = pl.ds(pl.multiple_of(side * (VOX - PLANE), PLANE), PLANE)
        for k in range(HX):
            row = sends_ref[side, k]
            brick = own_ref[jnp.minimum(row, SLOTS - 1), rows, :]
            out_ref[k] = jnp.where(row < SLOTS, brick, jnp.zeros_like(brick))


def x_shapes(faces):
    send = shape((HX, PLANE if faces else VOX, CH), BF16)
    return (send, send)


def prepare_kernel(
    place_ref, counts_ref, sends_ref, feat_ref, occ_ref, own_ref, mask_ref, low_ref, high_ref, *, faces
):
    for s in range(SLOTS):
        live = (s < counts_ref[0, 0]).astype(F32)
        for k in range(VOX // CH):
            row = occ_ref[s : s + 1, k * CH : (k + 1) * CH].astype(F32) * live
            column = jnp.transpose(jnp.broadcast_to(row, (CH, CH)))
            rows = pl.ds(k * CH, CH)
            mask_ref[s, rows, :] = column.astype(BF16)
            own_ref[s, rows, :] = (feat_ref[s, rows, :].astype(F32) * column).astype(BF16)
    pick_x(place_ref, sends_ref, own_ref, low_ref, high_ref, faces)


def prepare(place, counts, sends_x, features, occupancy, faces):
    return pl.pallas_call(
        functools.partial(prepare_kernel, faces=faces),
        out_shape=(shape((SLOTS, VOX, CH), BF16),) * 2 + x_shapes(faces),
        in_specs=[SM, SM, SM, VM, VM],
        out_specs=(VM, VM, VM, VM),
        compiler_params=params(),
        cost_estimate=cost(1 << 20, 2 << 20),
        name="prepare",
    )(place, counts, sends_x, features, occupancy)


def pick_y_kernel(place_ref, sends_ref, own_ref, xl_ref, xu_ref, low_ref, high_ref):
    for side, out_ref in ((0, low_ref), (1, high_ref)):
        for k in range(HY):
            row = sends_ref[side, k]

            @pl.when(row < SLOTS)
            def _():
                out_ref[k] = own_ref[jnp.minimum(row, SLOTS - 1)]

            @pl.when((row >= SLOTS) & (row < SLOTS + HX))
            def _():
                out_ref[k] = xl_ref[jnp.clip(row - SLOTS, 0, HX - 1)]

            @pl.when((row >= SLOTS + HX) & (row < SLOTS + 2 * HX))
            def _():
                out_ref[k] = xu_ref[jnp.clip(row - SLOTS - HX, 0, HX - 1)]

            @pl.when(row >= SLOTS + 2 * HX)
            def _():
                out_ref[k] = jnp.zeros((VOX, CH), BF16)


def pick_y_faces_kernel(place_ref, sends_ref, own_ref, x1_ref, x2_ref, first_ref, second_ref):
    lines = lax.broadcasted_iota(jnp.int32, (16, CH), 0)
    odd = place_ref[0]
    for turn, out_ref in ((0, first_ref), (1, second_ref)):
        side = side_of(turn, place_ref[1])
        skip = side * (PLANE - 16)

        def piece(base):
            return pl.ds(pl.multiple_of(base + skip, 16), 16)

        def edge(block):
            block = block.astype(F32)
            return jnp.where(side == 0, block[:EDGE], block[EDGE:])

        origin = jnp.zeros((16, CH), F32)
        for k in range(HY):
            row = sends_ref[side, k]
            rows = pl.ds(k * PLANE, PLANE)
            lower = (row >= SLOTS) & (row < SLOTS + HX)
            upper = (row >= SLOTS + HX) & (row < SLOTS + 2 * HX)
            code = jnp.where(lower, 1.0, jnp.where(upper, 2.0, 0.0))
            origin = jnp.where(lines == k, code, origin)

            @pl.when(row < SLOTS)
            def _():
                brick = jnp.minimum(row, SLOTS - 1)
                parts = [edge(own_ref[brick, piece(a * PLANE), :]) for a in range(EDGE)]
                out_ref[rows, :] = jnp.concatenate(parts, axis=0).astype(BF16)

            @pl.when(lower | upper)
            def _():
                at = jnp.where(lower, row - SLOTS, row - SLOTS - HX)
                at = jnp.clip(at, 0, HX - 1)
                down, up = lower_upper(odd, x1_ref[at, piece(0), :], x2_ref[at, piece(0), :])
                part = edge(jnp.where(lower, down, up))
                empty = jnp.zeros((PLANE - 2 * EDGE, CH), F32)
                blank = jnp.zeros_like(part)
                front, back = jnp.where(lower, blank, part), jnp.where(lower, part, blank)
                out_ref[rows, :] = jnp.concatenate((front, empty, back), axis=0).astype(BF16)

            @pl.when(row >= SLOTS + 2 * HX)
            def _():
                out_ref[rows, :] = jnp.zeros((PLANE, CH), BF16)

        out_ref[HY * PLANE : FACE_ROWS, :] = origin.astype(BF16)


def pick_y(place, sends_y, own, xl, xu, faces):
    send = shape((FACE_ROWS, CH) if faces else (HY, VOX, CH), BF16)
    return pl.pallas_call(
        pick_y_faces_kernel if faces else pick_y_kernel,
        out_shape=(send, send),
        in_specs=[SM, SM, VM, VM, VM],
        out_specs=(VM, VM),
        compiler_params=params(),
        cost_estimate=cost(1 << 20, 2 << 20),
        name="pick_y",
    )(place, sends_y, own, xl, xu)


def axis_size(axes):
    size = 1
    for axis in axes:
        size *= lax.axis_size(axis)
    return size


def neighbours(first, second, axes, faces):
    size = axis_size(axes)
    if faces:
        pairs = [[(i, i + 1) for i in range(1 - turn, size - 1, 2)] for turn in (0, 1)]
        one, two = [pair + [(j, i) for i, j in pair] for pair in pairs]
        return lax.ppermute(first, axes, one), lax.ppermute(second, axes, two)
    up = [(i, i + 1) for i in range(size - 1)]
    down = [(j, i) for i, j in up]
    return lax.ppermute(second, axes, up), lax.ppermute(first, axes, down)


def fill_plane(map_ref, slot, table_ref, x9_ref, move, base, row):
    sub = lax.broadcasted_iota(jnp.int32, (EDGE + 2, EDGE, CH), 1)
    spans = []
    for r in (-1, 0, 1):
        tap = 9 * (move + 1) + r + 1
        first, whole_plane, last = pl.ds(base + 48, 16), pl.ds(base, PLANE), pl.ds(base, 16)
        before = table_ref[map_ref[slot, tap], first, :].astype(F32)[8:]
        middle = table_ref[map_ref[slot, tap + 3], whole_plane, :].astype(F32)
        after = table_ref[map_ref[slot, tap + 6], last, :].astype(F32)[:8]
        spans.append(jnp.concatenate((before, middle, after), axis=0).reshape(EDGE + 2, EDGE, CH))
    low, centre, high = spans
    down = pltpu.roll(jnp.where(sub == EDGE - 1, low, centre), 1, 1)
    up = pltpu.roll(jnp.where(sub == 0, high, centre), EDGE - 1, 1)
    for r, source in ((-1, down), (0, centre), (1, up)):
        for q in (-1, 0, 1):
            rows = source[q + 1 : q + 1 + EDGE].reshape(PLANE, CH).astype(BF16)
            lane = (3 * (q + 1) + r + 1) * CH
            x9_ref[pl.ds(row, PLANE), lane : lane + CH] = rows


def fill_columns(map_ref, slot, table_ref, x9_ref, unroll=True):
    fill = functools.partial(fill_plane, map_ref, slot, table_ref, x9_ref)
    fill(-1, VOX - PLANE, 0)
    if unroll:
        for a in range(EDGE):
            fill(0, a * PLANE, (a + 1) * PLANE)
    else:

        def inner(a, carry):
            base = pl.multiple_of(a * PLANE, PLANE)
            fill(0, base, pl.multiple_of(base + PLANE, PLANE))
            return carry

        lax.fori_loop(0, EDGE, inner, 0)
    fill(1, 0, (EDGE + 1) * PLANE)


def fill_whole(place_ref, table_ref, refs):
    start = 0
    for ref in refs:
        table_ref[start : start + ref.shape[0]] = ref[...]
        start += ref.shape[0]


def fill_faces(place_ref, table_ref, refs):
    own_ref, x1_ref, x2_ref, y1_ref, y2_ref = refs
    table_ref[0:SLOTS] = own_ref[...]
    for k in range(HX):
        low, high = lower_upper(place_ref[0], x1_ref[k], x2_ref[k])
        table_ref[SLOTS + k, VOX - PLANE : VOX, :] = low
        table_ref[SLOTS + HX + k, 0:PLANE, :] = high
    empty = jnp.zeros((EDGE, CH), F32)
    first = SLOTS + 2 * HX
    for k in range(HY):
        rows = slice(k * PLANE, (k + 1) * PLANE)
        low, high = lower_upper(
            place_ref[1], y1_ref[rows, :].astype(F32), y2_ref[rows, :].astype(F32)
        )
        for a in range(EDGE):
            part = slice(a * EDGE, (a + 1) * EDGE)
            base = a * PLANE
            table_ref[first + k, base + 48 : base + 64, :] = jnp.concatenate(
                (empty, low[part]), axis=0
            ).astype(BF16)
            table_ref[first + HY + k, base : base + 16, :] = jnp.concatenate(
                (high[part], empty), axis=0
            ).astype(BF16)


def count_misfits(place_ref, rows, y1_ref, y2_ref):
    lane = lax.broadcasted_iota(jnp.int32, rows.shape, 1)
    within = lane - jnp.where(lane >= 9, 9, 0) - jnp.where(lane >= 18, 9, 0)
    not_down, not_up = lane >= 9, lane < 18
    bad = (rows >= SLOTS) & (rows < SLOTS + HX) & not_down
    bad = bad | ((rows >= SLOTS + HX) & (rows < SLOTS + 2 * HX) & not_up)
    marks = slice(HY * PLANE, FACE_ROWS)
    low, high = lower_upper(
        place_ref[1], y1_ref[marks, :].astype(F32), y2_ref[marks, :].astype(F32)
    )
    for start, origin, wrong in (
        (SLOTS + 2 * HX, low, within >= 3),
        (SLOTS + 2 * HX + HY, high, within < 6),
    ):
        for k in range(HY):
            code = jnp.broadcast_to(origin[k : k + 1, 0 : rows.shape[1]], rows.shape)
            fault = wrong | ((code == 1.0) & not_down) | ((code == 2.0) & not_up)
            bad = bad | ((rows == start + k) & fault)
    return jnp.sum(jnp.where(bad, 1.0, 0.0))


def conv_kernel(
    place_ref, map_ref, rows_ref, own_ref, xl_ref, xu_ref, yl_ref, yu_ref, w_ref, mask_ref,
    out_ref, x9_out, stat_ref, table_ref, x9_ref, sems,
):
    fill_faces(place_ref, table_ref, (own_ref, xl_ref, xu_ref, yl_ref, yu_ref))
    table_ref[16] = jnp.zeros((VOX, CH), BF16)
    sums = [jnp.zeros((1, CH), F32)] * 3
    copies = []

    def columns(slot):
        fill_columns(map_ref, slot, table_ref, x9_ref.at[slot])
        copies.append(pltpu.make_async_copy(x9_ref.at[slot], x9_out.at[slot], sems.at[slot]))
        copies[-1].start()

    columns(0)
    for slot in range(SLOTS):
        if slot + 1 < SLOTS:
            columns(slot + 1)
        total = None
        for p in range(3):
            term = jnp.dot(
                x9_ref[slot, p * PLANE : p * PLANE + VOX, :], w_ref[p], preferred_element_type=F32
            )
            total = term if total is None else total + term
        mask = mask_ref[slot].astype(F32)
        masked = total * mask
        out_ref[slot] = total
        terms = (masked, masked * total, mask)
        sums = [s + jnp.sum(term, axis=0, keepdims=True) for s, term in zip(sums, terms)]
    misfits = count_misfits(place_ref, rows_ref[...], yl_ref, yu_ref)
    sums.append(jnp.broadcast_to(misfits, (1, CH)))
    stat_ref[...] = jnp.concatenate(sums + [jnp.zeros((4, CH), F32)], axis=0)
    for copy in copies:
        copy.wait()


def conv(place, row_map, own, xl, xu, yl, yu, weight, mask):
    columns = (SLOTS, 10 * PLANE, 9 * CH)
    return pl.pallas_call(
        conv_kernel,
        out_shape=(shape((SLOTS, VOX, CH), F32), shape(columns, BF16), shape((8, CH), F32)),
        in_specs=[SM, SM] + [VM] * 8,
        out_specs=(VM, pl.BlockSpec(memory_space=pl.ANY), VM),
        scratch_shapes=[
            pltpu.VMEM((17, VOX, CH), BF16),
            pltpu.VMEM(columns, BF16),
            pltpu.SemaphoreType.DMA((SLOTS,)),
        ],
        compiler_params=params(28),
        cost_estimate=cost(6000000000, 12 << 20),
        name="forward_conv",
    )(place, row_map, row_map, own, xl, xu, yl, yu, weight, mask)


def step_kernel(
    place_ref, map_ref, rows_ref, own_ref, xl_ref, xu_ref, yl_ref, yu_ref, w_ref, mask_ref, *rest,
    forward, faces
):
    slot = pl.program_id(0)
    if forward:
        out_ref, x9_out, stat_ref, table_ref = rest
        x9_ref = x9_out.at[0]
    else:
        out_ref, table_ref, x9_ref = rest

    @pl.when(slot == 0)
    def _():
        fill = fill_faces if faces else fill_whole
        fill(place_ref, table_ref, (own_ref, xl_ref, xu_ref, yl_ref, yu_ref))
        table_ref[16] = jnp.zeros((VOX, CH), BF16)
        if forward:
            stat_ref[...] = jnp.zeros_like(stat_ref)

    fill_columns(map_ref, slot, table_ref, x9_ref, faces)
    total = None
    for p in range(3):
        term = jnp.dot(
            x9_ref[p * PLANE : p * PLANE + VOX, :], w_ref[p], preferred_element_type=F32
        )
        total = term if total is None else total + term
    mask = mask_ref[0].astype(F32)
    masked = total * mask
    if forward:
        out_ref[0] = total
        stat_ref[0:1] += jnp.sum(masked, axis=0, keepdims=True)
        stat_ref[1:2] += jnp.sum(masked * total, axis=0, keepdims=True)
        stat_ref[2:3] += jnp.sum(mask, axis=0, keepdims=True)
    else:
        out_ref[0] = masked.astype(BF16)


def whole(*dims):
    return pl.BlockSpec(dims, lambda s: (0,) * len(dims))


def conv_steps(place, row_map, own, xl, xu, yl, yu, weight, mask, forward, faces):
    brick = pl.BlockSpec((1, VOX, CH), lambda s: (s, 0, 0))
    scratch = [pltpu.VMEM((17, VOX, CH), BF16)]
    if forward:
        out_shape = (
            shape((SLOTS, VOX, CH), F32),
            shape((SLOTS, 10 * PLANE, 9 * CH), BF16),
            shape((8, CH), F32),
        )
        out_specs = (brick, pl.BlockSpec((1, 10 * PLANE, 9 * CH), lambda s: (s, 0, 0)), whole(8, CH))
    else:
        out_shape = shape((SLOTS, VOX, CH), BF16)
        out_specs = brick
        scratch.append(pltpu.VMEM((10 * PLANE, 9 * CH), BF16))
    return pl.pallas_call(
        functools.partial(step_kernel, forward=forward, faces=faces),
        grid=(SLOTS,),
        out_shape=out_shape,
        in_specs=[
            SM,
            SM,
            whole(*row_map.shape),
            whole(*own.shape),
            whole(*xl.shape),
            whole(*xu.shape),
            whole(*yl.shape),
            whole(*yu.shape),
            whole(3, 9 * CH, CH),
            brick,
        ],
        out_specs=out_specs,
        scratch_shapes=scratch,
        compiler_params=params(24),
        cost_estimate=cost(6000000000, 12 << 20),
        name="forward_steps" if forward else "transposed_conv",
    )(place, row_map, row_map, own, xl, xu, yl, yu, weight, mask)


def norm_terms(stats):
    count = stats[2:3]
    mean = stats[0:1] / count
    variance = stats[1:2] / count - mean * mean
    return count, mean, lax.rsqrt(variance + EPSILON)


def activate(slot, stats, cot_ref, conv_ref, mask_ref, gain_ref, shift_ref, act_ref, ga_ref, g_ref):
    count, mean, inverse = stats
    mask = mask_ref[slot].astype(F32)
    normed = (conv_ref[slot] - mean) * inverse
    pre = gain_ref[...] * normed + shift_ref[...]
    sig = jax.nn.sigmoid(pre)
    act_ref[slot] = (pre * sig * mask).astype(BF16)
    ga = cot_ref[slot].astype(F32) * mask * sig * (1.0 + pre * (1.0 - sig))
    ga_ref[slot] = ga
    nm = normed * mask
    for k in range(VOX // CH):
        rows = slice(k * CH, (k + 1) * CH)
        g_ref[slot, 0:CH, rows] = jnp.transpose(ga[rows]).astype(BF16)
        g_ref[slot, CH : 2 * CH, rows] = jnp.transpose(nm[rows]).astype(BF16)
        g_ref[slot, 2 * CH : 2 * CH + 16, rows] = jnp.transpose(mask[rows])[0:16].astype(BF16)
    sums = (jnp.sum(ga, axis=0, keepdims=True), jnp.sum(ga * normed, axis=0, keepdims=True))
    return jnp.concatenate(sums, axis=0)


def split(value, pieces):
    parts = []
    for _ in range(pieces):
        part = value.astype(BF16).astype(F32)
        parts.append(part)
        value = value - part
    return parts


def pack(ones, sums):
    parts = split(ones, 2) + split(sums[0:1], 3) + split(sums[1:2], 3)
    used = sum(part.shape[0] for part in parts)
    rows = -(-used // 16) * 16
    if used < rows:
        parts.append(jnp.zeros((rows - used, CH), F32))
    return jnp.concatenate(parts, axis=0).astype(BF16)


def unpack(rows, taps):
    ones = rows[0:taps] + rows[taps : 2 * taps]
    at = 2 * taps
    first = rows[at : at + 1] + rows[at + 1 : at + 2] + rows[at + 2 : at + 3]
    second = rows[at + 3 : at + 4] + rows[at + 4 : at + 5] + rows[at + 5 : at + 6]
    return ones, jnp.concatenate((first, second), axis=0)


def wgrad_kernel(
    place_ref, stat_ref, conv_ref, cot_ref, mask_ref, gain_ref, shift_ref, x9_hbm,
    act_ref, ga_ref, norm_ref, keep_ref, send_ref, g_ref, x9_ref, hold_ref, sems, *, unroll
):
    copies = [
        pltpu.make_async_copy(x9_hbm.at[s], x9_ref.at[s], sems.at[s]) for s in range(SLOTS)
    ]
    for copy in copies:
        copy.start()
    stats = norm_terms(jnp.sum(stat_ref[...], axis=0))
    count, mean, inverse = stats
    norm_ref[...] = jnp.concatenate((mean, inverse, count, jnp.zeros((5, CH), F32)), axis=0)

    def add_sums(s, sums):
        return sums + activate(
            s, stats, cot_ref, conv_ref, mask_ref, gain_ref, shift_ref, act_ref, ga_ref, g_ref
        )

    sums = lax.fori_loop(0, SLOTS, add_sums, jnp.zeros((2, CH), F32), unroll=unroll)
    for copy in copies:
        copy.wait()
    ones = [None] * 27
    for p in range(3):
        for q in range(0, 9, 2):
            width = min(2, 9 - q)
            lanes = slice(q * CH, (q + width) * CH)

            def add_term(s, total):
                rows = slice(p * PLANE, p * PLANE + VOX)
                return total + jnp.dot(
                    g_ref[s], x9_ref[s, rows, lanes], preferred_element_type=F32
                )

            if unroll:
                total = None
                for s in range(SLOTS):
                    total = add_term(s, 0.0 if total is None else total)
            else:
                empty = jnp.zeros((2 * CH + 16, width * CH), F32)
                total = lax.fori_loop(0, SLOTS, add_term, empty)
            for r in range(width):
                t = 9 * p + q + r
                tap = total[:, r * CH : (r + 1) * CH]
                ones[t] = tap[2 * CH : 2 * CH + 1]
                for half in (0, 1):
                    i = t - 13 * half
                    if 0 <= i < 14:
                        for k in range(16):
                            pair = jnp.concatenate(
                                (tap[8 * k : 8 * k + 8], tap[CH + 8 * k : CH + 8 * k + 8]), axis=0
                            )
                            row = k * MAIN + i * 16
                            hold_ref[half, row : row + 16, :] = pair
    for half in (0, 1):
        rows = jnp.concatenate(ones[13 * half : 13 * half + 14], axis=0)
        hold_ref[half, 16 * MAIN : 16 * MAIN + EXTRA, :] = pack(rows, sums).astype(F32)
    core = place_ref[1]
    keep_ref[...] = hold_ref[core]
    send_ref[...] = hold_ref[1 - core].astype(BF16)


def wgrad(place, stats, conv_out, cotangent, mask, gain, shift, x9, unroll):
    rows = 16 * MAIN + EXTRA
    return pl.pallas_call(
        functools.partial(wgrad_kernel, unroll=unroll),
        out_shape=(
            shape((SLOTS, VOX, CH), BF16),
            shape((SLOTS, VOX, CH), F32),
            shape((8, CH), F32),
            shape((rows, CH), F32),
            shape((rows, CH), BF16),
        ),
        in_specs=[SM] + [VM] * 6 + [pl.BlockSpec(memory_space=pl.ANY)],
        out_specs=(VM,) * 5,
        scratch_shapes=[
            pltpu.VMEM((SLOTS, 2 * CH + 16, VOX), BF16),
            pltpu.VMEM((SLOTS, 10 * PLANE, 9 * CH), BF16),
            pltpu.VMEM((2, rows, CH), F32),
            pltpu.SemaphoreType.DMA((SLOTS,)),
        ],
        compiler_params=params(28),
        cost_estimate=cost(6000000000, 12 << 20),
        name="weight_terms",
    )(place, stats, conv_out, cotangent, mask, gain, shift, x9)


def join_kernel(keep_ref, got_ref, out_ref):
    for k in range(16):
        rows = slice(k * MAIN, (k + 1) * MAIN)
        out_ref[k, 0:MAIN, :] = (keep_ref[rows, :] + got_ref[rows, :].astype(F32)).astype(BF16)
    rows = slice(16 * MAIN, 16 * MAIN + EXTRA)
    ones, sums = unpack(keep_ref[rows, :], 14)
    more_ones, more_sums = unpack(got_ref[rows, :].astype(F32), 14)
    extra = pack(ones + more_ones, sums + more_sums)
    for k in range(16):
        out_ref[k, MAIN : MAIN + EXTRA, :] = extra


def join(keep, got):
    return pl.pallas_call(
        join_kernel,
        out_shape=shape((16, MAIN + EXTRA, CH), BF16),
        in_specs=[VM, VM],
        out_specs=VM,
        compiler_params=params(),
        cost_estimate=cost(1 << 20, 3 << 20),
        name="join",
    )(keep, got)


def middle_kernel(parts_ref, out_ref):
    extra = None
    for k in range(16):
        ones, sums = unpack(parts_ref[k, MAIN : MAIN + EXTRA, :].astype(F32), 14)
        extra = (ones, sums) if extra is None else (extra[0] + ones, extra[1] + sums)
    for z in range(8):
        if z < 7:
            total = None
            for k in range(16):
                term = parts_ref[k, 32 * z : 32 * (z + 1), :].astype(F32)
                total = term if total is None else total + term
            ones = extra[0][2 * z : 2 * z + 2]
        else:
            total, ones = jnp.zeros((32, CH), F32), jnp.zeros((2, CH), F32)
        out_ref[z] = jnp.concatenate((total, ones, extra[1], jnp.zeros((4, CH), F32)), axis=0)


def middle(parts):
    return pl.pallas_call(
        middle_kernel,
        out_shape=shape((8, 40, CH), F32),
        in_specs=[VM],
        out_specs=VM,
        compiler_params=params(),
        cost_estimate=cost(1 << 20, 2 << 20),
        name="middle",
    )(parts)


def column(row):
    return jnp.transpose(jnp.broadcast_to(row, (CH, CH)))


def combine_kernel(place_ref, parts_ref, norm_ref, gain_ref, out_ref, gg_ref, sg_ref, coef_ref):
    total = jnp.sum(parts_ref[...], axis=0)
    main, ones, sums = total[0:32], total[32:34], total[34:36]
    inverse, count = norm_ref[1:2], norm_ref[2:3]
    scale = lax.rsqrt(count)
    sg_ref[...] = sums[0:1] * scale
    gg_ref[...] = sums[1:2] * scale
    coef_ref[0] = column(gain_ref[...] * inverse * scale)
    coef_ref[1] = column(sums[0:1] / count)
    coef_ref[2] = column(sums[1:2] / count)
    mine = pl.ds(pl.multiple_of(place_ref[2] * 8, 8), 8)
    factor, first, second = coef_ref[0, mine, :], coef_ref[1, mine, :], coef_ref[2, mine, :]
    values = []
    for i in range(2):
        base, cross = main[16 * i : 16 * i + 8], main[16 * i + 8 : 16 * i + 16]
        values.append(factor * (base - first * ones[i : i + 1] - second * cross))
    value = jnp.concatenate(values, axis=0).astype(BF16)
    for z in range(8):
        out_ref[z] = value


def combine(place, parts, norm, gain):
    return pl.pallas_call(
        combine_kernel,
        out_shape=(shape((8, 16, CH), BF16), shape((1, CH), F32), shape((1, CH), F32)),
        in_specs=[SM] + [VM] * 3,
        out_specs=(VM,) * 3,
        scratch_shapes=[pltpu.VMEM((3, CH, CH), F32)],
        compiler_params=params(),
        cost_estimate=cost(1 << 20, 1 << 20),
        name="combine",
    )(place, parts, norm, gain)


def grad_kernel(
    place_ref, sends_ref, parts_ref, norm_ref, gain_ref, conv_ref, ga_ref, mask_ref, out_ref, low_ref, high_ref, *, faces
):
    totals = jnp.sum(parts_ref[...], axis=0)[34:36]
    mean, inverse, count = norm_ref[0:1], norm_ref[1:2], norm_ref[2:3]
    factor = gain_ref[...] * inverse
    for s in range(SLOTS):
        normed = (conv_ref[s] - mean) * inverse
        inner = ga_ref[s] - (totals[0:1] + normed * totals[1:2]) / count
        out_ref[s] = (factor * inner * mask_ref[s].astype(F32)).astype(BF16)
    pick_x(place_ref, sends_ref, out_ref, low_ref, high_ref, faces)


def grad(place, sends_x, parts, norm, gain, conv_out, ga, mask, faces):
    return pl.pallas_call(
        functools.partial(grad_kernel, faces=faces),
        out_shape=(shape((SLOTS, VOX, CH), BF16),) + x_shapes(faces),
        in_specs=[SM, SM] + [VM] * 6,
        out_specs=(VM,) * 3,
        compiler_params=params(),
        cost_estimate=cost(4 << 20, 4 << 20),
        name="grad_conv",
    )(place, sends_x, parts, norm, gain, conv_out, ga, mask)


def finish_kernel(place_ref, mine_ref, other_ref, out_ref):
    for half in (0, 1):
        here = place_ref[1] == half
        for z in range(7):
            pairs = []
            for k in range(16):
                rows = slice(16 * z, 16 * (z + 1))
                pairs.append(jnp.where(here, mine_ref[k, rows, :], other_ref[k, rows, :]).astype(F32))
            for i in range(2):
                tap = 13 * half + 2 * z + i
                if half == 1 and tap == 13:
                    continue
                rows = jnp.concatenate([pair[8 * i : 8 * i + 8] for pair in pairs], axis=0)
                out_ref[tap] = jnp.transpose(rows)


def finish(place, mine, other):
    return pl.pallas_call(
        finish_kernel,
        out_shape=shape((27, CH, CH), F32),
        in_specs=[SM, VM, VM],
        out_specs=VM,
        compiler_params=params(),
        cost_estimate=cost(1 << 20, 3 << 20),
        name="finish",
    )(place, mine, other)


def spread(value, axes):
    size = axis_size(axes)
    return lax.all_to_all(jnp.broadcast_to(value[None], (size,) + value.shape), axes, 0, 0)


def all_sum_parts(value):
    return spread(jnp.sum(spread(value, ("z", "c")), axis=0), CROSS)


def swap(value):
    return lax.ppermute(value, "c", [(0, 1), (1, 0)])


def turn_kernel(w_ref, out_ref):
    for t in range(27):
        rows = slice((t % 9) * CH, (t % 9 + 1) * CH)
        out_ref[t // 9, rows, :] = jnp.transpose(w_ref[26 - t].astype(F32)).astype(BF16)


def turn(weight):
    return pl.pallas_call(
        turn_kernel,
        out_shape=shape((3, 9 * CH, CH), BF16),
        in_specs=[VM],
        out_specs=VM,
        compiler_params=params(),
        cost_estimate=cost(1 << 20, 2 << 20),
        name="turn",
    )(weight)


def shards(
    features,
    occupancy,
    counts,
    kernel_map,
    x_send,
    y_send,
    weight,
    norm_gain,
    norm_shift,
    cotangent,
):
    row_map, sends_x, sends_y = kernel_map[0, 0], x_send[0, 0], y_send[0, 0]
    gain, shift = norm_gain.reshape(1, CH), norm_shift.reshape(1, CH)
    place = jnp.stack((lax.axis_index("y") % 2, lax.axis_index("c"), lax.axis_index(CROSS)))
    ahead = weight.reshape(3, 9 * CH, CH)

    def first(faces):
        own, mask, low, high = prepare(place, counts, sends_x, features[0, 0], occupancy[0, 0], faces)
        later, low, high = lax.optimization_barrier((weight, low, high))
        xl, xu = neighbours(low, high, ("xh", "y"), faces)
        xl, xu, turned = lax.optimization_barrier((xl, xu, turn(later)))
        low, high = pick_y(place, sends_y, own, xl, xu, faces)
        yl, yu = neighbours(low, high, ("xl", "z", "c"), faces)
        table = (place, row_map, own, xl, xu, yl, yu, ahead, mask)
        conv_out, x9, stats = conv(*table) if faces else conv_steps(*table, True, False)
        return conv_out, x9, mask, turned, all_sum_parts(stats)

    def second(conv_out, x9, mask, turned, stats, faces):
        activations, ga, norm, keep, send = wgrad(
            place, stats, conv_out, cotangent[0, 0], mask, gain, shift, x9, faces
        )
        parts = lax.all_to_all(join(keep, swap(send)), CROSS, 0, 0)
        parts = lax.all_to_all(middle(parts), "z", 0, 0)
        grads, low, high = grad(place, sends_x, parts, norm, gain, conv_out, ga, mask, faces)
        parts, low, high = lax.optimization_barrier((parts, low, high))
        xl, xu = neighbours(low, high, ("xh", "y"), faces)
        value, gain_grad, shift_grad = combine(place, parts, norm, gain)
        mine = lax.all_to_all(value, "z", 0, 0).reshape(8 * 16, CH)[: 7 * 16]
        low, high = pick_y(place, sends_y, grads, xl, xu, faces)
        mine, low, high = lax.optimization_barrier((mine, low, high))
        yl, yu = neighbours(low, high, ("xl", "z", "c"), faces)
        mine = spread(mine, CROSS)
        features_grad = conv_steps(place, row_map, grads, xl, xu, yl, yu, turned, mask, False, faces)
        mine, features_grad = lax.optimization_barrier((mine, features_grad))
        weight_grad = finish(place, mine, swap(mine))
        return activations, features_grad, weight_grad, gain_grad, shift_grad

    state = first(True)
    misfits = jnp.sum(state[4][:, 3, 0])
    activations, features_grad, weight_grad, gain_grad, shift_grad = lax.cond(
        misfits > 0,
        lambda *_: second(*first(False), False),
        lambda *given: second(*given, True),
        *state,
    )
    return (
        activations[None, None],
        features_grad[None, None],
        weight_grad,
        gain_grad.reshape(CH),
        shift_grad.reshape(CH),
    )


def solution(mesh):
    fine = jax.sharding.Mesh(mesh.devices.reshape(2, 4, 2, 8, 2), ("xh", "y", "xl", "z", "c"))
    gx, gy = ("xh", "y"), ("xl", "z", "c")
    tiles = P(gx, gy, None, None, None)
    lists = P(gx, gy, None, None)
    return jax.shard_map(
        shards,
        mesh=fine,
        in_specs=(tiles, lists, P(gx, gy), lists, lists, lists, P(), P(), P(), tiles),
        out_specs=(tiles, tiles, P(), P(), P()),
        check_vma=False,
    )
```

```python
import functools

import jax
import jax.numpy as jnp
from jax import lax
from jax.experimental import pallas as pl
from jax.experimental.pallas import tpu as pltpu
from jax.sharding import PartitionSpec as P

EDGE = 8
PLANE = 64
VOX = 512
CH = 128
SLOTS = 4
HX = 2
HY = 4
EPSILON = 1e-05
F32 = jnp.float32
BF16 = jnp.bfloat16

VM = pl.BlockSpec(memory_space=pltpu.VMEM)
SM = pl.BlockSpec(memory_space=pltpu.SMEM)
MAIN = 224
EXTRA = 48
FACE_ROWS = HY * PLANE + 16
MIB = 1024 * 1024
CROSS = ("xh", "y", "xl")


def params(limit=20):
    return pltpu.CompilerParams(vmem_limit_bytes=limit * MIB)


def cost(flops, moved):
    return pl.CostEstimate(flops=flops, bytes_accessed=moved, transcendentals=0)


def shape(dims, kind):
    return jax.ShapeDtypeStruct(dims, kind)


def side_of(turn, odd):
    return 1 - odd if turn else odd


def lower_upper(odd, first, second):
    even = odd == 0
    return jnp.where(even, first, second), jnp.where(even, second, first)


def pick_x(place_ref, sends_ref, own_ref, first_ref, second_ref, faces):
    for turn, out_ref in ((0, first_ref), (1, second_ref)):
        side, rows = turn, slice(0, VOX)
        if faces:
            side = side_of(turn, place_ref[0])
            rows = pl.ds(pl.multiple_of(side * (VOX - PLANE), PLANE), PLANE)
        for k in range(HX):
            row = sends_ref[side, k]
            brick = own_ref[jnp.minimum(row, SLOTS - 1), rows, :]
            out_ref[k] = jnp.where(row < SLOTS, brick, jnp.zeros_like(brick))


def x_shapes(faces):
    send = shape((HX, PLANE if faces else VOX, CH), BF16)
    return (send, send)


def prepare_kernel(
    place_ref, counts_ref, sends_ref, feat_ref, occ_ref, own_ref, mask_ref, low_ref, high_ref, *, faces
):
    for s in range(SLOTS):
        live = (s < counts_ref[0, 0]).astype(F32)
        for k in range(VOX // CH):
            row = occ_ref[s : s + 1, k * CH : (k + 1) * CH].astype(F32) * live
            column = jnp.transpose(jnp.broadcast_to(row, (CH, CH)))
            rows = pl.ds(k * CH, CH)
            mask_ref[s, rows, :] = column.astype(BF16)
            own_ref[s, rows, :] = (feat_ref[s, rows, :].astype(F32) * column).astype(BF16)
    pick_x(place_ref, sends_ref, own_ref, low_ref, high_ref, faces)


def prepare(place, counts, sends_x, features, occupancy, faces):
    return pl.pallas_call(
        functools.partial(prepare_kernel, faces=faces),
        out_shape=(shape((SLOTS, VOX, CH), BF16),) * 2 + x_shapes(faces),
        in_specs=[SM, SM, SM, VM, VM],
        out_specs=(VM, VM, VM, VM),
        compiler_params=params(),
        cost_estimate=cost(1 << 20, 2 << 20),
        name="prepare",
    )(place, counts, sends_x, features, occupancy)


def pick_y_kernel(place_ref, sends_ref, own_ref, xl_ref, xu_ref, low_ref, high_ref):
    for side, out_ref in ((0, low_ref), (1, high_ref)):
        for k in range(HY):
            row = sends_ref[side, k]

            @pl.when(row < SLOTS)
            def _():
                out_ref[k] = own_ref[jnp.minimum(row, SLOTS - 1)]

            @pl.when((row >= SLOTS) & (row < SLOTS + HX))
            def _():
                out_ref[k] = xl_ref[jnp.clip(row - SLOTS, 0, HX - 1)]

            @pl.when((row >= SLOTS + HX) & (row < SLOTS + 2 * HX))
            def _():
                out_ref[k] = xu_ref[jnp.clip(row - SLOTS - HX, 0, HX - 1)]

            @pl.when(row >= SLOTS + 2 * HX)
            def _():
                out_ref[k] = jnp.zeros((VOX, CH), BF16)


def pick_y_faces_kernel(place_ref, sends_ref, own_ref, x1_ref, x2_ref, first_ref, second_ref):
    lines = lax.broadcasted_iota(jnp.int32, (16, CH), 0)
    odd = place_ref[0]
    for turn, out_ref in ((0, first_ref), (1, second_ref)):
        side = side_of(turn, place_ref[1])
        skip = side * (PLANE - 16)

        def piece(base):
            return pl.ds(pl.multiple_of(base + skip, 16), 16)

        def edge(block):
            block = block.astype(F32)
            return jnp.where(side == 0, block[:EDGE], block[EDGE:])

        origin = jnp.zeros((16, CH), F32)
        for k in range(HY):
            row = sends_ref[side, k]
            rows = pl.ds(k * PLANE, PLANE)
            lower = (row >= SLOTS) & (row < SLOTS + HX)
            upper = (row >= SLOTS + HX) & (row < SLOTS + 2 * HX)
            code = jnp.where(lower, 1.0, jnp.where(upper, 2.0, 0.0))
            origin = jnp.where(lines == k, code, origin)

            @pl.when(row < SLOTS)
            def _():
                brick = jnp.minimum(row, SLOTS - 1)
                parts = [edge(own_ref[brick, piece(a * PLANE), :]) for a in range(EDGE)]
                out_ref[rows, :] = jnp.concatenate(parts, axis=0).astype(BF16)

            @pl.when(lower | upper)
            def _():
                at = jnp.where(lower, row - SLOTS, row - SLOTS - HX)
                at = jnp.clip(at, 0, HX - 1)
                down, up = lower_upper(odd, x1_ref[at, piece(0), :], x2_ref[at, piece(0), :])
                part = edge(jnp.where(lower, down, up))
                empty = jnp.zeros((PLANE - 2 * EDGE, CH), F32)
                blank = jnp.zeros_like(part)
                front, back = jnp.where(lower, blank, part), jnp.where(lower, part, blank)
                out_ref[rows, :] = jnp.concatenate((front, empty, back), axis=0).astype(BF16)

            @pl.when(row >= SLOTS + 2 * HX)
            def _():
                out_ref[rows, :] = jnp.zeros((PLANE, CH), BF16)

        out_ref[HY * PLANE : FACE_ROWS, :] = origin.astype(BF16)


def pick_y(place, sends_y, own, xl, xu, faces):
    send = shape((FACE_ROWS, CH) if faces else (HY, VOX, CH), BF16)
    return pl.pallas_call(
        pick_y_faces_kernel if faces else pick_y_kernel,
        out_shape=(send, send),
        in_specs=[SM, SM, VM, VM, VM],
        out_specs=(VM, VM),
        compiler_params=params(),
        cost_estimate=cost(1 << 20, 2 << 20),
        name="pick_y",
    )(place, sends_y, own, xl, xu)


def axis_size(axes):
    size = 1
    for axis in axes:
        size *= lax.axis_size(axis)
    return size


def neighbours(first, second, axes, faces):
    size = axis_size(axes)
    if faces:
        pairs = [[(i, i + 1) for i in range(1 - turn, size - 1, 2)] for turn in (0, 1)]
        one, two = [pair + [(j, i) for i, j in pair] for pair in pairs]
        return lax.ppermute(first, axes, one), lax.ppermute(second, axes, two)
    up = [(i, i + 1) for i in range(size - 1)]
    down = [(j, i) for i, j in up]
    return lax.ppermute(second, axes, up), lax.ppermute(first, axes, down)


def fill_plane(map_ref, slot, table_ref, x9_ref, move, base, row):
    sub = lax.broadcasted_iota(jnp.int32, (EDGE + 2, EDGE, CH), 1)
    spans = []
    for r in (-1, 0, 1):
        tap = 9 * (move + 1) + r + 1
        first, whole_plane, last = pl.ds(base + 48, 16), pl.ds(base, PLANE), pl.ds(base, 16)
        before = table_ref[map_ref[slot, tap], first, :].astype(F32)[8:]
        middle = table_ref[map_ref[slot, tap + 3], whole_plane, :].astype(F32)
        after = table_ref[map_ref[slot, tap + 6], last, :].astype(F32)[:8]
        spans.append(jnp.concatenate((before, middle, after), axis=0).reshape(EDGE + 2, EDGE, CH))
    low, centre, high = spans
    down = pltpu.roll(jnp.where(sub == EDGE - 1, low, centre), 1, 1)
    up = pltpu.roll(jnp.where(sub == 0, high, centre), EDGE - 1, 1)
    for r, source in ((-1, down), (0, centre), (1, up)):
        for q in (-1, 0, 1):
            rows = source[q + 1 : q + 1 + EDGE].reshape(PLANE, CH).astype(BF16)
            lane = (3 * (q + 1) + r + 1) * CH
            x9_ref[pl.ds(row, PLANE), lane : lane + CH] = rows


def fill_columns(map_ref, slot, table_ref, x9_ref, unroll=True):
    fill = functools.partial(fill_plane, map_ref, slot, table_ref, x9_ref)
    fill(-1, VOX - PLANE, 0)
    if unroll:
        for a in range(EDGE):
            fill(0, a * PLANE, (a + 1) * PLANE)
    else:

        def inner(a, carry):
            base = pl.multiple_of(a * PLANE, PLANE)
            fill(0, base, pl.multiple_of(base + PLANE, PLANE))
            return carry

        lax.fori_loop(0, EDGE, inner, 0)
    fill(1, 0, (EDGE + 1) * PLANE)


def fill_whole(place_ref, table_ref, refs):
    start = 0
    for ref in refs:
        table_ref[start : start + ref.shape[0]] = ref[...]
        start += ref.shape[0]


def fill_faces(place_ref, table_ref, refs):
    own_ref, x1_ref, x2_ref, y1_ref, y2_ref = refs
    table_ref[0:SLOTS] = own_ref[...]
    for k in range(HX):
        low, high = lower_upper(place_ref[0], x1_ref[k], x2_ref[k])
        table_ref[SLOTS + k, VOX - PLANE : VOX, :] = low
        table_ref[SLOTS + HX + k, 0:PLANE, :] = high
    empty = jnp.zeros((EDGE, CH), F32)
    first = SLOTS + 2 * HX
    for k in range(HY):
        rows = slice(k * PLANE, (k + 1) * PLANE)
        low, high = lower_upper(
            place_ref[1], y1_ref[rows, :].astype(F32), y2_ref[rows, :].astype(F32)
        )
        for a in range(EDGE):
            part = slice(a * EDGE, (a + 1) * EDGE)
            base = a * PLANE
            table_ref[first + k, base + 48 : base + 64, :] = jnp.concatenate(
                (empty, low[part]), axis=0
            ).astype(BF16)
            table_ref[first + HY + k, base : base + 16, :] = jnp.concatenate(
                (high[part], empty), axis=0
            ).astype(BF16)


def count_misfits(place_ref, rows, y1_ref, y2_ref):
    lane = lax.broadcasted_iota(jnp.int32, rows.shape, 1)
    within = lane - jnp.where(lane >= 9, 9, 0) - jnp.where(lane >= 18, 9, 0)
    not_down, not_up = lane >= 9, lane < 18
    bad = (rows >= SLOTS) & (rows < SLOTS + HX) & not_down
    bad = bad | ((rows >= SLOTS + HX) & (rows < SLOTS + 2 * HX) & not_up)
    marks = slice(HY * PLANE, FACE_ROWS)
    low, high = lower_upper(
        place_ref[1], y1_ref[marks, :].astype(F32), y2_ref[marks, :].astype(F32)
    )
    for start, origin, wrong in (
        (SLOTS + 2 * HX, low, within >= 3),
        (SLOTS + 2 * HX + HY, high, within < 6),
    ):
        for k in range(HY):
            code = jnp.broadcast_to(origin[k : k + 1, 0 : rows.shape[1]], rows.shape)
            fault = wrong | ((code == 1.0) & not_down) | ((code == 2.0) & not_up)
            bad = bad | ((rows == start + k) & fault)
    return jnp.sum(jnp.where(bad, 1.0, 0.0))


def conv_kernel(
    place_ref, map_ref, rows_ref, own_ref, xl_ref, xu_ref, yl_ref, yu_ref, w_ref, mask_ref,
    out_ref, x9_out, stat_ref, table_ref, x9_ref, sems,
):
    fill_faces(place_ref, table_ref, (own_ref, xl_ref, xu_ref, yl_ref, yu_ref))
    table_ref[16] = jnp.zeros((VOX, CH), BF16)
    sums = [jnp.zeros((1, CH), F32)] * 3
    copies = []

    def columns(slot):
        fill_columns(map_ref, slot, table_ref, x9_ref.at[slot])
        copies.append(pltpu.make_async_copy(x9_ref.at[slot], x9_out.at[slot], sems.at[slot]))
        copies[-1].start()

    columns(0)
    for slot in range(SLOTS):
        if slot + 1 < SLOTS:
            columns(slot + 1)
        total = None
        for p in range(3):
            term = jnp.dot(
                x9_ref[slot, p * PLANE : p * PLANE + VOX, :], w_ref[p], preferred_element_type=F32
            )
            total = term if total is None else total + term
        mask = mask_ref[slot].astype(F32)
        masked = total * mask
        out_ref[slot] = total
        terms = (masked, masked * total, mask)
        sums = [s + jnp.sum(term, axis=0, keepdims=True) for s, term in zip(sums, terms)]
    misfits = count_misfits(place_ref, rows_ref[...], yl_ref, yu_ref)
    sums.append(jnp.broadcast_to(misfits, (1, CH)))
    stat_ref[...] = jnp.concatenate(sums + [jnp.zeros((4, CH), F32)], axis=0)
    for copy in copies:
        copy.wait()


def conv(place, row_map, own, xl, xu, yl, yu, weight, mask):
    columns = (SLOTS, 10 * PLANE, 9 * CH)
    return pl.pallas_call(
        conv_kernel,
        out_shape=(shape((SLOTS, VOX, CH), F32), shape(columns, BF16), shape((8, CH), F32)),
        in_specs=[SM, SM] + [VM] * 8,
        out_specs=(VM, pl.BlockSpec(memory_space=pl.ANY), VM),
        scratch_shapes=[
            pltpu.VMEM((17, VOX, CH), BF16),
            pltpu.VMEM(columns, BF16),
            pltpu.SemaphoreType.DMA((SLOTS,)),
        ],
        compiler_params=params(28),
        cost_estimate=cost(6000000000, 12 << 20),
        name="forward_conv",
    )(place, row_map, row_map, own, xl, xu, yl, yu, weight, mask)


def step_kernel(
    place_ref, map_ref, rows_ref, own_ref, xl_ref, xu_ref, yl_ref, yu_ref, w_ref, mask_ref, *rest,
    forward, faces
):
    slot = pl.program_id(0)
    if forward:
        out_ref, x9_out, stat_ref, table_ref = rest
        x9_ref = x9_out.at[0]
    else:
        out_ref, table_ref, x9_ref = rest

    @pl.when(slot == 0)
    def _():
        fill = fill_faces if faces else fill_whole
        fill(place_ref, table_ref, (own_ref, xl_ref, xu_ref, yl_ref, yu_ref))
        table_ref[16] = jnp.zeros((VOX, CH), BF16)
        if forward:
            stat_ref[...] = jnp.zeros_like(stat_ref)

    fill_columns(map_ref, slot, table_ref, x9_ref, faces)
    total = None
    for p in range(3):
        term = jnp.dot(
            x9_ref[p * PLANE : p * PLANE + VOX, :], w_ref[p], preferred_element_type=F32
        )
        total = term if total is None else total + term
    mask = mask_ref[0].astype(F32)
    masked = total * mask
    if forward:
        out_ref[0] = total
        stat_ref[0:1] += jnp.sum(masked, axis=0, keepdims=True)
        stat_ref[1:2] += jnp.sum(masked * total, axis=0, keepdims=True)
        stat_ref[2:3] += jnp.sum(mask, axis=0, keepdims=True)
    else:
        out_ref[0] = masked.astype(BF16)


def whole(*dims):
    return pl.BlockSpec(dims, lambda s: (0,) * len(dims))


def conv_steps(place, row_map, own, xl, xu, yl, yu, weight, mask, forward, faces):
    brick = pl.BlockSpec((1, VOX, CH), lambda s: (s, 0, 0))
    scratch = [pltpu.VMEM((17, VOX, CH), BF16)]
    if forward:
        out_shape = (
            shape((SLOTS, VOX, CH), F32),
            shape((SLOTS, 10 * PLANE, 9 * CH), BF16),
            shape((8, CH), F32),
        )
        out_specs = (brick, pl.BlockSpec((1, 10 * PLANE, 9 * CH), lambda s: (s, 0, 0)), whole(8, CH))
    else:
        out_shape = shape((SLOTS, VOX, CH), BF16)
        out_specs = brick
        scratch.append(pltpu.VMEM((10 * PLANE, 9 * CH), BF16))
    return pl.pallas_call(
        functools.partial(step_kernel, forward=forward, faces=faces),
        grid=(SLOTS,),
        out_shape=out_shape,
        in_specs=[
            SM,
            SM,
            whole(*row_map.shape),
            whole(*own.shape),
            whole(*xl.shape),
            whole(*xu.shape),
            whole(*yl.shape),
            whole(*yu.shape),
            whole(3, 9 * CH, CH),
            brick,
        ],
        out_specs=out_specs,
        scratch_shapes=scratch,
        compiler_params=params(24),
        cost_estimate=cost(6000000000, 12 << 20),
        name="forward_steps" if forward else "transposed_conv",
    )(place, row_map, row_map, own, xl, xu, yl, yu, weight, mask)


def norm_terms(stats):
    count = stats[2:3]
    mean = stats[0:1] / count
    variance = stats[1:2] / count - mean * mean
    return count, mean, lax.rsqrt(variance + EPSILON)


def activate(slot, stats, cot_ref, conv_ref, mask_ref, gain_ref, shift_ref, act_ref, ga_ref, g_ref):
    count, mean, inverse = stats
    mask = mask_ref[slot].astype(F32)
    normed = (conv_ref[slot] - mean) * inverse
    pre = gain_ref[...] * normed + shift_ref[...]
    sig = jax.nn.sigmoid(pre)
    act_ref[slot] = (pre * sig * mask).astype(BF16)
    ga = cot_ref[slot].astype(F32) * mask * sig * (1.0 + pre * (1.0 - sig))
    ga_ref[slot] = ga
    nm = normed * mask
    for k in range(VOX // CH):
        rows = slice(k * CH, (k + 1) * CH)
        g_ref[slot, 0:CH, rows] = jnp.transpose(ga[rows]).astype(BF16)
        g_ref[slot, CH : 2 * CH, rows] = jnp.transpose(nm[rows]).astype(BF16)
        g_ref[slot, 2 * CH : 2 * CH + 16, rows] = jnp.transpose(mask[rows])[0:16].astype(BF16)
    sums = (jnp.sum(ga, axis=0, keepdims=True), jnp.sum(ga * normed, axis=0, keepdims=True))
    return jnp.concatenate(sums, axis=0)


def split(value, pieces):
    parts = []
    for _ in range(pieces):
        part = value.astype(BF16).astype(F32)
        parts.append(part)
        value = value - part
    return parts


def pack(ones, sums):
    parts = split(ones, 2) + split(sums[0:1], 3) + split(sums[1:2], 3)
    used = sum(part.shape[0] for part in parts)
    rows = -(-used // 16) * 16
    if used < rows:
        parts.append(jnp.zeros((rows - used, CH), F32))
    return jnp.concatenate(parts, axis=0).astype(BF16)


def unpack(rows, taps):
    ones = rows[0:taps] + rows[taps : 2 * taps]
    at = 2 * taps
    first = rows[at : at + 1] + rows[at + 1 : at + 2] + rows[at + 2 : at + 3]
    second = rows[at + 3 : at + 4] + rows[at + 4 : at + 5] + rows[at + 5 : at + 6]
    return ones, jnp.concatenate((first, second), axis=0)


def wgrad_kernel(
    place_ref, stat_ref, conv_ref, cot_ref, mask_ref, gain_ref, shift_ref, x9_hbm,
    act_ref, ga_ref, norm_ref, keep_ref, send_ref, g_ref, x9_ref, hold_ref, sems, *, unroll
):
    copies = [
        pltpu.make_async_copy(x9_hbm.at[s], x9_ref.at[s], sems.at[s]) for s in range(SLOTS)
    ]
    for copy in copies:
        copy.start()
    stats = norm_terms(jnp.sum(stat_ref[...], axis=0))
    count, mean, inverse = stats
    norm_ref[...] = jnp.concatenate((mean, inverse, count, jnp.zeros((5, CH), F32)), axis=0)

    def add_sums(s, sums):
        return sums + activate(
            s, stats, cot_ref, conv_ref, mask_ref, gain_ref, shift_ref, act_ref, ga_ref, g_ref
        )

    sums = lax.fori_loop(0, SLOTS, add_sums, jnp.zeros((2, CH), F32), unroll=unroll)
    for copy in copies:
        copy.wait()
    ones = [None] * 27
    for p in range(3):
        for q in range(0, 9, 2):
            width = min(2, 9 - q)
            lanes = slice(q * CH, (q + width) * CH)

            def add_term(s, total):
                rows = slice(p * PLANE, p * PLANE + VOX)
                return total + jnp.dot(
                    g_ref[s], x9_ref[s, rows, lanes], preferred_element_type=F32
                )

            if unroll:
                total = None
                for s in range(SLOTS):
                    total = add_term(s, 0.0 if total is None else total)
            else:
                empty = jnp.zeros((2 * CH + 16, width * CH), F32)
                total = lax.fori_loop(0, SLOTS, add_term, empty)
            for r in range(width):
                t = 9 * p + q + r
                tap = total[:, r * CH : (r + 1) * CH]
                ones[t] = tap[2 * CH : 2 * CH + 1]
                for half in (0, 1):
                    i = t - 13 * half
                    if 0 <= i < 14:
                        for k in range(16):
                            pair = jnp.concatenate(
                                (tap[8 * k : 8 * k + 8], tap[CH + 8 * k : CH + 8 * k + 8]), axis=0
                            )
                            row = k * MAIN + i * 16
                            hold_ref[half, row : row + 16, :] = pair
    for half in (0, 1):
        rows = jnp.concatenate(ones[13 * half : 13 * half + 14], axis=0)
        hold_ref[half, 16 * MAIN : 16 * MAIN + EXTRA, :] = pack(rows, sums).astype(F32)
    core = place_ref[1]
    keep_ref[...] = hold_ref[core]
    send_ref[...] = hold_ref[1 - core].astype(BF16)


def wgrad(place, stats, conv_out, cotangent, mask, gain, shift, x9, unroll):
    rows = 16 * MAIN + EXTRA
    return pl.pallas_call(
        functools.partial(wgrad_kernel, unroll=unroll),
        out_shape=(
            shape((SLOTS, VOX, CH), BF16),
            shape((SLOTS, VOX, CH), F32),
            shape((8, CH), F32),
            shape((rows, CH), F32),
            shape((rows, CH), BF16),
        ),
        in_specs=[SM] + [VM] * 6 + [pl.BlockSpec(memory_space=pl.ANY)],
        out_specs=(VM,) * 5,
        scratch_shapes=[
            pltpu.VMEM((SLOTS, 2 * CH + 16, VOX), BF16),
            pltpu.VMEM((SLOTS, 10 * PLANE, 9 * CH), BF16),
            pltpu.VMEM((2, rows, CH), F32),
            pltpu.SemaphoreType.DMA((SLOTS,)),
        ],
        compiler_params=params(28),
        cost_estimate=cost(6000000000, 12 << 20),
        name="weight_terms",
    )(place, stats, conv_out, cotangent, mask, gain, shift, x9)


def join_kernel(keep_ref, got_ref, out_ref):
    for k in range(16):
        rows = slice(k * MAIN, (k + 1) * MAIN)
        out_ref[k, 0:MAIN, :] = (keep_ref[rows, :] + got_ref[rows, :].astype(F32)).astype(BF16)
    rows = slice(16 * MAIN, 16 * MAIN + EXTRA)
    ones, sums = unpack(keep_ref[rows, :], 14)
    more_ones, more_sums = unpack(got_ref[rows, :].astype(F32), 14)
    extra = pack(ones + more_ones, sums + more_sums)
    for k in range(16):
        out_ref[k, MAIN : MAIN + EXTRA, :] = extra


def join(keep, got):
    return pl.pallas_call(
        join_kernel,
        out_shape=shape((16, MAIN + EXTRA, CH), BF16),
        in_specs=[VM, VM],
        out_specs=VM,
        compiler_params=params(),
        cost_estimate=cost(1 << 20, 3 << 20),
        name="join",
    )(keep, got)


def middle_kernel(parts_ref, out_ref):
    extra = None
    for k in range(16):
        ones, sums = unpack(parts_ref[k, MAIN : MAIN + EXTRA, :].astype(F32), 14)
        extra = (ones, sums) if extra is None else (extra[0] + ones, extra[1] + sums)
    for z in range(8):
        if z < 7:
            total = None
            for k in range(16):
                term = parts_ref[k, 32 * z : 32 * (z + 1), :].astype(F32)
                total = term if total is None else total + term
            ones = extra[0][2 * z : 2 * z + 2]
        else:
            total, ones = jnp.zeros((32, CH), F32), jnp.zeros((2, CH), F32)
        out_ref[z] = jnp.concatenate((total, ones, extra[1], jnp.zeros((4, CH), F32)), axis=0)


def middle(parts):
    return pl.pallas_call(
        middle_kernel,
        out_shape=shape((8, 40, CH), F32),
        in_specs=[VM],
        out_specs=VM,
        compiler_params=params(),
        cost_estimate=cost(1 << 20, 2 << 20),
        name="middle",
    )(parts)


def column(row):
    return jnp.transpose(jnp.broadcast_to(row, (CH, CH)))


def combine_kernel(place_ref, parts_ref, norm_ref, gain_ref, out_ref, gg_ref, sg_ref, coef_ref):
    total = jnp.sum(parts_ref[...], axis=0)
    main, ones, sums = total[0:32], total[32:34], total[34:36]
    inverse, count = norm_ref[1:2], norm_ref[2:3]
    scale = lax.rsqrt(count)
    sg_ref[...] = sums[0:1] * scale
    gg_ref[...] = sums[1:2] * scale
    coef_ref[0] = column(gain_ref[...] * inverse * scale)
    coef_ref[1] = column(sums[0:1] / count)
    coef_ref[2] = column(sums[1:2] / count)
    mine = pl.ds(pl.multiple_of(place_ref[2] * 8, 8), 8)
    factor, first, second = coef_ref[0, mine, :], coef_ref[1, mine, :], coef_ref[2, mine, :]
    values = []
    for i in range(2):
        base, cross = main[16 * i : 16 * i + 8], main[16 * i + 8 : 16 * i + 16]
        values.append(factor * (base - first * ones[i : i + 1] - second * cross))
    value = jnp.concatenate(values, axis=0).astype(BF16)
    for z in range(8):
        out_ref[z] = value


def combine(place, parts, norm, gain):
    return pl.pallas_call(
        combine_kernel,
        out_shape=(shape((8, 16, CH), BF16), shape((1, CH), F32), shape((1, CH), F32)),
        in_specs=[SM] + [VM] * 3,
        out_specs=(VM,) * 3,
        scratch_shapes=[pltpu.VMEM((3, CH, CH), F32)],
        compiler_params=params(),
        cost_estimate=cost(1 << 20, 1 << 20),
        name="combine",
    )(place, parts, norm, gain)


def grad_kernel(
    place_ref, sends_ref, parts_ref, norm_ref, gain_ref, conv_ref, ga_ref, mask_ref, out_ref, low_ref, high_ref, *, faces
):
    totals = jnp.sum(parts_ref[...], axis=0)[34:36]
    mean, inverse, count = norm_ref[0:1], norm_ref[1:2], norm_ref[2:3]
    factor = gain_ref[...] * inverse
    for s in range(SLOTS):
        normed = (conv_ref[s] - mean) * inverse
        inner = ga_ref[s] - (totals[0:1] + normed * totals[1:2]) / count
        out_ref[s] = (factor * inner * mask_ref[s].astype(F32)).astype(BF16)
    pick_x(place_ref, sends_ref, out_ref, low_ref, high_ref, faces)


def grad(place, sends_x, parts, norm, gain, conv_out, ga, mask, faces):
    return pl.pallas_call(
        functools.partial(grad_kernel, faces=faces),
        out_shape=(shape((SLOTS, VOX, CH), BF16),) + x_shapes(faces),
        in_specs=[SM, SM] + [VM] * 6,
        out_specs=(VM,) * 3,
        compiler_params=params(),
        cost_estimate=cost(4 << 20, 4 << 20),
        name="grad_conv",
    )(place, sends_x, parts, norm, gain, conv_out, ga, mask)


def finish_kernel(place_ref, mine_ref, other_ref, out_ref):
    for half in (0, 1):
        here = place_ref[1] == half
        for z in range(7):
            pairs = []
            for k in range(16):
                rows = slice(16 * z, 16 * (z + 1))
                pairs.append(jnp.where(here, mine_ref[k, rows, :], other_ref[k, rows, :]).astype(F32))
            for i in range(2):
                tap = 13 * half + 2 * z + i
                if half == 1 and tap == 13:
                    continue
                rows = jnp.concatenate([pair[8 * i : 8 * i + 8] for pair in pairs], axis=0)
                out_ref[tap] = jnp.transpose(rows)


def finish(place, mine, other):
    return pl.pallas_call(
        finish_kernel,
        out_shape=shape((27, CH, CH), F32),
        in_specs=[SM, VM, VM],
        out_specs=VM,
        compiler_params=params(),
        cost_estimate=cost(1 << 20, 3 << 20),
        name="finish",
    )(place, mine, other)


def spread(value, axes):
    size = axis_size(axes)
    return lax.all_to_all(jnp.broadcast_to(value[None], (size,) + value.shape), axes, 0, 0)


def all_sum_parts(value):
    return spread(jnp.sum(spread(value, ("z", "c")), axis=0), CROSS)


def swap(value):
    return lax.ppermute(value, "c", [(0, 1), (1, 0)])


def turn_kernel(w_ref, out_ref):
    for t in range(27):
        rows = slice((t % 9) * CH, (t % 9 + 1) * CH)
        out_ref[t // 9, rows, :] = jnp.transpose(w_ref[26 - t].astype(F32)).astype(BF16)


def turn(weight):
    return pl.pallas_call(
        turn_kernel,
        out_shape=shape((3, 9 * CH, CH), BF16),
        in_specs=[VM],
        out_specs=VM,
        compiler_params=params(),
        cost_estimate=cost(1 << 20, 2 << 20),
        name="turn",
    )(weight)


def shards(
    features,
    occupancy,
    counts,
    kernel_map,
    x_send,
    y_send,
    weight,
    norm_gain,
    norm_shift,
    cotangent,
):
    row_map, sends_x, sends_y = kernel_map[0, 0], x_send[0, 0], y_send[0, 0]
    gain, shift = norm_gain.reshape(1, CH), norm_shift.reshape(1, CH)
    place = jnp.stack((lax.axis_index("y") % 2, lax.axis_index("c"), lax.axis_index(CROSS)))
    ahead = weight.reshape(3, 9 * CH, CH)

    def first(faces):
        own, mask, low, high = prepare(place, counts, sends_x, features[0, 0], occupancy[0, 0], faces)
        xl, xu = neighbours(low, high, ("xh", "y"), faces)
        low, high = pick_y(place, sends_y, own, xl, xu, faces)
        later, low, high = lax.optimization_barrier((weight, low, high))
        yl, yu = neighbours(low, high, ("xl", "z", "c"), faces)
        yl, yu, turned = lax.optimization_barrier((yl, yu, turn(later)))
        table = (place, row_map, own, xl, xu, yl, yu, ahead, mask)
        conv_out, x9, stats = conv(*table) if faces else conv_steps(*table, True, False)
        return conv_out, x9, mask, turned, all_sum_parts(stats)

    def second(conv_out, x9, mask, turned, stats, faces):
        activations, ga, norm, keep, send = wgrad(
            place, stats, conv_out, cotangent[0, 0], mask, gain, shift, x9, faces
        )
        parts = lax.all_to_all(join(keep, swap(send)), CROSS, 0, 0)
        parts = lax.all_to_all(middle(parts), "z", 0, 0)
        grads, low, high = grad(place, sends_x, parts, norm, gain, conv_out, ga, mask, faces)
        parts, low, high = lax.optimization_barrier((parts, low, high))
        xl, xu = neighbours(low, high, ("xh", "y"), faces)
        value, gain_grad, shift_grad = combine(place, parts, norm, gain)
        mine = lax.all_to_all(value, "z", 0, 0).reshape(8 * 16, CH)[: 7 * 16]
        low, high = pick_y(place, sends_y, grads, xl, xu, faces)
        mine, low, high = lax.optimization_barrier((mine, low, high))
        yl, yu = neighbours(low, high, ("xl", "z", "c"), faces)
        mine = spread(mine, CROSS)
        features_grad = conv_steps(place, row_map, grads, xl, xu, yl, yu, turned, mask, False, faces)
        mine, features_grad = lax.optimization_barrier((mine, features_grad))
        weight_grad = finish(place, mine, swap(mine))
        return activations, features_grad, weight_grad, gain_grad, shift_grad

    state = first(True)
    misfits = jnp.sum(state[4][:, 3, 0])
    activations, features_grad, weight_grad, gain_grad, shift_grad = lax.cond(
        misfits > 0,
        lambda *_: second(*first(False), False),
        lambda *given: second(*given, True),
        *state,
    )
    return (
        activations[None, None],
        features_grad[None, None],
        weight_grad,
        gain_grad.reshape(CH),
        shift_grad.reshape(CH),
    )


def solution(mesh):
    fine = jax.sharding.Mesh(mesh.devices.reshape(2, 4, 2, 8, 2), ("xh", "y", "xl", "z", "c"))
    gx, gy = ("xh", "y"), ("xl", "z", "c")
    tiles = P(gx, gy, None, None, None)
    lists = P(gx, gy, None, None)
    return jax.shard_map(
        shards,
        mesh=fine,
        in_specs=(tiles, lists, P(gx, gy), lists, lists, lists, P(), P(), P(), tiles),
        out_specs=(tiles, tiles, P(), P(), P()),
        check_vma=False,
    )
```
